32 devices in a mesh: ens: 4 (over y, x), oy: 2 (over core), ox: 4 (over z).
Axes of the slice: x: 2, y: 2, z: 4, core: 2. Of those that a mesh axis runs over, the one named last changes fastest.
Arguments:
- state: bfloat16 [4, 8, 512, 256], P('ens', 'oy', 'ox'), may hold values from -6 to 6
- state_cot: bfloat16 [4, 8, 512, 256], P('ens', 'oy', 'ox'), may hold values from -6 to 6
- flux_cot: bfloat16 [4, 512, 4, 128], P('ens', ('oy', 'ox')), may hold values from -6 to 6
- conv_weight: bfloat16 [9, 256, 256], replicated, may hold values from -0.125 to 0.125
- mix_weight: bfloat16 [256, 256], replicated, may hold values from -0.375 to 0.375
- flux_weight: bfloat16 [4, 256], replicated, may hold values from -3 to 3
- regrid_weights: bfloat16 [16, 128, 128], replicated, may hold values from -0.5 to 0.5
- intersection_atm: int32 [8, 4, 4], replicated, may hold values from 0 to 511, as said below
- intersection_offset: int32 [8, 4, 4], replicated, may hold values from 0 to 15
- wet_rows: int32 [2, 4], P('oy', 'ox'), may hold values from 1 to 4
Outputs:
- input_grad: bfloat16 [4, 8, 512, 256], P('ens', 'oy', 'ox')
- weight_grads: float32 [2560, 256], P(('oy', 'ox'))
- flux_grad: float32 [4, 256], replicated
The draws below stay inside these ranges and needn't reach their ends.
Inputs may be any that keep to these rules, and one draw needn't show every extreme that they name: `intersection_atm`: atmosphere block a lies on device a // 64, numbered oy 4 + ox. The intersections of the ocean blocks of device (oy, ox), that is of latitude rows oy 4 to oy 4 + 3 and longitude block ox, lie on exactly four atmosphere devices, two with index oy and two with index (oy + 1) mod 2 along oy. At most 5 of that device's 4 x 4 intersections lie on one atmosphere device, and for every ocean device exactly 5 lie on one of them.
All inputs are finite; a program needn't handle non-finite values.
Results may differ from the reference program's by a relative error of at most 0.0085.
Values may be sent and summed in bfloat16 or wider, within the bound.
A program may use at most 64 MiB of HBM per device.

```python
import math
import jax
import jax.numpy as jnp
from jax import lax

C = 256
BLOCK = 128
FLUX = 4
INTERSECTIONS = 4
ROWS_DEV = 4
ATM_DEV = 64
NMAT = 16
CAP = 5
LAT_TILES = 2
LON_BLOCKS = 4
MEMBERS = 4
NLAT = 8
NLON = 512
ATM_BLOCKS = 512


def draw_intersection_atm(key, part):
    device_count = LAT_TILES * LON_BLOCKS
    entries = ROWS_DEV * INTERSECTIONS

    def draw_device(dev_index):
        dev_key = jax.random.fold_in(jax.random.fold_in(key, 7301), dev_index)
        key_rest, key_mix, key_corner, key_first, key_second, key_local = jax.random.split(dev_key, 6)
        pool_index = jax.random.permutation(key_rest, 3 * CAP - 3)[:entries - CAP - 3]
        pool_group = 1 + pool_index // (CAP - 1)
        pool_slot = pool_group * CAP + 1 + pool_index % (CAP - 1)
        firsts = jnp.arange(1, 4) * CAP
        chosen = jnp.concatenate([jnp.arange(CAP), firsts, pool_slot])
        chosen = jax.random.permutation(key_mix, chosen)
        owner_slot = chosen // CAP
        corner_order = jax.random.permutation(key_corner, 4)
        corner = corner_order[owner_slot]
        cols_first = jax.random.permutation(key_first, LON_BLOCKS)[:2]
        cols_second = jax.random.permutation(key_second, LON_BLOCKS)[:2]
        dev_row = dev_index // LON_BLOCKS
        owner_row = (dev_row + corner // 2) % LAT_TILES
        owner_col = jnp.where(corner // 2 == 0, cols_first[corner % 2], cols_second[corner % 2])
        local_block = jax.random.randint(key_local, (entries,), 0, ATM_DEV)
        return (owner_row * LON_BLOCKS + owner_col) * ATM_DEV + local_block
    owner_table = jax.vmap(draw_device)(jnp.arange(device_count))
    owner_table = owner_table.reshape(LAT_TILES, LON_BLOCKS, ROWS_DEV, INTERSECTIONS).transpose(0, 2, 1, 3)
    return owner_table.reshape(LAT_TILES * ROWS_DEV, LON_BLOCKS, INTERSECTIONS).astype(jnp.int32)


def with_ends(values, rng, least, high):
    longest = values.shape.index(max(values.shape))
    spots = []
    for shift in (0, 1):
        where = [jax.random.randint(jax.random.fold_in(rng, axis), (), 0, length) for axis, length in enumerate(values.shape)]
        where[longest] = (where[longest] + shift) % values.shape[longest]
        spots.append(tuple(where))
    return values.at[spots[0]].set(least).at[spots[1]].set(high)


def block_scale(key, extent, cuts, low, largest):
    level, own = 1.0, jax.random.fold_in(key, 6)
    for axis_at, blocks in cuts:
        steps = jnp.exp(jax.random.uniform(jax.random.fold_in(own, axis_at), (blocks,), jnp.float32, low / len(cuts), largest / len(cuts)))
        level = level * jnp.repeat(steps, extent[axis_at] // blocks).reshape([-1 if axis == axis_at else 1 for axis in range(len(extent))])
    return level


def centred(stream_key, extent, deviation, limit, cuts=(), dtype=jnp.bfloat16):
    drawn = jax.random.normal(stream_key, extent, jnp.float32) * deviation
    if len(cuts) > 0:
        drawn = block_scale(stream_key, extent, cuts, -0.22, 0.18) * drawn
    return jnp.clip(drawn, min=-limit, max=limit).astype(dtype)


def setup_inputs(seed: int = 0) -> dict:
    arg_keys = jax.random.split(jax.random.key(seed), 11)
    state = centred(arg_keys[0], (MEMBERS, NLAT, NLON, C), 1.0, 6.0, ((0, 4), (1, 2), (2, 4)))
    state_cot = centred(arg_keys[1], (MEMBERS, NLAT, NLON, C), 1.0, 6.0, ((0, 4), (1, 2), (2, 4)))
    flux_cot = centred(arg_keys[2], (MEMBERS, ATM_BLOCKS, FLUX, BLOCK), 1.0, 6.0, ((0, 4), (1, 8)))
    conv_weight = centred(arg_keys[3], (9, C, C), (9 * C) ** -0.5, 0.125)
    mix_weight = centred(arg_keys[4], (C, C), C ** -0.5, 0.375)
    flux_weight = centred(arg_keys[5], (FLUX, C), 0.5, 3.0)
    regrid_weights = centred(arg_keys[6], (NMAT, BLOCK, BLOCK), BLOCK ** -0.5, 0.5)
    intersection_atm = draw_intersection_atm(jax.random.fold_in(arg_keys[10], 71), 0)
    intersection_offset = with_ends(jax.random.randint(arg_keys[8], (NLAT, LON_BLOCKS, INTERSECTIONS), 0, NMAT), jax.random.fold_in(arg_keys[8], 1), 0, NMAT - 1).astype(jnp.int32)
    wet_rows = with_ends(jax.random.randint(arg_keys[9], (LAT_TILES, LON_BLOCKS), 1, ROWS_DEV + 1), jax.random.fold_in(arg_keys[9], 1), 1, ROWS_DEV).astype(jnp.int32)
    return {"state": state, "state_cot": state_cot, "flux_cot": flux_cot, "conv_weight": conv_weight, "mix_weight": mix_weight, "flux_weight": flux_weight, "regrid_weights": regrid_weights, "intersection_atm": intersection_atm, "intersection_offset": intersection_offset, "wet_rows": wet_rows}


def rim_pad(field):
    padded = jnp.pad(field, ((1, 1), (0, 0), (0, 0)))
    return jnp.concatenate([padded[:, -1:], padded, padded[:, :1]], axis=1)

def one_member(tile_state, tile_cot, member_flux, conv_weight, mix_weight, flux_weight, regrid_weights, intersection_atm, intersection_offset, wet_mask):
    lat_rows, lon_cells, channels = tile_state.shape
    padded = rim_pad(tile_state)
    hidden = jnp.zeros((lat_rows * lon_cells, channels), jnp.float32)
    for tap_index in range(9):
        tap_row, tap_col = (tap_index // 3, tap_index % 3)
        patch_rows = padded[tap_row:tap_row + lat_rows, tap_col:tap_col + lon_cells].reshape(-1, channels)
        hidden = hidden + jnp.dot(patch_rows, conv_weight[tap_index], preferred_element_type=jnp.float32)
    activation = jax.nn.silu(hidden).astype(jnp.bfloat16)
    flux_cells = jnp.zeros((lat_rows, LON_BLOCKS, FLUX, BLOCK), jnp.float32)
    for intersection in range(INTERSECTIONS):
        picked_cot = member_flux[intersection_atm[:, :, intersection]].astype(jnp.float32)
        picked_maps = regrid_weights[intersection_offset[:, :, intersection]].astype(jnp.float32)
        contribution = jnp.einsum('ijfa,ijoa->ijfo', picked_cot, picked_maps).astype(jnp.bfloat16)
        contribution = lax.optimization_barrier(contribution)
        flux_cells = flux_cells + contribution.astype(jnp.float32)
    flux_cells = flux_cells * wet_mask[:, :, None, None]
    cot_flat = tile_cot.reshape(-1, channels)
    act_grad = lax.dot_general(cot_flat, mix_weight, (((1,), (1,)), ((), ())), preferred_element_type=jnp.float32)
    act_grad = act_grad + jnp.einsum('ijfb,fc->ijbc', flux_cells, flux_weight.astype(jnp.float32)).reshape(-1, channels)
    gate_sig = jax.nn.sigmoid(hidden)
    hidden_grad = (act_grad * gate_sig * (1.0 + hidden * (1.0 - gate_sig))).astype(jnp.bfloat16)
    padded_grad = rim_pad(hidden_grad.reshape(lat_rows, lon_cells, channels))
    input_grad = cot_flat.astype(jnp.float32)
    tap_grads = []
    for tap_index in range(9):
        tap_row, tap_col = (tap_index // 3, tap_index % 3)
        back_rows = padded_grad[2 - tap_row:2 - tap_row + lat_rows, 2 - tap_col:2 - tap_col + lon_cells].reshape(-1, channels)
        input_grad = input_grad + lax.dot_general(back_rows, conv_weight[tap_index], (((1,), (1,)), ((), ())), preferred_element_type=jnp.float32)
        patch_rows = padded[tap_row:tap_row + lat_rows, tap_col:tap_col + lon_cells].reshape(-1, channels)
        tap_grads.append(lax.dot_general(patch_rows, hidden_grad, (((0,), (0,)), ((), ())), preferred_element_type=jnp.float32))
    tap_grads.append(lax.dot_general(activation, cot_flat, (((0,), (0,)), ((), ())), preferred_element_type=jnp.float32))
    weight_term = jnp.concatenate(tap_grads, axis=0)
    flux_term = jnp.einsum('ijfb,ijbc->fc', flux_cells, activation.reshape(lat_rows, LON_BLOCKS, BLOCK, channels).astype(jnp.float32))
    return (input_grad.reshape(lat_rows, lon_cells, channels).astype(jnp.bfloat16), weight_term, flux_term)

def reference(state, state_cot, flux_cot, conv_weight, mix_weight, flux_weight, regrid_weights, intersection_atm, intersection_offset, wet_rows):
    row_local = jnp.arange(NLAT).astype(jnp.int32) % ROWS_DEV
    wet_counts = jnp.repeat(wet_rows, ROWS_DEV, axis=0)
    wet_mask = (row_local[:, None] < wet_counts).astype(jnp.float32)

    def member_step(inputs):
        return one_member(inputs[0], inputs[1], inputs[2], conv_weight, mix_weight, flux_weight, regrid_weights, intersection_atm, intersection_offset, wet_mask)
    input_grad, weight_terms, flux_terms = lax.map(member_step, (state, state_cot, flux_cot))
    grad_scale = 1.0 / math.sqrt(MEMBERS * NLAT * NLON)
    weight_grads = lax.optimization_barrier(jnp.sum(weight_terms, axis=0)) * grad_scale
    flux_grad = lax.optimization_barrier(jnp.sum(flux_terms, axis=0)) * grad_scale
    return (input_grad, weight_grads, flux_grad)
```

```python
import functools
import math

import jax
import jax.numpy as jnp
from jax import lax
from jax.experimental import pallas as pl
from jax.experimental.pallas import tpu as pltpu
from jax.sharding import PartitionSpec as P

CAP = 5


def with_halo(cells, sides, width):
    for axis, dim in sides:
        count = lax.axis_size(axis)
        head = lax.slice_in_dim(cells, 0, width, axis=dim)
        tail = lax.slice_in_dim(cells, cells.shape[dim] - width, cells.shape[dim], axis=dim)
        cells = jnp.concatenate(
            [
                lax.ppermute(tail, axis, [(i, (i + 1) % count) for i in range(count)]),
                cells,
                lax.ppermute(head, axis, [((i + 1) % count, i) for i in range(count)]),
            ],
            axis=dim,
        )
    return cells


def shifted(value, axis, steps):
    count = lax.axis_size(axis)
    pairs = [(source, (source + steps) % count) for source in range(count)]
    return lax.ppermute(value, axis, pairs)


def zero_ends(padded, row_index, lat_tiles):
    top_keep = jnp.where(row_index > 0, 1.0, 0.0).astype(padded.dtype)
    bottom = jnp.where(row_index < lat_tiles - 1, 1.0, 0.0).astype(padded.dtype)
    return jnp.concatenate([padded[:1] * top_keep, padded[1:-1], padded[-1:] * bottom], axis=0)


def owner_rank(owners):
    entry_count = owners.shape[-1]
    same_owner = owners[..., :, None] == owners[..., None, :]
    earlier = jnp.arange(entry_count)[None, :] < jnp.arange(entry_count)[:, None]
    return jnp.sum(jnp.logical_and(same_owner, earlier), axis=-1)


def body(
    state,
    state_cot,
    flux_cot,
    conv_weight,
    mix_weight,
    flux_weight,
    regrid_weights,
    intersection_atm,
    intersection_offset,
    wet_rows,
):
    lat_tiles = lax.axis_size("oy")
    lon_tiles = lax.axis_size("ox")
    members = lax.axis_size("ens")
    row_index = lax.axis_index("oy")
    col_index = lax.axis_index("ox")
    tile_state = state[0]
    tile_rows, block_cells, channels = tile_state.shape
    cot_flat = state_cot[0].reshape(-1, channels)
    grad_scale = 1.0 / math.sqrt(members * lat_tiles * tile_rows * lon_tiles * block_cells)
    padded = with_halo(tile_state, (("oy", 0), ("ox", 1)), 1)
    padded = zero_ends(padded, row_index, lat_tiles)
    hidden = jnp.zeros((tile_rows * block_cells, channels), jnp.float32)
    for tap_index in range(9):
        tap_row, tap_col = (tap_index // 3, tap_index % 3)
        patch_rows = padded[tap_row : tap_row + tile_rows, tap_col : tap_col + block_cells].reshape(
            -1, channels
        )
        hidden = hidden + jnp.dot(
            patch_rows, conv_weight[tap_index], preferred_element_type=jnp.float32
        )
    activation = jax.nn.silu(hidden).astype(jnp.bfloat16)
    atm_dev = flux_cot.shape[1]
    cot_blocks = flux_cot[0]
    flux_fields = cot_blocks.shape[1]
    intersections = intersection_atm.shape[2]
    entries = tile_rows * intersections
    per_dev = (
        intersection_atm.reshape(lat_tiles, tile_rows, lon_tiles, intersections)
        .transpose(0, 2, 1, 3)
        .reshape(lat_tiles, lon_tiles, entries)
    )
    per_dev_offset = (
        intersection_offset.reshape(lat_tiles, tile_rows, lon_tiles, intersections)
        .transpose(0, 2, 1, 3)
        .reshape(lat_tiles, lon_tiles, entries)
    )
    band_rows = jnp.stack([row_index, (row_index + lat_tiles - 1) % lat_tiles])
    candidate = jnp.take(per_dev, band_rows, axis=0)
    candidate_offset = jnp.take(per_dev_offset, band_rows, axis=0)
    flat_index = row_index * lon_tiles + col_index
    candidate_owner = candidate // atm_dev
    is_mine = candidate_owner == flat_index
    slot_rank = owner_rank(candidate_owner)
    local_block = jnp.where(is_mine, candidate % atm_dev, 0)
    picked_cot = cot_blocks[local_block]
    picked_maps = regrid_weights[candidate_offset]
    products = jnp.einsum(
        "qsefa,qseoa->qsefo", picked_cot, picked_maps, preferred_element_type=jnp.float32
    )
    one_hot = jnp.logical_and(
        slot_rank[..., None] == jnp.arange(CAP)[None, None, None, :], is_mine[..., None]
    ).astype(jnp.float32)
    outbound = jnp.einsum("qsec,qsefo->qscfo", one_hot, products).astype(jnp.bfloat16)
    own_entries = per_dev[row_index, col_index]
    own_owner = own_entries // atm_dev
    own_slot = owner_rank(own_owner)
    same_in, next_in = (
        lax.all_to_all(outbound[0], "ox", split_axis=0, concat_axis=0, tiled=True),
        lax.all_to_all(outbound[1], "ox", split_axis=0, concat_axis=0, tiled=True),
    )
    next_in = shifted(next_in, "oy", -1)
    arrived = jnp.concatenate([same_in, next_in], axis=0).reshape(-1, flux_fields, block_cells)
    in_next = (own_owner // lon_tiles != row_index).astype(jnp.int32)
    slot_index = (in_next * lon_tiles + own_owner % lon_tiles) * CAP + own_slot
    values = (
        arrived[slot_index]
        .astype(jnp.float32)
        .reshape(tile_rows, intersections, flux_fields, block_cells)
    )
    wet_mask = (jnp.arange(tile_rows) < wet_rows[0, 0]).astype(jnp.float32)
    flux_cells = jnp.sum(values, axis=1) * wet_mask[:, None, None]
    act_grad = lax.dot_general(
        cot_flat, mix_weight, (((1,), (1,)), ((), ())), preferred_element_type=jnp.float32
    )
    act_grad = act_grad + jnp.einsum(
        "rfb,fc->rbc", flux_cells, flux_weight.astype(jnp.float32)
    ).reshape(-1, channels)
    gate_sig = jax.nn.sigmoid(hidden)
    hidden_grad = (act_grad * gate_sig * (1.0 + hidden * (1.0 - gate_sig))).astype(jnp.bfloat16)
    padded_grad = with_halo(
        hidden_grad.reshape(tile_rows, block_cells, channels), (("oy", 0), ("ox", 1)), 1
    )
    padded_grad = zero_ends(padded_grad, row_index, lat_tiles)
    input_grad = cot_flat.astype(jnp.float32)
    tap_grads = []
    for tap_index in range(9):
        tap_row, tap_col = (tap_index // 3, tap_index % 3)
        back_rows = padded_grad[
            2 - tap_row : 2 - tap_row + tile_rows, 2 - tap_col : 2 - tap_col + block_cells
        ].reshape(-1, channels)
        input_grad = input_grad + lax.dot_general(
            back_rows,
            conv_weight[tap_index],
            (((1,), (1,)), ((), ())),
            preferred_element_type=jnp.float32,
        )
        patch_rows = padded[tap_row : tap_row + tile_rows, tap_col : tap_col + block_cells].reshape(
            -1, channels
        )
        tap_grads.append(
            lax.dot_general(
                patch_rows,
                hidden_grad,
                (((0,), (0,)), ((), ())),
                preferred_element_type=jnp.float32,
            )
        )
    tap_grads.append(
        lax.dot_general(
            activation, cot_flat, (((0,), (0,)), ((), ())), preferred_element_type=jnp.float32
        )
    )
    weight_term = jnp.concatenate(tap_grads, axis=0) * grad_scale
    flux_term = (
        jnp.einsum(
            "rfb,rbc->fc",
            flux_cells,
            activation.reshape(tile_rows, block_cells, channels).astype(jnp.float32),
        )
        * grad_scale
    )
    weight_rows = lax.psum_scatter(weight_term, ("oy", "ox"), scatter_dimension=0, tiled=True)
    weight_out = lax.psum(weight_rows, "ens")
    flux_total = lax.psum(flux_term, ("ens", "oy", "ox"))
    input_out = input_grad.reshape(1, tile_rows, block_cells, channels).astype(jnp.bfloat16)
    return (input_out, weight_out, flux_total)


F32 = jnp.float32
BF16 = jnp.bfloat16
MESH = pl.DeviceIdType.MESH
EDGE = 16


def dot(a, b, dims=((1,), (0,))):
    return lax.dot_general(a, b, (dims, ((), ())), preferred_element_type=F32)


def remote(src, dst, send_sem, recv_sem, target):
    return pltpu.make_async_remote_copy(
        src_ref=src,
        dst_ref=dst,
        send_sem=send_sem,
        recv_sem=recv_sem,
        device_id=target,
        device_id_type=MESH,
    )


def start_all(copies):
    for copy in copies:
        copy.start()
    return copies


def halo_copies(src, src_at, padded, rows, cells, lat, lon, lon_tiles, sems):
    row0, col0 = src_at
    other = 1 - lat
    east = lax.rem(lon + 1, lon_tiles)
    west = lax.rem(lon + lon_tiles - 1, lon_tiles)
    edge_row = row0 + other * (rows - 1)
    land_row = lat * (rows + 1)
    body_rows, dst_rows = pl.ds(row0, rows), pl.ds(1, rows)
    head, last = pl.ds(col0, EDGE), pl.ds(col0 + cells - EDGE, EDGE)
    left, middle, right = pl.ds(0, EDGE), pl.ds(EDGE, cells), pl.ds(EDGE + cells, EDGE)
    plan = [
        (src.at[pl.ds(edge_row, 1), pl.ds(col0, cells)], padded.at[pl.ds(land_row, 1), middle], other, lon),
        (src.at[body_rows, last], padded.at[dst_rows, left], lat, east),
        (src.at[body_rows, head], padded.at[dst_rows, right], lat, west),
        (src.at[pl.ds(edge_row, 1), last], padded.at[pl.ds(land_row, 1), left], other, east),
        (src.at[pl.ds(edge_row, 1), head], padded.at[pl.ds(land_row, 1), right], other, west),
    ]
    send, recv = sems
    return [
        remote(a, b, send.at[n], recv.at[n], {"oy": y, "ox": x})
        for n, (a, b, y, x) in enumerate(plan)
    ]


def exchange(axis, count, me, source, target, sems, base=0):
    send, recv = sems
    copies = []
    for step in range(1, count):
        to = lax.rem(me + step, count)
        copies.append(
            remote(source(to), target(me), send.at[base + step - 1], recv.at[base + step - 1], {axis: to})
        )
    return copies


def shift_cells(padded, wide, shifts, rows, cells):
    for row in range(rows + 2):
        wide[row] = padded[row].astype(F32)
        for col in range(3):
            shifts[col, row] = wide[row, pl.ds(EDGE - 1 + col, cells), :].astype(BF16)


def fused_kernel(
    sizes,
    state,
    cot,
    flux_cot,
    conv,
    mix,
    flux_weight,
    regrid,
    atm,
    offset,
    wet,
    input_out,
    weight_out,
    flux_out,
    padded,
    padded_grad,
    wide,
    shifts,
    turned,
    grad_shifts,
    entry_cell,
    entry_map,
    flux_send,
    flux_recv,
    flux_rows,
    grads,
    grads_half,
    recv_lat,
    sum_lat,
    recv_ens,
    sum_ens,
    recv_lon,
    rows_all,
    flux_lat,
    flux_ens,
    flux_lon,
    state_sems,
    grad_sems,
    flux_sems,
    lat_sems,
    ens_sems,
    lon_sems,
    out_sems,
):
    members, lat_tiles, lon_tiles, grad_scale = sizes
    ens, lat, lon = lax.axis_index("ens"), lax.axis_index("oy"), lax.axis_index("ox")
    rows, cells, channels = state.shape
    fields = flux_weight.shape[0]
    intersections = atm.shape[2]
    maps = regrid.shape[0]
    tiles = lat_tiles * lon_tiles
    flat = lat * lon_tiles + lon
    blocks = flux_cot.shape[0] // fields

    barrier = pltpu.get_barrier_semaphore()
    for step in range(1, tiles):
        peer = lax.rem(flat + step, tiles)
        pl.semaphore_signal(
            barrier, inc=1, device_id={"oy": peer // lon_tiles, "ox": lax.rem(peer, lon_tiles)}, device_id_type=MESH
        )
    for step in range(1, members):
        pl.semaphore_signal(
            barrier, inc=1, device_id={"ens": lax.rem(ens + step, members)}, device_id_type=MESH
        )

    field_iota = lax.broadcasted_iota(jnp.int32, (fields, cells), 0)
    entry = 0
    for k in range(intersections):
        for tile in range(tiles):
            for row in range(rows):
                at = ((tile // lon_tiles) * rows + row, tile % lon_tiles, k)
                block = atm[at]
                local = jnp.where(block // blocks == flat, lax.rem(block, blocks) * fields, -fields)
                entry_cell[pl.ds(entry, fields), :] = field_iota + local
                entry_map[pl.ds(entry, fields), :] = jnp.full((fields, cells), offset[at], jnp.int32)
                entry += fields
    which_cell = entry_cell[...]
    which_map = entry_map[...]
    lane = lax.broadcasted_iota(jnp.int32, which_cell.shape, 1)
    picked = jnp.zeros(which_cell.shape, F32)
    for part in range(blocks * fields // cells):
        one_hot = jnp.where(which_cell == lane + part * cells, 1.0, 0.0).astype(BF16)
        picked = picked + dot(one_hot, flux_cot[pl.ds(part * cells, cells), :])
    products = jnp.zeros(which_cell.shape, F32)
    for m in range(maps):
        chosen = jnp.where(which_map == m, picked, 0.0).astype(BF16)
        products = products + dot(chosen, regrid[m], ((1,), (1,)))
    products = products.astype(BF16).astype(F32)
    span = tiles * rows * fields
    share = products[:span]
    for k in range(1, intersections):
        share = share + products[k * span : (k + 1) * span]
    flux_send[...] = share.reshape(flux_send.shape)
    flux_recv[pl.ds(flat, 1)] = flux_send[pl.ds(flat, 1)]

    outside = lat * (rows + 1)
    padded[pl.ds(outside, 1)] = jnp.zeros((1,) + padded.shape[1:], BF16)
    padded_grad[pl.ds(outside, 1)] = jnp.zeros((1,) + padded.shape[1:], BF16)
    padded[1 : rows + 1, EDGE : EDGE + cells] = state[...]
    flux_rows[...] = jnp.zeros(flux_rows.shape, F32)
    for n in range(2 * rows):
        flux_rows[n * fields : (n + 1) * fields, :] = flux_weight[...].astype(F32)

    pl.semaphore_wait(barrier, tiles - 1 + members - 1)
    state_copies = start_all(
        halo_copies(state, (0, 0), padded, rows, cells, lat, lon, lon_tiles, state_sems)
    )
    flux_copies = []
    for step in range(1, tiles):
        peer = lax.rem(flat + step, tiles)
        flux_copies.append(
            remote(
                flux_send.at[peer],
                flux_recv.at[flat],
                flux_sems[0].at[step - 1],
                flux_sems[1].at[step - 1],
                {"oy": peer // lon_tiles, "ox": lax.rem(peer, lon_tiles)},
            )
        )
    start_all(flux_copies)

    cot_flat = cot[...].reshape(rows * cells, channels)
    act_grad = dot(cot_flat, mix[...], ((1,), (1,)))
    for copy in state_copies:
        copy.wait_recv()
    shift_cells(padded, wide, shifts, rows, cells)
    hidden = jnp.zeros((rows * cells, channels), F32)
    for tap in range(9):
        p, q = tap // 3, tap % 3
        hidden = hidden + dot(shifts[q, p : p + rows].reshape(rows * cells, channels), conv[tap])
    gate = jax.nn.sigmoid(hidden)
    activation = (hidden * gate).astype(BF16)
    slope = gate * (1.0 + hidden * (1.0 - gate))
    for q in range(3):
        turned[q] = shifts[q].reshape((rows + 2) * cells, channels).T

    for copy in flux_copies:
        copy.wait_recv()
    row_iota = lax.broadcasted_iota(jnp.int32, (rows * fields, cells), 0) // fields
    flux = flux_recv[0]
    for tile in range(1, tiles):
        flux = flux + flux_recv[tile]
    flux = jnp.where(row_iota < wet[0, 0], flux, 0.0)
    flux_high = flux.astype(BF16).astype(F32)
    flux_low = flux - flux_high
    both = jnp.concatenate([flux_high, flux_low], axis=0)
    both_iota = jnp.concatenate([row_iota, row_iota], axis=0)
    heads = flux_rows[...].astype(BF16)
    flux_term = jnp.zeros((2 * rows * fields, channels), F32)
    for row in range(rows):
        mine = jnp.where(both_iota == row, both, 0.0).astype(BF16)
        here = slice(row * cells, (row + 1) * cells)
        extra = dot(mine, heads, ((0,), (0,)))
        grad = ((act_grad[here] + extra) * slope[here]).astype(BF16)
        padded_grad[row + 1, EDGE : EDGE + cells] = grad
        flux_term = flux_term + dot(mine, activation[here])
    grad_copies = start_all(
        halo_copies(padded_grad, (1, EDGE), padded_grad, rows, cells, lat, lon, lon_tiles, grad_sems)
    )

    flux_rows[...] = flux_term
    total = flux_rows[:fields, :]
    for n in range(1, 2 * rows):
        total = total + flux_rows[n * fields : (n + 1) * fields, :]
    flux_lat[pl.ds(lat, 1)] = jnp.zeros((1,) + flux_lat.shape[1:], F32)
    flux_lat[pl.ds(lat, 1), 0:fields, :] = total[None]

    hidden_grad = padded_grad[1 : rows + 1, EDGE : EDGE + cells].reshape(rows * cells, channels)
    for tap in range(10):
        p, q = tap // 3, tap % 3
        if tap < 9:
            term = dot(turned[q, :, p * cells : (p + rows) * cells], hidden_grad)
        else:
            term = dot(activation, cot_flat, ((0,), (0,)))
        grads[tap * channels : (tap + 1) * channels, :] = term
        grads_half[tap * channels : (tap + 1) * channels, :] = term.astype(BF16)

    band = grads.shape[0] // lat_tiles
    lat_copies = start_all(
        exchange(
            "oy",
            lat_tiles,
            lat,
            lambda to: grads_half.at[pl.ds(pl.multiple_of(to * band, band), band)],
            lambda me: recv_lat,
            lat_sems,
        )
        + exchange("oy", lat_tiles, lat, lambda to: flux_lat.at[lat], lambda me: flux_lat.at[me], lat_sems, lat_tiles)
    )
    for copy in lat_copies:
        copy.wait_recv()
    own = grads[pl.ds(pl.multiple_of(lat * band, band), band), :]
    sum_lat[...] = (own + recv_lat[...].astype(F32)).astype(BF16).reshape(sum_lat.shape)
    total = flux_lat[0]
    for n in range(1, lat_tiles):
        total = total + flux_lat[n]
    flux_ens[pl.ds(ens, 1)] = total[None]
    ens_copies = start_all(
        exchange("ens", members, ens, lambda to: sum_lat.at[:, to], lambda me: recv_ens.at[me], ens_sems)
        + exchange("ens", members, ens, lambda to: flux_ens.at[ens], lambda me: flux_ens.at[me], ens_sems, members)
    )
    recv_ens[pl.ds(ens, 1)] = sum_lat[:, pl.ds(ens, 1)].reshape((1,) + recv_ens.shape[1:])

    for copy in grad_copies:
        copy.wait_recv()
    shift_cells(padded_grad, wide, grad_shifts, rows, cells)
    input_grad = cot_flat.astype(F32)
    for tap in range(9):
        p, q = tap // 3, tap % 3
        back = grad_shifts[2 - q, 2 - p : 2 - p + rows].reshape(rows * cells, channels)
        input_grad = input_grad + dot(back, conv[tap], ((1,), (1,)))
    input_out[...] = input_grad.astype(BF16).reshape(input_out.shape)

    for copy in ens_copies:
        copy.wait_recv()
    total = recv_ens[0].astype(F32)
    for n in range(1, members):
        total = total + recv_ens[n].astype(F32)
    sum_ens[...] = total.astype(BF16)
    total = flux_ens[0]
    for n in range(1, members):
        total = total + flux_ens[n]
    flux_lon[pl.ds(lon, 1)] = total[None]
    lon_copies = start_all(
        exchange("ox", lon_tiles, lon, lambda to: sum_ens.at[to], lambda me: recv_lon.at[me], lon_sems)
        + exchange("ox", lon_tiles, lon, lambda to: flux_lon.at[lon], lambda me: flux_lon.at[me], lon_sems, lon_tiles)
    )
    recv_lon[pl.ds(lon, 1)] = sum_ens[pl.ds(lon, 1)]
    for copy in lon_copies:
        copy.wait_recv()
    total = recv_lon[0].astype(F32)
    for n in range(1, lon_tiles):
        total = total + recv_lon[n].astype(F32)
    rows_all[pl.ds(ens, 1)] = (total * grad_scale).astype(BF16)[None]
    out_copies = start_all(
        exchange("ens", members, ens, lambda to: rows_all.at[ens], lambda me: rows_all.at[me], out_sems)
    )
    total = flux_lon[0]
    for n in range(1, lon_tiles):
        total = total + flux_lon[n]
    flux_out[...] = total[:fields] * grad_scale
    for copy in out_copies:
        copy.wait_recv()
    weight_out[...] = rows_all[...].astype(F32).reshape(weight_out.shape)
    for copy in state_copies + flux_copies + grad_copies + lat_copies + ens_copies + lon_copies + out_copies:
        copy.wait_send()


def fused_body(
    state,
    state_cot,
    flux_cot,
    conv_weight,
    mix_weight,
    flux_weight,
    regrid_weights,
    intersection_atm,
    intersection_offset,
    wet_rows,
):
    members, lat_tiles, lon_tiles = (lax.axis_size(name) for name in ("ens", "oy", "ox"))
    tile = state.shape[1:]
    rows, cells, channels = tile
    fields = flux_weight.shape[0]
    tiles = lat_tiles * lon_tiles
    grad_rows = (conv_weight.shape[0] + 1) * channels
    band = grad_rows // lat_tiles
    sub = band // lon_tiles // members
    grad_scale = 1.0 / math.sqrt(members * lat_tiles * rows * lon_tiles * cells)
    entries = tiles * rows * intersection_atm.shape[2] * fields
    halo = (rows + 2, cells + 2 * EDGE, channels)
    spread = (3, rows + 2, cells, channels)
    small = 2 * fields

    def pair(count):
        return (pltpu.SemaphoreType.DMA((count,)), pltpu.SemaphoreType.DMA((count,)))

    vmem = pl.BlockSpec(memory_space=pltpu.VMEM)
    smem = pl.BlockSpec(memory_space=pltpu.SMEM)
    scratch = [
        pltpu.VMEM(halo, BF16),
        pltpu.VMEM(halo, BF16),
        pltpu.VMEM(halo, F32),
        pltpu.VMEM(spread, BF16),
        pltpu.VMEM((3, channels, (rows + 2) * cells), BF16),
        pltpu.VMEM(spread, BF16),
        pltpu.VMEM((entries, cells), jnp.int32),
        pltpu.VMEM((entries, cells), jnp.int32),
        pltpu.VMEM((tiles, rows * fields, cells), F32),
        pltpu.VMEM((tiles, rows * fields, cells), F32),
        pltpu.VMEM((2 * rows * fields, channels), F32),
        pltpu.VMEM((grad_rows, channels), F32),
        pltpu.VMEM((grad_rows, channels), BF16),
        pltpu.VMEM((band, channels), BF16),
        pltpu.VMEM((lon_tiles, members, sub, channels), BF16),
        pltpu.VMEM((members, lon_tiles, sub, channels), BF16),
        pltpu.VMEM((lon_tiles, sub, channels), BF16),
        pltpu.VMEM((lon_tiles, sub, channels), BF16),
        pltpu.VMEM((members, sub, channels), BF16),
        pltpu.VMEM((lat_tiles, small, channels), F32),
        pltpu.VMEM((members, small, channels), F32),
        pltpu.VMEM((lon_tiles, small, channels), F32),
        pair(5),
        pair(5),
        pair(tiles),
        pair(2 * lat_tiles),
        pair(2 * members),
        pair(2 * lon_tiles),
        pair(members),
    ]
    cost = pl.CostEstimate(
        flops=2 * rows * cells * channels * channels * 29, bytes_accessed=3 << 20, transcendentals=rows * cells * channels
    )
    input_grad, weight_grads, flux_grad = pl.pallas_call(
        functools.partial(fused_kernel, (members, lat_tiles, lon_tiles, grad_scale)),
        out_shape=(
            jax.ShapeDtypeStruct(state.shape, BF16),
            jax.ShapeDtypeStruct((band // lon_tiles, channels), F32),
            jax.ShapeDtypeStruct((fields, channels), F32),
        ),
        in_specs=[vmem] * 7 + [smem] * 3,
        out_specs=(vmem, vmem, vmem),
        scratch_shapes=scratch,
        cost_estimate=cost,
        compiler_params=pltpu.CompilerParams(
            collective_id=0, has_side_effects=True, vmem_limit_bytes=48 << 20
        ),
    )(
        state[0],
        state_cot[0],
        flux_cot[0].reshape(-1, cells),
        conv_weight,
        mix_weight,
        flux_weight,
        regrid_weights,
        intersection_atm,
        intersection_offset,
        wet_rows,
    )
    return input_grad, weight_grads, flux_grad


def step(state, state_cot, flux_cot, conv_weight, *rest):
    members, lat_tiles, lon_tiles = (lax.axis_size(name) for name in ("ens", "oy", "ox"))
    grad_rows = (conv_weight.shape[0] + 1) * state.shape[3]
    whole_tiles = grad_rows % (lat_tiles * lon_tiles * members * EDGE) == 0
    fused = lat_tiles == 2 and lon_tiles > 1 and whole_tiles
    return (fused_body if fused else body)(state, state_cot, flux_cot, conv_weight, *rest)


def solution(mesh):
    in_specs = (
        P("ens", "oy", "ox", None),
        P("ens", "oy", "ox", None),
        P("ens", ("oy", "ox"), None, None),
        P(),
        P(),
        P(),
        P(),
        P(),
        P(),
        P("oy", "ox"),
    )
    out_specs = (P("ens", "oy", "ox", None), P(("oy", "ox"), None), P())
    return jax.shard_map(step, mesh=mesh, in_specs=in_specs, out_specs=out_specs, check_vma=False)
```

```python
import functools
import math

import jax
import jax.numpy as jnp
from jax import lax
from jax.experimental import pallas as pl
from jax.experimental.pallas import tpu as pltpu
from jax.sharding import PartitionSpec as P

CAP = 5


def with_halo(cells, sides, width):
    for axis, dim in sides:
        count = lax.axis_size(axis)
        head = lax.slice_in_dim(cells, 0, width, axis=dim)
        tail = lax.slice_in_dim(cells, cells.shape[dim] - width, cells.shape[dim], axis=dim)
        cells = jnp.concatenate(
            [
                lax.ppermute(tail, axis, [(i, (i + 1) % count) for i in range(count)]),
                cells,
                lax.ppermute(head, axis, [((i + 1) % count, i) for i in range(count)]),
            ],
            axis=dim,
        )
    return cells


def shifted(value, axis, steps):
    count = lax.axis_size(axis)
    pairs = [(source, (source + steps) % count) for source in range(count)]
    return lax.ppermute(value, axis, pairs)


def zero_ends(padded, row_index, lat_tiles):
    top_keep = jnp.where(row_index > 0, 1.0, 0.0).astype(padded.dtype)
    bottom = jnp.where(row_index < lat_tiles - 1, 1.0, 0.0).astype(padded.dtype)
    return jnp.concatenate([padded[:1] * top_keep, padded[1:-1], padded[-1:] * bottom], axis=0)


def owner_rank(owners):
    entry_count = owners.shape[-1]
    same_owner = owners[..., :, None] == owners[..., None, :]
    earlier = jnp.arange(entry_count)[None, :] < jnp.arange(entry_count)[:, None]
    return jnp.sum(jnp.logical_and(same_owner, earlier), axis=-1)


def body(
    state,
    state_cot,
    flux_cot,
    conv_weight,
    mix_weight,
    flux_weight,
    regrid_weights,
    intersection_atm,
    intersection_offset,
    wet_rows,
):
    lat_tiles = lax.axis_size("oy")
    lon_tiles = lax.axis_size("ox")
    members = lax.axis_size("ens")
    row_index = lax.axis_index("oy")
    col_index = lax.axis_index("ox")
    tile_state = state[0]
    tile_rows, block_cells, channels = tile_state.shape
    cot_flat = state_cot[0].reshape(-1, channels)
    grad_scale = 1.0 / math.sqrt(members * lat_tiles * tile_rows * lon_tiles * block_cells)
    padded = with_halo(tile_state, (("oy", 0), ("ox", 1)), 1)
    padded = zero_ends(padded, row_index, lat_tiles)
    hidden = jnp.zeros((tile_rows * block_cells, channels), jnp.float32)
    for tap_index in range(9):
        tap_row, tap_col = (tap_index // 3, tap_index % 3)
        patch_rows = padded[tap_row : tap_row + tile_rows, tap_col : tap_col + block_cells].reshape(
            -1, channels
        )
        hidden = hidden + jnp.dot(
            patch_rows, conv_weight[tap_index], preferred_element_type=jnp.float32
        )
    activation = jax.nn.silu(hidden).astype(jnp.bfloat16)
    atm_dev = flux_cot.shape[1]
    cot_blocks = flux_cot[0]
    flux_fields = cot_blocks.shape[1]
    intersections = intersection_atm.shape[2]
    entries = tile_rows * intersections
    per_dev = (
        intersection_atm.reshape(lat_tiles, tile_rows, lon_tiles, intersections)
        .transpose(0, 2, 1, 3)
        .reshape(lat_tiles, lon_tiles, entries)
    )
    per_dev_offset = (
        intersection_offset.reshape(lat_tiles, tile_rows, lon_tiles, intersections)
        .transpose(0, 2, 1, 3)
        .reshape(lat_tiles, lon_tiles, entries)
    )
    band_rows = jnp.stack([row_index, (row_index + lat_tiles - 1) % lat_tiles])
    candidate = jnp.take(per_dev, band_rows, axis=0)
    candidate_offset = jnp.take(per_dev_offset, band_rows, axis=0)
    flat_index = row_index * lon_tiles + col_index
    candidate_owner = candidate // atm_dev
    is_mine = candidate_owner == flat_index
    slot_rank = owner_rank(candidate_owner)
    local_block = jnp.where(is_mine, candidate % atm_dev, 0)
    picked_cot = cot_blocks[local_block]
    picked_maps = regrid_weights[candidate_offset]
    products = jnp.einsum(
        "qsefa,qseoa->qsefo", picked_cot, picked_maps, preferred_element_type=jnp.float32
    )
    one_hot = jnp.logical_and(
        slot_rank[..., None] == jnp.arange(CAP)[None, None, None, :], is_mine[..., None]
    ).astype(jnp.float32)
    outbound = jnp.einsum("qsec,qsefo->qscfo", one_hot, products).astype(jnp.bfloat16)
    own_entries = per_dev[row_index, col_index]
    own_owner = own_entries // atm_dev
    own_slot = owner_rank(own_owner)
    same_in, next_in = (
        lax.all_to_all(outbound[0], "ox", split_axis=0, concat_axis=0, tiled=True),
        lax.all_to_all(outbound[1], "ox", split_axis=0, concat_axis=0, tiled=True),
    )
    next_in = shifted(next_in, "oy", -1)
    arrived = jnp.concatenate([same_in, next_in], axis=0).reshape(-1, flux_fields, block_cells)
    in_next = (own_owner // lon_tiles != row_index).astype(jnp.int32)
    slot_index = (in_next * lon_tiles + own_owner % lon_tiles) * CAP + own_slot
    values = (
        arrived[slot_index]
        .astype(jnp.float32)
        .reshape(tile_rows, intersections, flux_fields, block_cells)
    )
    wet_mask = (jnp.arange(tile_rows) < wet_rows[0, 0]).astype(jnp.float32)
    flux_cells = jnp.sum(values, axis=1) * wet_mask[:, None, None]
    act_grad = lax.dot_general(
        cot_flat, mix_weight, (((1,), (1,)), ((), ())), preferred_element_type=jnp.float32
    )
    act_grad = act_grad + jnp.einsum(
        "rfb,fc->rbc", flux_cells, flux_weight.astype(jnp.float32)
    ).reshape(-1, channels)
    gate_sig = jax.nn.sigmoid(hidden)
    hidden_grad = (act_grad * gate_sig * (1.0 + hidden * (1.0 - gate_sig))).astype(jnp.bfloat16)
    padded_grad = with_halo(
        hidden_grad.reshape(tile_rows, block_cells, channels), (("oy", 0), ("ox", 1)), 1
    )
    padded_grad = zero_ends(padded_grad, row_index, lat_tiles)
    input_grad = cot_flat.astype(jnp.float32)
    tap_grads = []
    for tap_index in range(9):
        tap_row, tap_col = (tap_index // 3, tap_index % 3)
        back_rows = padded_grad[
            2 - tap_row : 2 - tap_row + tile_rows, 2 - tap_col : 2 - tap_col + block_cells
        ].reshape(-1, channels)
        input_grad = input_grad + lax.dot_general(
            back_rows,
            conv_weight[tap_index],
            (((1,), (1,)), ((), ())),
            preferred_element_type=jnp.float32,
        )
        patch_rows = padded[tap_row : tap_row + tile_rows, tap_col : tap_col + block_cells].reshape(
            -1, channels
        )
        tap_grads.append(
            lax.dot_general(
                patch_rows,
                hidden_grad,
                (((0,), (0,)), ((), ())),
                preferred_element_type=jnp.float32,
            )
        )
    tap_grads.append(
        lax.dot_general(
            activation, cot_flat, (((0,), (0,)), ((), ())), preferred_element_type=jnp.float32
        )
    )
    weight_term = jnp.concatenate(tap_grads, axis=0) * grad_scale
    flux_term = (
        jnp.einsum(
            "rfb,rbc->fc",
            flux_cells,
            activation.reshape(tile_rows, block_cells, channels).astype(jnp.float32),
        )
        * grad_scale
    )
    weight_rows = lax.psum_scatter(weight_term, ("oy", "ox"), scatter_dimension=0, tiled=True)
    weight_out = lax.psum(weight_rows, "ens")
    flux_total = lax.psum(flux_term, ("ens", "oy", "ox"))
    input_out = input_grad.reshape(1, tile_rows, block_cells, channels).astype(jnp.bfloat16)
    return (input_out, weight_out, flux_total)


F32 = jnp.float32
BF16 = jnp.bfloat16
MESH = pl.DeviceIdType.MESH
EDGE = 16


def dot(a, b, dims=((1,), (0,))):
    return lax.dot_general(a, b, (dims, ((), ())), preferred_element_type=F32)


def remote(src, dst, send_sem, recv_sem, target):
    return pltpu.make_async_remote_copy(
        src_ref=src,
        dst_ref=dst,
        send_sem=send_sem,
        recv_sem=recv_sem,
        device_id=target,
        device_id_type=MESH,
    )


def start_all(copies):
    for copy in copies:
        copy.start()
    return copies


def halo_copies(src, src_at, padded, rows, cells, lat, lon, lon_tiles, sems):
    row0, col0 = src_at
    other = 1 - lat
    east = lax.rem(lon + 1, lon_tiles)
    west = lax.rem(lon + lon_tiles - 1, lon_tiles)
    edge_row = row0 + other * (rows - 1)
    land_row = lat * (rows + 1)
    body_rows, dst_rows = pl.ds(row0, rows), pl.ds(1, rows)
    head, last = pl.ds(col0, EDGE), pl.ds(col0 + cells - EDGE, EDGE)
    left, middle, right = pl.ds(0, EDGE), pl.ds(EDGE, cells), pl.ds(EDGE + cells, EDGE)
    plan = [
        (src.at[pl.ds(edge_row, 1), pl.ds(col0, cells)], padded.at[pl.ds(land_row, 1), middle], other, lon),
        (src.at[body_rows, last], padded.at[dst_rows, left], lat, east),
        (src.at[body_rows, head], padded.at[dst_rows, right], lat, west),
        (src.at[pl.ds(edge_row, 1), last], padded.at[pl.ds(land_row, 1), left], other, east),
        (src.at[pl.ds(edge_row, 1), head], padded.at[pl.ds(land_row, 1), right], other, west),
    ]
    send, recv = sems
    return [
        remote(a, b, send.at[n], recv.at[n], {"oy": y, "ox": x})
        for n, (a, b, y, x) in enumerate(plan)
    ]


def exchange(axis, count, me, source, target, sems, base=0):
    send, recv = sems
    copies = []
    for step in range(1, count):
        to = lax.rem(me + step, count)
        copies.append(
            remote(source(to), target(me), send.at[base + step - 1], recv.at[base + step - 1], {axis: to})
        )
    return copies


def wait_all(copies):
    for copy in copies:
        copy.wait_recv()


def shift_cells(padded, wide, columns, rows, cells, order):
    channels = padded.shape[2]
    for row in range(rows + 2):
        wide[row] = padded[row].astype(F32)
        for n, col in enumerate(order):
            here = slice(n * channels, (n + 1) * channels)
            if col == 1:
                columns[row, :, here] = padded[row, EDGE : EDGE + cells]
            else:
                columns[row, :, here] = wide[row, pl.ds(EDGE - 1 + col, cells), :].astype(BF16)


def store_rows(target, first, value):
    pieces, sub = target.shape[1:3]
    done = 0
    while done < value.shape[0]:
        at = first + done
        piece, row = at // sub, at % sub
        count = min(sub - row, value.shape[0] - done)
        target[piece // pieces, piece % pieces, row : row + count, :] = value[done : done + count].astype(
            target.dtype
        )
        done += count


def fused_kernel(
    sizes,
    state_in,
    cot_in,
    flux_cot_in,
    conv_in,
    mix_in,
    flux_weight_in,
    regrid_in,
    atm_in,
    offset_in,
    wet,
    input_out,
    weight_out,
    flux_out,
    cot,
    flux_cot,
    conv,
    mix,
    flux_weight,
    regrid,
    atm,
    offset,
    padded,
    padded_grad,
    wide,
    columns,
    turned,
    grad_columns,
    entry_cell,
    entry_map,
    flux_send,
    flux_recv,
    flux_rows,
    grads,
    grads_half,
    recv_lat,
    sum_lat,
    recv_ens,
    sum_ens,
    recv_lon,
    rows_all,
    flux_lat,
    flux_ens,
    flux_lon,
    load_sems,
    state_sems,
    grad_sems,
    flux_sems,
    flux_lat_sems,
    flux_ens_sems,
    flux_lon_sems,
    lat_sems,
    ens_sems,
    lon_sems,
    out_sems,
):
    members, lat_tiles, lon_tiles, grad_scale, chunks = sizes
    ens, lat, lon = lax.axis_index("ens"), lax.axis_index("oy"), lax.axis_index("ox")
    rows, cells, channels = cot.shape
    fields = flux_weight.shape[0]
    intersections = atm.shape[1]
    maps = regrid.shape[0]
    tiles = lat_tiles * lon_tiles
    flat = lat * lon_tiles + lon
    cells_here = flux_cot.shape[0]

    barrier = pltpu.get_barrier_semaphore()
    for step in range(1, tiles):
        peer = lax.rem(flat + step, tiles)
        pl.semaphore_signal(
            barrier, inc=1, device_id={"oy": peer // lon_tiles, "ox": lax.rem(peer, lon_tiles)}, device_id_type=MESH
        )
    for step in range(1, members):
        pl.semaphore_signal(
            barrier, inc=1, device_id={"ens": lax.rem(ens + step, members)}, device_id_type=MESH
        )
    loads = [
        pltpu.make_async_copy(src, dst, load_sems.at[n])
        for n, (src, dst) in enumerate(
            [
                (atm_in, atm),
                (offset_in, offset),
                (flux_cot_in, flux_cot),
                (regrid_in, regrid),
                (cot_in, cot),
                (mix_in, mix),
                (state_in, padded.at[pl.ds(1, rows), pl.ds(EDGE, cells)]),
                (flux_weight_in, flux_weight),
                (conv_in, conv),
            ]
        )
    ]
    for load in loads:
        load.start()

    loads[0].wait()
    loads[1].wait()
    entry = 0
    for k in range(intersections):
        for tile in range(tiles):
            for row in range(rows):
                at = (tile % lon_tiles, k, (tile // lon_tiles) * rows + row)
                entry_cell[pl.ds(entry, fields), :] = jnp.full((fields, cells), atm[at], jnp.int32)
                entry_map[pl.ds(entry, fields), :] = jnp.full((fields, cells), offset[at], jnp.int32)
                entry += fields
    field_iota = lax.broadcasted_iota(jnp.int32, entry_cell.shape, 0) % fields
    lane = lax.broadcasted_iota(jnp.int32, entry_cell.shape, 1)
    which_cell = entry_cell[...] * fields + (field_iota - lane - flat * cells_here)
    which_map = entry_map[...]
    loads[2].wait()
    one_hot = [
        jnp.where(which_cell == part * cells, 1.0, 0.0).astype(BF16) for part in range(cells_here // cells)
    ]
    picked = dot(jnp.concatenate(one_hot, axis=1), flux_cot[...])
    loads[3].wait()
    products = jnp.zeros(which_cell.shape, F32)
    for m in range(0, maps, 2):
        chosen = [jnp.where(which_map == n, picked, 0.0).astype(BF16) for n in range(m, min(m + 2, maps))]
        taken = [regrid[n] for n in range(m, min(m + 2, maps))]
        products = products + dot(
            jnp.concatenate(chosen, axis=1), jnp.concatenate(taken, axis=1), ((1,), (1,))
        )
    products = products.astype(BF16).astype(F32)
    span = tiles * rows * fields
    share = products[:span]
    for k in range(1, intersections):
        share = share + products[k * span : (k + 1) * span]
    flux_send[...] = share.reshape(flux_send.shape)
    flux_recv[pl.ds(flat, 1)] = flux_send[pl.ds(flat, 1)]

    outside = lat * (rows + 1)
    padded[pl.ds(outside, 1)] = jnp.zeros((1,) + padded.shape[1:], BF16)
    padded_grad[pl.ds(outside, 1)] = jnp.zeros((1,) + padded.shape[1:], BF16)

    pl.semaphore_wait(barrier, tiles - 1 + members - 1)
    state_copies = start_all(
        halo_copies(state_in, (0, 0), padded, rows, cells, lat, lon, lon_tiles, state_sems)
    )
    flux_copies = []
    for step in range(1, tiles):
        peer = lax.rem(flat + step, tiles)
        flux_copies.append(
            remote(
                flux_send.at[peer],
                flux_recv.at[flat],
                flux_sems[0].at[step - 1],
                flux_sems[1].at[step - 1],
                {"oy": peer // lon_tiles, "ox": lax.rem(peer, lon_tiles)},
            )
        )
    start_all(flux_copies)

    for load in loads[4:]:
        load.wait()
    flux_rows[...] = jnp.zeros(flux_rows.shape, F32)
    for n in range(2 * rows):
        flux_rows[n * fields : (n + 1) * fields, :] = flux_weight[...].astype(F32)
    cot_flat = cot[...].reshape(rows * cells, channels)
    act_grad = dot(cot_flat, mix[...], ((1,), (1,)))
    wait_all(state_copies)
    shift_cells(padded, wide, columns, rows, cells, (0, 1, 2))
    hidden = jnp.zeros((rows * cells, channels), F32)
    for p in range(3):
        hidden = hidden + dot(
            columns[p : p + rows].reshape(rows * cells, 3 * channels),
            conv[3 * p : 3 * p + 3].reshape(3 * channels, channels),
        )
    gate = jax.nn.sigmoid(hidden)
    activation = (hidden * gate).astype(BF16)
    slope = gate * (1.0 + hidden * (1.0 - gate))
    turned[...] = columns[...].reshape((rows + 2) * cells, 3 * channels).T
    term = dot(activation, cot_flat, ((0,), (0,)))
    store_rows(grads, 9 * channels, term)
    store_rows(grads_half, 9 * channels, term)

    wait_all(flux_copies)
    row_iota = lax.broadcasted_iota(jnp.int32, (rows * fields, cells), 0) // fields
    flux = flux_recv[0]
    for tile in range(1, tiles):
        flux = flux + flux_recv[tile]
    flux = jnp.where(row_iota < wet[0, 0], flux, 0.0)
    flux_high = flux.astype(BF16).astype(F32)
    flux_low = flux - flux_high
    both = jnp.concatenate([flux_high, flux_low], axis=0)
    both_iota = jnp.concatenate([row_iota, row_iota], axis=0)
    heads = flux_rows[...].astype(BF16)
    masked = []
    for row in range(rows):
        mine = jnp.where(both_iota == row, both, 0.0).astype(BF16)
        masked.append(mine)
        here = slice(row * cells, (row + 1) * cells)
        extra = dot(mine, heads, ((0,), (0,)))
        padded_grad[row + 1, EDGE : EDGE + cells] = ((act_grad[here] + extra) * slope[here]).astype(BF16)
    grad_copies = start_all(
        halo_copies(padded_grad, (1, EDGE), padded_grad, rows, cells, lat, lon, lon_tiles, grad_sems)
    )

    hidden_grad = padded_grad[1 : rows + 1, EDGE : EDGE + cells].reshape(rows * cells, channels)
    for p in range(3):
        term = dot(turned[:, p * cells : (p + rows) * cells], hidden_grad)
        store_rows(grads, 3 * p * channels, term)
        store_rows(grads_half, 3 * p * channels, term)

    lat_copies = [
        start_all(
            exchange(
                "oy",
                lat_tiles,
                lat,
                lambda to: grads_half.at[to, :, pl.ds(at, count)],
                lambda me: recv_lat.at[:, pl.ds(at, count)],
                lat_sems,
                n * lat_tiles,
            )
        )
        for n, (at, count) in enumerate(chunks)
    ]
    flux_rows[...] = dot(jnp.concatenate(masked, axis=1), activation)
    total = flux_rows[:fields, :]
    for n in range(1, 2 * rows):
        total = total + flux_rows[n * fields : (n + 1) * fields, :]
    flux_lat[pl.ds(lat, 1)] = jnp.zeros((1,) + flux_lat.shape[1:], F32)
    flux_lat[pl.ds(lat, 1), 0:fields, :] = total[None]
    flux_lat_copies = start_all(
        exchange("oy", lat_tiles, lat, lambda to: flux_lat.at[lat], lambda me: flux_lat.at[me], flux_lat_sems)
    )

    ens_copies = []
    for n, (at, count) in enumerate(chunks):
        wait_all(lat_copies[n])
        own = grads[pl.ds(lat, 1), :, at : at + count]
        part = (own[0] + recv_lat[:, at : at + count].astype(F32)).astype(BF16)
        sum_lat[:, :, at : at + count] = part.reshape(lon_tiles, members, count, channels)
        ens_copies.append(
            start_all(
                exchange(
                    "ens",
                    members,
                    ens,
                    lambda to: sum_lat.at[:, to, pl.ds(at, count)],
                    lambda me: recv_ens.at[me, :, pl.ds(at, count)],
                    ens_sems,
                    n * members,
                )
            )
        )
    recv_ens[pl.ds(ens, 1)] = sum_lat[:, pl.ds(ens, 1)].reshape((1,) + recv_ens.shape[1:])
    wait_all(flux_lat_copies)
    total = flux_lat[0]
    for n in range(1, lat_tiles):
        total = total + flux_lat[n]
    flux_ens[pl.ds(ens, 1)] = total[None]
    flux_ens_copies = start_all(
        exchange("ens", members, ens, lambda to: flux_ens.at[ens], lambda me: flux_ens.at[me], flux_ens_sems)
    )

    wait_all(grad_copies)
    shift_cells(padded_grad, wide, grad_columns, rows, cells, (2, 1, 0))
    input_grad = cot_flat.astype(F32)
    for p in range(3):
        back = grad_columns[2 - p : 2 - p + rows].reshape(rows * cells, 3 * channels)
        taps = jnp.concatenate([conv[3 * p + q] for q in range(3)], axis=1)
        input_grad = input_grad + dot(back, taps, ((1,), (1,)))
    input_out[...] = input_grad.astype(BF16).reshape(input_out.shape)

    lon_copies, out_copies = [], []

    def gather_chunk(n):
        at, count = chunks[n]
        wait_all(lon_copies[n])
        total = recv_lon[0, at : at + count].astype(F32)
        for other in range(1, lon_tiles):
            total = total + recv_lon[other, at : at + count].astype(F32)
        rows_all[pl.ds(ens, 1), at : at + count] = (total * grad_scale).astype(BF16)[None]
        out_copies.append(
            start_all(
                exchange(
                    "ens",
                    members,
                    ens,
                    lambda to: rows_all.at[ens, pl.ds(at, count)],
                    lambda me: rows_all.at[me, pl.ds(at, count)],
                    out_sems,
                    n * members,
                )
            )
        )

    for n, (at, count) in enumerate(chunks):
        wait_all(ens_copies[n])
        total = recv_ens[0, :, at : at + count].astype(F32)
        for other in range(1, members):
            total = total + recv_ens[other, :, at : at + count].astype(F32)
        sum_ens[:, at : at + count] = total.astype(BF16)
        lon_copies.append(
            start_all(
                exchange(
                    "ox",
                    lon_tiles,
                    lon,
                    lambda to: sum_ens.at[to, pl.ds(at, count)],
                    lambda me: recv_lon.at[me, pl.ds(at, count)],
                    lon_sems,
                    n * lon_tiles,
                )
            )
        )
        recv_lon[pl.ds(lon, 1), at : at + count] = sum_ens[pl.ds(lon, 1), at : at + count]
        if n == 0:
            wait_all(flux_ens_copies)
            total = flux_ens[0]
            for other in range(1, members):
                total = total + flux_ens[other]
            flux_lon[pl.ds(lon, 1)] = total[None]
            flux_lon_copies = start_all(
                exchange("ox", lon_tiles, lon, lambda to: flux_lon.at[lon], lambda me: flux_lon.at[me], flux_lon_sems)
            )
        else:
            gather_chunk(n - 1)
    wait_all(flux_lon_copies)
    total = flux_lon[0]
    for n in range(1, lon_tiles):
        total = total + flux_lon[n]
    flux_out[...] = total[:fields] * grad_scale
    gather_chunk(len(chunks) - 1)
    for copies in out_copies:
        wait_all(copies)
    weight_out[...] = rows_all[...].astype(F32).reshape(weight_out.shape)
    started = state_copies + flux_copies + grad_copies + flux_lat_copies + flux_ens_copies + flux_lon_copies
    for copies in [started] + lat_copies + ens_copies + lon_copies + out_copies:
        for copy in copies:
            copy.wait_send()


def place_kernel(*refs):
    count = len(refs) // 2
    sems = refs[-1]
    copies = [pltpu.make_async_copy(refs[n], refs[count + n], sems.at[n]) for n in range(count)]
    for copy in copies:
        copy.start()
    for copy in copies:
        copy.wait()


def place(arrays):
    anywhere = pl.BlockSpec(memory_space=pl.ANY)
    return pl.pallas_call(
        place_kernel,
        out_shape=tuple(jax.ShapeDtypeStruct(a.shape, a.dtype) for a in arrays),
        in_specs=[anywhere] * len(arrays),
        out_specs=tuple([anywhere] * len(arrays)),
        scratch_shapes=[pltpu.SemaphoreType.DMA((len(arrays),))],
        compiler_params=pltpu.CompilerParams(vmem_limit_bytes=60 << 20),
    )(*arrays)


def fused_body(
    state,
    state_cot,
    flux_cot,
    conv_weight,
    mix_weight,
    flux_weight,
    regrid_weights,
    intersection_atm,
    intersection_offset,
    wet_rows,
):
    members, lat_tiles, lon_tiles = (lax.axis_size(name) for name in ("ens", "oy", "ox"))
    rows, cells, channels = state.shape[1:]
    fields = flux_weight.shape[0]
    tiles = lat_tiles * lon_tiles
    grad_rows = (conv_weight.shape[0] + 1) * channels
    band = grad_rows // lat_tiles
    pieces = lon_tiles * members
    sub = band // pieces
    grad_scale = 1.0 / math.sqrt(members * lat_tiles * rows * lon_tiles * cells)
    entries = tiles * rows * intersection_atm.shape[2] * fields
    halo = (rows + 2, cells + 2 * EDGE, channels)
    spread = (rows + 2, cells, 3 * channels)
    small = 2 * fields
    size = 2 * EDGE
    chunks = [(at, min(size, sub - at)) for at in range(0, sub, size)]

    def pair(count):
        return (pltpu.SemaphoreType.DMA((count,)), pltpu.SemaphoreType.DMA((count,)))

    vmem = pl.BlockSpec(memory_space=pltpu.VMEM)
    smem = pl.BlockSpec(memory_space=pltpu.SMEM)
    anywhere = pl.BlockSpec(memory_space=pl.ANY)
    flux_flat = flux_cot[0].reshape(-1, cells)
    tables = [table.transpose(1, 2, 0) for table in (intersection_atm, intersection_offset)]
    scratch = [
        pltpu.VMEM((rows, cells, channels), BF16),
        pltpu.VMEM(flux_flat.shape, BF16),
        pltpu.VMEM(conv_weight.shape, BF16),
        pltpu.VMEM(mix_weight.shape, BF16),
        pltpu.VMEM(flux_weight.shape, BF16),
        pltpu.VMEM(regrid_weights.shape, BF16),
        pltpu.SMEM(tables[0].shape, jnp.int32),
        pltpu.SMEM(tables[1].shape, jnp.int32),
        pltpu.VMEM(halo, BF16),
        pltpu.VMEM(halo, BF16),
        pltpu.VMEM(halo, F32),
        pltpu.VMEM(spread, BF16),
        pltpu.VMEM((3 * channels, (rows + 2) * cells), BF16),
        pltpu.VMEM(spread, BF16),
        pltpu.VMEM((entries, cells), jnp.int32),
        pltpu.VMEM((entries, cells), jnp.int32),
        pltpu.VMEM((tiles, rows * fields, cells), F32),
        pltpu.VMEM((tiles, rows * fields, cells), F32),
        pltpu.VMEM((2 * rows * fields, channels), F32),
        pltpu.VMEM((lat_tiles, pieces, sub, channels), F32),
        pltpu.VMEM((lat_tiles, pieces, sub, channels), BF16),
        pltpu.VMEM((pieces, sub, channels), BF16),
        pltpu.VMEM((lon_tiles, members, sub, channels), BF16),
        pltpu.VMEM((members, lon_tiles, sub, channels), BF16),
        pltpu.VMEM((lon_tiles, sub, channels), BF16),
        pltpu.VMEM((lon_tiles, sub, channels), BF16),
        pltpu.VMEM((members, sub, channels), BF16),
        pltpu.VMEM((lat_tiles, small, channels), F32),
        pltpu.VMEM((members, small, channels), F32),
        pltpu.VMEM((lon_tiles, small, channels), F32),
        pltpu.SemaphoreType.DMA((9,)),
        pair(5),
        pair(5),
        pair(tiles),
        pair(lat_tiles),
        pair(members),
        pair(lon_tiles),
        pair(len(chunks) * lat_tiles),
        pair(len(chunks) * members),
        pair(len(chunks) * lon_tiles),
        pair(len(chunks) * members),
    ]
    cost = pl.CostEstimate(
        flops=2 * rows * cells * channels * channels * 29, bytes_accessed=3 << 20, transcendentals=rows * cells * channels
    )
    outs = pl.pallas_call(
        functools.partial(fused_kernel, (members, lat_tiles, lon_tiles, grad_scale, chunks)),
        out_shape=(
            jax.ShapeDtypeStruct(state.shape, BF16),
            jax.ShapeDtypeStruct((band // lon_tiles, channels), F32),
            jax.ShapeDtypeStruct((fields, channels), F32),
        ),
        in_specs=[anywhere] * 9 + [smem],
        out_specs=(vmem, vmem, vmem),
        scratch_shapes=scratch,
        cost_estimate=cost,
        compiler_params=pltpu.CompilerParams(
            collective_id=0, has_side_effects=True, vmem_limit_bytes=56 << 20
        ),
    )(
        state[0],
        state_cot[0],
        flux_flat,
        conv_weight,
        mix_weight,
        flux_weight,
        regrid_weights,
        tables[0],
        tables[1],
        wet_rows,
    )
    return place(outs)


def step(state, state_cot, flux_cot, conv_weight, *rest):
    members, lat_tiles, lon_tiles = (lax.axis_size(name) for name in ("ens", "oy", "ox"))
    grad_rows = (conv_weight.shape[0] + 1) * state.shape[3]
    whole_tiles = grad_rows % (lat_tiles * lon_tiles * members * EDGE) == 0
    fused = lat_tiles == 2 and lon_tiles > 1 and whole_tiles
    return (fused_body if fused else body)(state, state_cot, flux_cot, conv_weight, *rest)


def solution(mesh):
    in_specs = (
        P("ens", "oy", "ox", None),
        P("ens", "oy", "ox", None),
        P("ens", ("oy", "ox"), None, None),
        P(),
        P(),
        P(),
        P(),
        P(),
        P(),
        P("oy", "ox"),
    )
    out_specs = (P("ens", "oy", "ox", None), P(("oy", "ox"), None), P())
    return jax.shard_map(step, mesh=mesh, in_specs=in_specs, out_specs=out_specs, check_vma=False)
```

```python
import functools
import math

import jax
import jax.numpy as jnp
from jax import lax
from jax.experimental import pallas as pl
from jax.experimental.pallas import tpu as pltpu
from jax.sharding import PartitionSpec as P

CAP = 5


def with_halo(cells, sides, width):
    for axis, dim in sides:
        count = lax.axis_size(axis)
        head = lax.slice_in_dim(cells, 0, width, axis=dim)
        tail = lax.slice_in_dim(cells, cells.shape[dim] - width, cells.shape[dim], axis=dim)
        cells = jnp.concatenate(
            [
                lax.ppermute(tail, axis, [(i, (i + 1) % count) for i in range(count)]),
                cells,
                lax.ppermute(head, axis, [((i + 1) % count, i) for i in range(count)]),
            ],
            axis=dim,
        )
    return cells


def shifted(value, axis, steps):
    count = lax.axis_size(axis)
    pairs = [(source, (source + steps) % count) for source in range(count)]
    return lax.ppermute(value, axis, pairs)


def zero_ends(padded, row_index, lat_tiles):
    top_keep = jnp.where(row_index > 0, 1.0, 0.0).astype(padded.dtype)
    bottom = jnp.where(row_index < lat_tiles - 1, 1.0, 0.0).astype(padded.dtype)
    return jnp.concatenate([padded[:1] * top_keep, padded[1:-1], padded[-1:] * bottom], axis=0)


def owner_rank(owners):
    entry_count = owners.shape[-1]
    same_owner = owners[..., :, None] == owners[..., None, :]
    earlier = jnp.arange(entry_count)[None, :] < jnp.arange(entry_count)[:, None]
    return jnp.sum(jnp.logical_and(same_owner, earlier), axis=-1)


def body(
    state,
    state_cot,
    flux_cot,
    conv_weight,
    mix_weight,
    flux_weight,
    regrid_weights,
    intersection_atm,
    intersection_offset,
    wet_rows,
):
    lat_tiles = lax.axis_size("oy")
    lon_tiles = lax.axis_size("ox")
    members = lax.axis_size("ens")
    row_index = lax.axis_index("oy")
    col_index = lax.axis_index("ox")
    tile_state = state[0]
    tile_rows, block_cells, channels = tile_state.shape
    cot_flat = state_cot[0].reshape(-1, channels)
    grad_scale = 1.0 / math.sqrt(members * lat_tiles * tile_rows * lon_tiles * block_cells)
    padded = with_halo(tile_state, (("oy", 0), ("ox", 1)), 1)
    padded = zero_ends(padded, row_index, lat_tiles)
    hidden = jnp.zeros((tile_rows * block_cells, channels), jnp.float32)
    for tap_index in range(9):
        tap_row, tap_col = (tap_index // 3, tap_index % 3)
        patch_rows = padded[tap_row : tap_row + tile_rows, tap_col : tap_col + block_cells].reshape(
            -1, channels
        )
        hidden = hidden + jnp.dot(
            patch_rows, conv_weight[tap_index], preferred_element_type=jnp.float32
        )
    activation = jax.nn.silu(hidden).astype(jnp.bfloat16)
    atm_dev = flux_cot.shape[1]
    cot_blocks = flux_cot[0]
    flux_fields = cot_blocks.shape[1]
    intersections = intersection_atm.shape[2]
    entries = tile_rows * intersections
    per_dev = (
        intersection_atm.reshape(lat_tiles, tile_rows, lon_tiles, intersections)
        .transpose(0, 2, 1, 3)
        .reshape(lat_tiles, lon_tiles, entries)
    )
    per_dev_offset = (
        intersection_offset.reshape(lat_tiles, tile_rows, lon_tiles, intersections)
        .transpose(0, 2, 1, 3)
        .reshape(lat_tiles, lon_tiles, entries)
    )
    band_rows = jnp.stack([row_index, (row_index + lat_tiles - 1) % lat_tiles])
    candidate = jnp.take(per_dev, band_rows, axis=0)
    candidate_offset = jnp.take(per_dev_offset, band_rows, axis=0)
    flat_index = row_index * lon_tiles + col_index
    candidate_owner = candidate // atm_dev
    is_mine = candidate_owner == flat_index
    slot_rank = owner_rank(candidate_owner)
    local_block = jnp.where(is_mine, candidate % atm_dev, 0)
    picked_cot = cot_blocks[local_block]
    picked_maps = regrid_weights[candidate_offset]
    products = jnp.einsum(
        "qsefa,qseoa->qsefo", picked_cot, picked_maps, preferred_element_type=jnp.float32
    )
    one_hot = jnp.logical_and(
        slot_rank[..., None] == jnp.arange(CAP)[None, None, None, :], is_mine[..., None]
    ).astype(jnp.float32)
    outbound = jnp.einsum("qsec,qsefo->qscfo", one_hot, products).astype(jnp.bfloat16)
    own_entries = per_dev[row_index, col_index]
    own_owner = own_entries // atm_dev
    own_slot = owner_rank(own_owner)
    same_in, next_in = (
        lax.all_to_all(outbound[0], "ox", split_axis=0, concat_axis=0, tiled=True),
        lax.all_to_all(outbound[1], "ox", split_axis=0, concat_axis=0, tiled=True),
    )
    next_in = shifted(next_in, "oy", -1)
    arrived = jnp.concatenate([same_in, next_in], axis=0).reshape(-1, flux_fields, block_cells)
    in_next = (own_owner // lon_tiles != row_index).astype(jnp.int32)
    slot_index = (in_next * lon_tiles + own_owner % lon_tiles) * CAP + own_slot
    values = (
        arrived[slot_index]
        .astype(jnp.float32)
        .reshape(tile_rows, intersections, flux_fields, block_cells)
    )
    wet_mask = (jnp.arange(tile_rows) < wet_rows[0, 0]).astype(jnp.float32)
    flux_cells = jnp.sum(values, axis=1) * wet_mask[:, None, None]
    act_grad = lax.dot_general(
        cot_flat, mix_weight, (((1,), (1,)), ((), ())), preferred_element_type=jnp.float32
    )
    act_grad = act_grad + jnp.einsum(
        "rfb,fc->rbc", flux_cells, flux_weight.astype(jnp.float32)
    ).reshape(-1, channels)
    gate_sig = jax.nn.sigmoid(hidden)
    hidden_grad = (act_grad * gate_sig * (1.0 + hidden * (1.0 - gate_sig))).astype(jnp.bfloat16)
    padded_grad = with_halo(
        hidden_grad.reshape(tile_rows, block_cells, channels), (("oy", 0), ("ox", 1)), 1
    )
    padded_grad = zero_ends(padded_grad, row_index, lat_tiles)
    input_grad = cot_flat.astype(jnp.float32)
    tap_grads = []
    for tap_index in range(9):
        tap_row, tap_col = (tap_index // 3, tap_index % 3)
        back_rows = padded_grad[
            2 - tap_row : 2 - tap_row + tile_rows, 2 - tap_col : 2 - tap_col + block_cells
        ].reshape(-1, channels)
        input_grad = input_grad + lax.dot_general(
            back_rows,
            conv_weight[tap_index],
            (((1,), (1,)), ((), ())),
            preferred_element_type=jnp.float32,
        )
        patch_rows = padded[tap_row : tap_row + tile_rows, tap_col : tap_col + block_cells].reshape(
            -1, channels
        )
        tap_grads.append(
            lax.dot_general(
                patch_rows,
                hidden_grad,
                (((0,), (0,)), ((), ())),
                preferred_element_type=jnp.float32,
            )
        )
    tap_grads.append(
        lax.dot_general(
            activation, cot_flat, (((0,), (0,)), ((), ())), preferred_element_type=jnp.float32
        )
    )
    weight_term = jnp.concatenate(tap_grads, axis=0) * grad_scale
    flux_term = (
        jnp.einsum(
            "rfb,rbc->fc",
            flux_cells,
            activation.reshape(tile_rows, block_cells, channels).astype(jnp.float32),
        )
        * grad_scale
    )
    weight_rows = lax.psum_scatter(weight_term, ("oy", "ox"), scatter_dimension=0, tiled=True)
    weight_out = lax.psum(weight_rows, "ens")
    flux_total = lax.psum(flux_term, ("ens", "oy", "ox"))
    input_out = input_grad.reshape(1, tile_rows, block_cells, channels).astype(jnp.bfloat16)
    return (input_out, weight_out, flux_total)


F32 = jnp.float32
BF16 = jnp.bfloat16
MESH = pl.DeviceIdType.MESH
EDGE = 16


def dot(a, b, dims=((1,), (0,))):
    return lax.dot_general(a, b, (dims, ((), ())), preferred_element_type=F32)


def remote(src, dst, send_sem, recv_sem, target):
    return pltpu.make_async_remote_copy(
        src_ref=src,
        dst_ref=dst,
        send_sem=send_sem,
        recv_sem=recv_sem,
        device_id=target,
        device_id_type=MESH,
    )


def start_all(copies):
    for copy in copies:
        copy.start()
    return copies


def halo_copies(src, src_at, padded, rows, cells, lat, lon, lon_tiles, sems):
    row0, col0 = src_at
    other = 1 - lat
    east = lax.rem(lon + 1, lon_tiles)
    west = lax.rem(lon + lon_tiles - 1, lon_tiles)
    edge_row = row0 + other * (rows - 1)
    land_row = lat * (rows + 1)
    body_rows, dst_rows = pl.ds(row0, rows), pl.ds(1, rows)
    head, last = pl.ds(col0, EDGE), pl.ds(col0 + cells - EDGE, EDGE)
    left, middle, right = pl.ds(0, EDGE), pl.ds(EDGE, cells), pl.ds(EDGE + cells, EDGE)
    plan = [
        (src.at[pl.ds(edge_row, 1), pl.ds(col0, cells)], padded.at[pl.ds(land_row, 1), middle], other, lon),
        (src.at[body_rows, last], padded.at[dst_rows, left], lat, east),
        (src.at[body_rows, head], padded.at[dst_rows, right], lat, west),
        (src.at[pl.ds(edge_row, 1), last], padded.at[pl.ds(land_row, 1), left], other, east),
        (src.at[pl.ds(edge_row, 1), head], padded.at[pl.ds(land_row, 1), right], other, west),
    ]
    send, recv = sems
    return [
        remote(a, b, send.at[n], recv.at[n], {"oy": y, "ox": x})
        for n, (a, b, y, x) in enumerate(plan)
    ]


def exchange(axis, count, me, source, target, sems, base=0):
    send, recv = sems
    copies = []
    for step in range(1, count):
        to = lax.rem(me + step, count)
        copies.append(
            remote(source(to), target(me), send.at[base + step - 1], recv.at[base + step - 1], {axis: to})
        )
    return copies


def wait_all(copies):
    for copy in copies:
        copy.wait_recv()


def shift_cells(padded, wide, columns, rows, cells, order):
    channels = padded.shape[2]
    for row in range(rows + 2):
        wide[row] = padded[row].astype(F32)
        for n, col in enumerate(order):
            here = slice(n * channels, (n + 1) * channels)
            if col == 1:
                columns[row, :, here] = padded[row, EDGE : EDGE + cells]
            else:
                columns[row, :, here] = wide[row, pl.ds(EDGE - 1 + col, cells), :].astype(BF16)


def store_rows(target, first, value):
    pieces, sub = target.shape[1:3]
    done = 0
    while done < value.shape[0]:
        at = first + done
        piece, row = at // sub, at % sub
        count = min(sub - row, value.shape[0] - done)
        target[piece // pieces, piece % pieces, row : row + count, :] = value[done : done + count].astype(
            target.dtype
        )
        done += count


def fused_kernel(
    sizes,
    state_in,
    cot_in,
    flux_cot_in,
    conv_in,
    mix_in,
    flux_weight_in,
    regrid_in,
    atm_in,
    offset_in,
    wet,
    input_out,
    weight_out,
    flux_out,
    cot,
    flux_cot,
    conv,
    mix,
    flux_weight,
    regrid,
    atm,
    offset,
    padded,
    padded_grad,
    wide,
    columns,
    turned,
    grad_columns,
    entry_cell,
    entry_map,
    flux_send,
    flux_recv,
    flux_rows,
    grads,
    grads_half,
    recv_lat,
    sum_lat,
    recv_ens,
    sum_ens,
    recv_lon,
    rows_all,
    flux_lat,
    flux_ens,
    flux_lon,
    load_sems,
    state_sems,
    grad_sems,
    flux_sems,
    flux_lat_sems,
    flux_ens_sems,
    flux_lon_sems,
    lat_sems,
    ens_sems,
    lon_sems,
    out_sems,
):
    members, lat_tiles, lon_tiles, grad_scale, chunks = sizes
    ens, lat, lon = lax.axis_index("ens"), lax.axis_index("oy"), lax.axis_index("ox")
    rows, cells, channels = cot.shape
    fields = flux_weight.shape[0]
    intersections = atm.shape[1]
    maps = regrid.shape[0]
    tiles = lat_tiles * lon_tiles
    flat = lat * lon_tiles + lon
    cells_here = flux_cot.shape[0]

    barrier = pltpu.get_barrier_semaphore()
    for step in range(1, tiles):
        peer = lax.rem(flat + step, tiles)
        pl.semaphore_signal(
            barrier, inc=1, device_id={"oy": peer // lon_tiles, "ox": lax.rem(peer, lon_tiles)}, device_id_type=MESH
        )
    for step in range(1, members):
        pl.semaphore_signal(
            barrier, inc=1, device_id={"ens": lax.rem(ens + step, members)}, device_id_type=MESH
        )
    loads = [
        pltpu.make_async_copy(src, dst, load_sems.at[n])
        for n, (src, dst) in enumerate(
            [
                (atm_in, atm),
                (offset_in, offset),
                (flux_cot_in, flux_cot),
                (regrid_in, regrid),
                (cot_in, cot),
                (mix_in, mix),
                (state_in, padded.at[pl.ds(1, rows), pl.ds(EDGE, cells)]),
                (flux_weight_in, flux_weight),
                (conv_in, conv),
            ]
        )
    ]
    for load in loads:
        load.start()

    loads[0].wait()
    loads[1].wait()
    entry = 0
    for k in range(intersections):
        for tile in range(tiles):
            for row in range(rows):
                at = (tile % lon_tiles, k, (tile // lon_tiles) * rows + row)
                entry_cell[pl.ds(entry, fields), :] = jnp.full((fields, cells), atm[at], jnp.int32)
                entry_map[pl.ds(entry, fields), :] = jnp.full((fields, cells), offset[at], jnp.int32)
                entry += fields
    field_iota = lax.broadcasted_iota(jnp.int32, entry_cell.shape, 0) % fields
    lane = lax.broadcasted_iota(jnp.int32, entry_cell.shape, 1)
    which_cell = entry_cell[...] * fields + (field_iota - lane - flat * cells_here)
    which_map = entry_map[...]
    loads[2].wait()
    one_hot = [
        jnp.where(which_cell == part * cells, 1.0, 0.0).astype(BF16) for part in range(cells_here // cells)
    ]
    picked = dot(jnp.concatenate(one_hot, axis=1), flux_cot[...])
    loads[3].wait()
    products = jnp.zeros(which_cell.shape, F32)
    for m in range(0, maps, 2):
        chosen = [jnp.where(which_map == n, picked, 0.0).astype(BF16) for n in range(m, min(m + 2, maps))]
        taken = [regrid[n] for n in range(m, min(m + 2, maps))]
        products = products + dot(
            jnp.concatenate(chosen, axis=1), jnp.concatenate(taken, axis=1), ((1,), (1,))
        )
    products = products.astype(BF16).astype(F32)
    span = tiles * rows * fields
    share = products[:span]
    for k in range(1, intersections):
        share = share + products[k * span : (k + 1) * span]
    flux_send[...] = share.reshape(flux_send.shape)
    flux_recv[pl.ds(flat, 1)] = flux_send[pl.ds(flat, 1)]

    outside = lat * (rows + 1)
    padded[pl.ds(outside, 1)] = jnp.zeros((1,) + padded.shape[1:], BF16)
    padded_grad[pl.ds(outside, 1)] = jnp.zeros((1,) + padded.shape[1:], BF16)

    pl.semaphore_wait(barrier, tiles - 1 + members - 1)
    state_copies = start_all(
        halo_copies(state_in, (0, 0), padded, rows, cells, lat, lon, lon_tiles, state_sems)
    )
    flux_copies = []
    for step in range(1, tiles):
        peer = lax.rem(flat + step, tiles)
        flux_copies.append(
            remote(
                flux_send.at[peer],
                flux_recv.at[flat],
                flux_sems[0].at[step - 1],
                flux_sems[1].at[step - 1],
                {"oy": peer // lon_tiles, "ox": lax.rem(peer, lon_tiles)},
            )
        )
    start_all(flux_copies)

    for load in loads[4:]:
        load.wait()
    flux_rows[...] = jnp.zeros(flux_rows.shape, F32)
    for n in range(2 * rows):
        flux_rows[n * fields : (n + 1) * fields, :] = flux_weight[...].astype(F32)
    cot_flat = cot[...].reshape(rows * cells, channels)
    act_grad = dot(cot_flat, mix[...], ((1,), (1,)))
    wait_all(state_copies)
    shift_cells(padded, wide, columns, rows, cells, (0, 1, 2))
    hidden = jnp.zeros((rows * cells, channels), F32)
    for p in range(3):
        hidden = hidden + dot(
            columns[p : p + rows].reshape(rows * cells, 3 * channels),
            conv[3 * p : 3 * p + 3].reshape(3 * channels, channels),
        )
    gate = jax.nn.sigmoid(hidden)
    activation = (hidden * gate).astype(BF16)
    slope = gate * (1.0 + hidden * (1.0 - gate))
    turned[...] = columns[...].reshape((rows + 2) * cells, 3 * channels).T
    term = dot(activation, cot_flat, ((0,), (0,)))
    store_rows(grads, 9 * channels, term)
    store_rows(grads_half, 9 * channels, term)

    wait_all(flux_copies)
    row_iota = lax.broadcasted_iota(jnp.int32, (rows * fields, cells), 0) // fields
    flux = flux_recv[0]
    for tile in range(1, tiles):
        flux = flux + flux_recv[tile]
    flux = jnp.where(row_iota < wet[0, 0], flux, 0.0)
    flux_high = flux.astype(BF16).astype(F32)
    flux_low = flux - flux_high
    both = jnp.concatenate([flux_high, flux_low], axis=0)
    both_iota = jnp.concatenate([row_iota, row_iota], axis=0)
    heads = flux_rows[...].astype(BF16)
    masked = []
    for row in range(rows):
        mine = jnp.where(both_iota == row, both, 0.0).astype(BF16)
        masked.append(mine)
        here = slice(row * cells, (row + 1) * cells)
        extra = dot(mine, heads, ((0,), (0,)))
        padded_grad[row + 1, EDGE : EDGE + cells] = ((act_grad[here] + extra) * slope[here]).astype(BF16)
    grad_copies = start_all(
        halo_copies(padded_grad, (1, EDGE), padded_grad, rows, cells, lat, lon, lon_tiles, grad_sems)
    )

    hidden_grad = padded_grad[1 : rows + 1, EDGE : EDGE + cells].reshape(rows * cells, channels)
    for p in range(3):
        term = dot(turned[:, p * cells : (p + rows) * cells], hidden_grad)
        store_rows(grads, 3 * p * channels, term)
        store_rows(grads_half, 3 * p * channels, term)

    lat_copies = [
        start_all(
            exchange(
                "oy",
                lat_tiles,
                lat,
                lambda to: grads_half.at[to, :, pl.ds(at, count)],
                lambda me: recv_lat.at[:, pl.ds(at, count)],
                lat_sems,
                n * lat_tiles,
            )
        )
        for n, (at, count) in enumerate(chunks)
    ]
    flux_rows[...] = dot(jnp.concatenate(masked, axis=1), activation)
    total = flux_rows[:fields, :]
    for n in range(1, 2 * rows):
        total = total + flux_rows[n * fields : (n + 1) * fields, :]
    flux_lat[pl.ds(lat, 1)] = jnp.zeros((1,) + flux_lat.shape[1:], F32)
    flux_lat[pl.ds(lat, 1), 0:fields, :] = total[None]
    flux_lat_copies = start_all(
        exchange("oy", lat_tiles, lat, lambda to: flux_lat.at[lat], lambda me: flux_lat.at[me], flux_lat_sems)
    )

    ens_copies = []
    for n, (at, count) in enumerate(chunks):
        wait_all(lat_copies[n])
        own = grads[pl.ds(lat, 1), :, at : at + count]
        part = (own[0] + recv_lat[:, at : at + count].astype(F32)).astype(BF16)
        sum_lat[:, :, at : at + count] = part.reshape(lon_tiles, members, count, channels)
        ens_copies.append(
            start_all(
                exchange(
                    "ens",
                    members,
                    ens,
                    lambda to: sum_lat.at[:, to, pl.ds(at, count)],
                    lambda me: recv_ens.at[me, :, pl.ds(at, count)],
                    ens_sems,
                    n * members,
                )
            )
        )
    recv_ens[pl.ds(ens, 1)] = sum_lat[:, pl.ds(ens, 1)].reshape((1,) + recv_ens.shape[1:])
    wait_all(flux_lat_copies)
    total = flux_lat[0]
    for n in range(1, lat_tiles):
        total = total + flux_lat[n]
    flux_ens[pl.ds(ens, 1)] = total[None]
    flux_ens_copies = start_all(
        exchange("ens", members, ens, lambda to: flux_ens.at[ens], lambda me: flux_ens.at[me], flux_ens_sems)
    )

    wait_all(grad_copies)
    shift_cells(padded_grad, wide, grad_columns, rows, cells, (2, 1, 0))
    input_grad = cot_flat.astype(F32)
    for p in range(3):
        back = grad_columns[2 - p : 2 - p + rows].reshape(rows * cells, 3 * channels)
        taps = jnp.concatenate([conv[3 * p + q] for q in range(3)], axis=1)
        input_grad = input_grad + dot(back, taps, ((1,), (1,)))
    input_out[...] = input_grad.astype(BF16).reshape(input_out.shape)

    lon_copies, out_copies = [], []

    def gather_chunk(n):
        at, count = chunks[n]
        wait_all(lon_copies[n])
        total = recv_lon[0, at : at + count].astype(F32)
        for other in range(1, lon_tiles):
            total = total + recv_lon[other, at : at + count].astype(F32)
        rows_all[pl.ds(ens, 1), at : at + count] = (total * grad_scale).astype(BF16)[None]
        out_copies.append(
            start_all(
                exchange(
                    "ens",
                    members,
                    ens,
                    lambda to: rows_all.at[ens, pl.ds(at, count)],
                    lambda me: rows_all.at[me, pl.ds(at, count)],
                    out_sems,
                    n * members,
                )
            )
        )

    for n, (at, count) in enumerate(chunks):
        wait_all(ens_copies[n])
        total = recv_ens[0, :, at : at + count].astype(F32)
        for other in range(1, members):
            total = total + recv_ens[other, :, at : at + count].astype(F32)
        sum_ens[:, at : at + count] = total.astype(BF16)
        lon_copies.append(
            start_all(
                exchange(
                    "ox",
                    lon_tiles,
                    lon,
                    lambda to: sum_ens.at[to, pl.ds(at, count)],
                    lambda me: recv_lon.at[me, pl.ds(at, count)],
                    lon_sems,
                    n * lon_tiles,
                )
            )
        )
        recv_lon[pl.ds(lon, 1), at : at + count] = sum_ens[pl.ds(lon, 1), at : at + count]
        if n == 0:
            wait_all(flux_ens_copies)
            total = flux_ens[0]
            for other in range(1, members):
                total = total + flux_ens[other]
            flux_lon[pl.ds(lon, 1)] = total[None]
            flux_lon_copies = start_all(
                exchange("ox", lon_tiles, lon, lambda to: flux_lon.at[lon], lambda me: flux_lon.at[me], flux_lon_sems)
            )
        else:
            gather_chunk(n - 1)
    wait_all(flux_lon_copies)
    total = flux_lon[0]
    for n in range(1, lon_tiles):
        total = total + flux_lon[n]
    flux_out[...] = total[:fields] * grad_scale
    gather_chunk(len(chunks) - 1)
    for copies in out_copies:
        wait_all(copies)
    weight_out[...] = rows_all[...]
    started = state_copies + flux_copies + grad_copies + flux_lat_copies + flux_ens_copies + flux_lon_copies
    for copies in [started] + lat_copies + ens_copies + lon_copies + out_copies:
        for copy in copies:
            copy.wait_send()


def place_kernel(input_grad, weight_rows, flux_grad, input_out, weight_out, flux_out, wide, sems):
    copies = [
        pltpu.make_async_copy(input_grad, input_out, sems.at[0]),
        pltpu.make_async_copy(flux_grad, flux_out, sems.at[1]),
        pltpu.make_async_copy(wide, weight_out, sems.at[2]),
    ]
    copies[0].start()
    copies[1].start()
    wide[...] = weight_rows[...].reshape(wide.shape).astype(F32)
    copies[2].start()
    for copy in copies:
        copy.wait()


def place(input_grad, weight_rows, flux_grad):
    channels = weight_rows.shape[2]
    weight_shape = (weight_rows.shape[0] * weight_rows.shape[1], channels)
    vmem = pl.BlockSpec(memory_space=pltpu.VMEM)
    hbm = pl.BlockSpec(memory_space=pltpu.HBM)
    return pl.pallas_call(
        place_kernel,
        out_shape=(
            jax.ShapeDtypeStruct(input_grad.shape, BF16),
            jax.ShapeDtypeStruct(weight_shape, F32),
            jax.ShapeDtypeStruct(flux_grad.shape, F32),
        ),
        in_specs=[vmem] * 3,
        out_specs=(hbm, hbm, hbm),
        scratch_shapes=[pltpu.VMEM(weight_shape, F32), pltpu.SemaphoreType.DMA((3,))],
        compiler_params=pltpu.CompilerParams(vmem_limit_bytes=56 << 20),
    )(input_grad, weight_rows, flux_grad)


def fused_body(
    state,
    state_cot,
    flux_cot,
    conv_weight,
    mix_weight,
    flux_weight,
    regrid_weights,
    intersection_atm,
    intersection_offset,
    wet_rows,
):
    members, lat_tiles, lon_tiles = (lax.axis_size(name) for name in ("ens", "oy", "ox"))
    rows, cells, channels = state.shape[1:]
    fields = flux_weight.shape[0]
    tiles = lat_tiles * lon_tiles
    grad_rows = (conv_weight.shape[0] + 1) * channels
    band = grad_rows // lat_tiles
    pieces = lon_tiles * members
    sub = band // pieces
    grad_scale = 1.0 / math.sqrt(members * lat_tiles * rows * lon_tiles * cells)
    entries = tiles * rows * intersection_atm.shape[2] * fields
    halo = (rows + 2, cells + 2 * EDGE, channels)
    spread = (rows + 2, cells, 3 * channels)
    small = 2 * fields
    size = 2 * EDGE
    chunks = [(at, min(size, sub - at)) for at in range(0, sub, size)]

    def pair(count):
        return (pltpu.SemaphoreType.DMA((count,)), pltpu.SemaphoreType.DMA((count,)))

    vmem = pl.BlockSpec(memory_space=pltpu.VMEM)
    smem = pl.BlockSpec(memory_space=pltpu.SMEM)
    hbm = pl.BlockSpec(memory_space=pltpu.HBM)
    flux_flat = flux_cot[0].reshape(-1, cells)
    tables = [table.transpose(1, 2, 0) for table in (intersection_atm, intersection_offset)]
    scratch = [
        pltpu.VMEM((rows, cells, channels), BF16),
        pltpu.VMEM(flux_flat.shape, BF16),
        pltpu.VMEM(conv_weight.shape, BF16),
        pltpu.VMEM(mix_weight.shape, BF16),
        pltpu.VMEM(flux_weight.shape, BF16),
        pltpu.VMEM(regrid_weights.shape, BF16),
        pltpu.SMEM(tables[0].shape, jnp.int32),
        pltpu.SMEM(tables[1].shape, jnp.int32),
        pltpu.VMEM(halo, BF16),
        pltpu.VMEM(halo, BF16),
        pltpu.VMEM(halo, F32),
        pltpu.VMEM(spread, BF16),
        pltpu.VMEM((3 * channels, (rows + 2) * cells), BF16),
        pltpu.VMEM(spread, BF16),
        pltpu.VMEM((entries, cells), jnp.int32),
        pltpu.VMEM((entries, cells), jnp.int32),
        pltpu.VMEM((tiles, rows * fields, cells), F32),
        pltpu.VMEM((tiles, rows * fields, cells), F32),
        pltpu.VMEM((2 * rows * fields, channels), F32),
        pltpu.VMEM((lat_tiles, pieces, sub, channels), F32),
        pltpu.VMEM((lat_tiles, pieces, sub, channels), BF16),
        pltpu.VMEM((pieces, sub, channels), BF16),
        pltpu.VMEM((lon_tiles, members, sub, channels), BF16),
        pltpu.VMEM((members, lon_tiles, sub, channels), BF16),
        pltpu.VMEM((lon_tiles, sub, channels), BF16),
        pltpu.VMEM((lon_tiles, sub, channels), BF16),
        pltpu.VMEM((members, sub, channels), BF16),
        pltpu.VMEM((lat_tiles, small, channels), F32),
        pltpu.VMEM((members, small, channels), F32),
        pltpu.VMEM((lon_tiles, small, channels), F32),
        pltpu.SemaphoreType.DMA((9,)),
        pair(5),
        pair(5),
        pair(tiles),
        pair(lat_tiles),
        pair(members),
        pair(lon_tiles),
        pair(len(chunks) * lat_tiles),
        pair(len(chunks) * members),
        pair(len(chunks) * lon_tiles),
        pair(len(chunks) * members),
    ]
    cost = pl.CostEstimate(
        flops=2 * rows * cells * channels * channels * 29, bytes_accessed=3 << 20, transcendentals=rows * cells * channels
    )
    outs = pl.pallas_call(
        functools.partial(fused_kernel, (members, lat_tiles, lon_tiles, grad_scale, chunks)),
        out_shape=(
            jax.ShapeDtypeStruct(state.shape, BF16),
            jax.ShapeDtypeStruct((members, sub, channels), BF16),
            jax.ShapeDtypeStruct((fields, channels), F32),
        ),
        in_specs=[hbm] * 9 + [smem],
        out_specs=(vmem, vmem, vmem),
        scratch_shapes=scratch,
        cost_estimate=cost,
        compiler_params=pltpu.CompilerParams(
            collective_id=0, has_side_effects=True, vmem_limit_bytes=56 << 20
        ),
    )(
        state[0],
        state_cot[0],
        flux_flat,
        conv_weight,
        mix_weight,
        flux_weight,
        regrid_weights,
        tables[0],
        tables[1],
        wet_rows,
    )
    return place(*outs)


def step(state, state_cot, flux_cot, conv_weight, *rest):
    members, lat_tiles, lon_tiles = (lax.axis_size(name) for name in ("ens", "oy", "ox"))
    grad_rows = (conv_weight.shape[0] + 1) * state.shape[3]
    whole_tiles = grad_rows % (lat_tiles * lon_tiles * members * EDGE) == 0
    fused = lat_tiles == 2 and lon_tiles > 1 and whole_tiles
    return (fused_body if fused else body)(state, state_cot, flux_cot, conv_weight, *rest)


def solution(mesh):
    in_specs = (
        P("ens", "oy", "ox", None),
        P("ens", "oy", "ox", None),
        P("ens", ("oy", "ox"), None, None),
        P(),
        P(),
        P(),
        P(),
        P(),
        P(),
        P("oy", "ox"),
    )
    out_specs = (P("ens", "oy", "ox", None), P(("oy", "ox"), None), P())
    return jax.shard_map(step, mesh=mesh, in_specs=in_specs, out_specs=out_specs, check_vma=False)
```

```python
import functools
import math

import jax
import jax.numpy as jnp
from jax import lax
from jax.experimental import pallas as pl
from jax.experimental.pallas import tpu as pltpu
from jax.sharding import PartitionSpec as P

CAP = 5


def with_halo(cells, sides, width):
    for axis, dim in sides:
        count = lax.axis_size(axis)
        head = lax.slice_in_dim(cells, 0, width, axis=dim)
        tail = lax.slice_in_dim(cells, cells.shape[dim] - width, cells.shape[dim], axis=dim)
        cells = jnp.concatenate(
            [
                lax.ppermute(tail, axis, [(i, (i + 1) % count) for i in range(count)]),
                cells,
                lax.ppermute(head, axis, [((i + 1) % count, i) for i in range(count)]),
            ],
            axis=dim,
        )
    return cells


def shifted(value, axis, steps):
    count = lax.axis_size(axis)
    pairs = [(source, (source + steps) % count) for source in range(count)]
    return lax.ppermute(value, axis, pairs)


def zero_ends(padded, row_index, lat_tiles):
    top_keep = jnp.where(row_index > 0, 1.0, 0.0).astype(padded.dtype)
    bottom = jnp.where(row_index < lat_tiles - 1, 1.0, 0.0).astype(padded.dtype)
    return jnp.concatenate([padded[:1] * top_keep, padded[1:-1], padded[-1:] * bottom], axis=0)


def owner_rank(owners):
    entry_count = owners.shape[-1]
    same_owner = owners[..., :, None] == owners[..., None, :]
    earlier = jnp.arange(entry_count)[None, :] < jnp.arange(entry_count)[:, None]
    return jnp.sum(jnp.logical_and(same_owner, earlier), axis=-1)


def body(
    state,
    state_cot,
    flux_cot,
    conv_weight,
    mix_weight,
    flux_weight,
    regrid_weights,
    intersection_atm,
    intersection_offset,
    wet_rows,
):
    lat_tiles = lax.axis_size("oy")
    lon_tiles = lax.axis_size("ox")
    members = lax.axis_size("ens")
    row_index = lax.axis_index("oy")
    col_index = lax.axis_index("ox")
    tile_state = state[0]
    tile_rows, block_cells, channels = tile_state.shape
    cot_flat = state_cot[0].reshape(-1, channels)
    grad_scale = 1.0 / math.sqrt(members * lat_tiles * tile_rows * lon_tiles * block_cells)
    padded = with_halo(tile_state, (("oy", 0), ("ox", 1)), 1)
    padded = zero_ends(padded, row_index, lat_tiles)
    hidden = jnp.zeros((tile_rows * block_cells, channels), jnp.float32)
    for tap_index in range(9):
        tap_row, tap_col = (tap_index // 3, tap_index % 3)
        patch_rows = padded[tap_row : tap_row + tile_rows, tap_col : tap_col + block_cells].reshape(
            -1, channels
        )
        hidden = hidden + jnp.dot(
            patch_rows, conv_weight[tap_index], preferred_element_type=jnp.float32
        )
    activation = jax.nn.silu(hidden).astype(jnp.bfloat16)
    atm_dev = flux_cot.shape[1]
    cot_blocks = flux_cot[0]
    flux_fields = cot_blocks.shape[1]
    intersections = intersection_atm.shape[2]
    entries = tile_rows * intersections
    per_dev = (
        intersection_atm.reshape(lat_tiles, tile_rows, lon_tiles, intersections)
        .transpose(0, 2, 1, 3)
        .reshape(lat_tiles, lon_tiles, entries)
    )
    per_dev_offset = (
        intersection_offset.reshape(lat_tiles, tile_rows, lon_tiles, intersections)
        .transpose(0, 2, 1, 3)
        .reshape(lat_tiles, lon_tiles, entries)
    )
    band_rows = jnp.stack([row_index, (row_index + lat_tiles - 1) % lat_tiles])
    candidate = jnp.take(per_dev, band_rows, axis=0)
    candidate_offset = jnp.take(per_dev_offset, band_rows, axis=0)
    flat_index = row_index * lon_tiles + col_index
    candidate_owner = candidate // atm_dev
    is_mine = candidate_owner == flat_index
    slot_rank = owner_rank(candidate_owner)
    local_block = jnp.where(is_mine, candidate % atm_dev, 0)
    picked_cot = cot_blocks[local_block]
    picked_maps = regrid_weights[candidate_offset]
    products = jnp.einsum(
        "qsefa,qseoa->qsefo", picked_cot, picked_maps, preferred_element_type=jnp.float32
    )
    one_hot = jnp.logical_and(
        slot_rank[..., None] == jnp.arange(CAP)[None, None, None, :], is_mine[..., None]
    ).astype(jnp.float32)
    outbound = jnp.einsum("qsec,qsefo->qscfo", one_hot, products).astype(jnp.bfloat16)
    own_entries = per_dev[row_index, col_index]
    own_owner = own_entries // atm_dev
    own_slot = owner_rank(own_owner)
    same_in, next_in = (
        lax.all_to_all(outbound[0], "ox", split_axis=0, concat_axis=0, tiled=True),
        lax.all_to_all(outbound[1], "ox", split_axis=0, concat_axis=0, tiled=True),
    )
    next_in = shifted(next_in, "oy", -1)
    arrived = jnp.concatenate([same_in, next_in], axis=0).reshape(-1, flux_fields, block_cells)
    in_next = (own_owner // lon_tiles != row_index).astype(jnp.int32)
    slot_index = (in_next * lon_tiles + own_owner % lon_tiles) * CAP + own_slot
    values = (
        arrived[slot_index]
        .astype(jnp.float32)
        .reshape(tile_rows, intersections, flux_fields, block_cells)
    )
    wet_mask = (jnp.arange(tile_rows) < wet_rows[0, 0]).astype(jnp.float32)
    flux_cells = jnp.sum(values, axis=1) * wet_mask[:, None, None]
    act_grad = lax.dot_general(
        cot_flat, mix_weight, (((1,), (1,)), ((), ())), preferred_element_type=jnp.float32
    )
    act_grad = act_grad + jnp.einsum(
        "rfb,fc->rbc", flux_cells, flux_weight.astype(jnp.float32)
    ).reshape(-1, channels)
    gate_sig = jax.nn.sigmoid(hidden)
    hidden_grad = (act_grad * gate_sig * (1.0 + hidden * (1.0 - gate_sig))).astype(jnp.bfloat16)
    padded_grad = with_halo(
        hidden_grad.reshape(tile_rows, block_cells, channels), (("oy", 0), ("ox", 1)), 1
    )
    padded_grad = zero_ends(padded_grad, row_index, lat_tiles)
    input_grad = cot_flat.astype(jnp.float32)
    tap_grads = []
    for tap_index in range(9):
        tap_row, tap_col = (tap_index // 3, tap_index % 3)
        back_rows = padded_grad[
            2 - tap_row : 2 - tap_row + tile_rows, 2 - tap_col : 2 - tap_col + block_cells
        ].reshape(-1, channels)
        input_grad = input_grad + lax.dot_general(
            back_rows,
            conv_weight[tap_index],
            (((1,), (1,)), ((), ())),
            preferred_element_type=jnp.float32,
        )
        patch_rows = padded[tap_row : tap_row + tile_rows, tap_col : tap_col + block_cells].reshape(
            -1, channels
        )
        tap_grads.append(
            lax.dot_general(
                patch_rows,
                hidden_grad,
                (((0,), (0,)), ((), ())),
                preferred_element_type=jnp.float32,
            )
        )
    tap_grads.append(
        lax.dot_general(
            activation, cot_flat, (((0,), (0,)), ((), ())), preferred_element_type=jnp.float32
        )
    )
    weight_term = jnp.concatenate(tap_grads, axis=0) * grad_scale
    flux_term = (
        jnp.einsum(
            "rfb,rbc->fc",
            flux_cells,
            activation.reshape(tile_rows, block_cells, channels).astype(jnp.float32),
        )
        * grad_scale
    )
    weight_rows = lax.psum_scatter(weight_term, ("oy", "ox"), scatter_dimension=0, tiled=True)
    weight_out = lax.psum(weight_rows, "ens")
    flux_total = lax.psum(flux_term, ("ens", "oy", "ox"))
    input_out = input_grad.reshape(1, tile_rows, block_cells, channels).astype(jnp.bfloat16)
    return (input_out, weight_out, flux_total)


F32 = jnp.float32
BF16 = jnp.bfloat16
MESH = pl.DeviceIdType.MESH
EDGE = 16


def dot(a, b, dims=((1,), (0,))):
    return lax.dot_general(a, b, (dims, ((), ())), preferred_element_type=F32)


def remote(src, dst, send_sem, recv_sem, target):
    return pltpu.make_async_remote_copy(
        src_ref=src,
        dst_ref=dst,
        send_sem=send_sem,
        recv_sem=recv_sem,
        device_id=target,
        device_id_type=MESH,
    )


def start_all(copies):
    for copy in copies:
        copy.start()
    return copies


def halo_copies(src, src_at, padded, rows, cells, lat, lon, lon_tiles, sems):
    row0, col0 = src_at
    other = 1 - lat
    east = lax.rem(lon + 1, lon_tiles)
    west = lax.rem(lon + lon_tiles - 1, lon_tiles)
    edge_row = row0 + other * (rows - 1)
    land_row = lat * (rows + 1)
    body_rows, dst_rows = pl.ds(row0, rows), pl.ds(1, rows)
    head, last = pl.ds(col0, EDGE), pl.ds(col0 + cells - EDGE, EDGE)
    left, middle, right = pl.ds(0, EDGE), pl.ds(EDGE, cells), pl.ds(EDGE + cells, EDGE)
    plan = [
        (src.at[pl.ds(edge_row, 1), pl.ds(col0, cells)], padded.at[pl.ds(land_row, 1), middle], other, lon),
        (src.at[body_rows, last], padded.at[dst_rows, left], lat, east),
        (src.at[body_rows, head], padded.at[dst_rows, right], lat, west),
        (src.at[pl.ds(edge_row, 1), last], padded.at[pl.ds(land_row, 1), left], other, east),
        (src.at[pl.ds(edge_row, 1), head], padded.at[pl.ds(land_row, 1), right], other, west),
    ]
    send, recv = sems
    return [
        remote(a, b, send.at[n], recv.at[n], {"oy": y, "ox": x})
        for n, (a, b, y, x) in enumerate(plan)
    ]


def exchange(axis, count, me, source, target, sems, base=0):
    send, recv = sems
    copies = []
    for step in range(1, count):
        to = lax.rem(me + step, count)
        copies.append(
            remote(source(to), target(me), send.at[base + step - 1], recv.at[base + step - 1], {axis: to})
        )
    return copies


def wait_all(copies):
    for copy in copies:
        copy.wait_recv()


def shift_cells(padded, wide, columns, rows, cells, order):
    channels = padded.shape[2]
    for row in range(rows + 2):
        wide[row] = padded[row].astype(F32)
        for n, col in enumerate(order):
            here = slice(n * channels, (n + 1) * channels)
            if col == 1:
                columns[row, :, here] = padded[row, EDGE : EDGE + cells]
            else:
                columns[row, :, here] = wide[row, pl.ds(EDGE - 1 + col, cells), :].astype(BF16)


def store_rows(target, first, value):
    pieces, sub = target.shape[1:3]
    done = 0
    while done < value.shape[0]:
        at = first + done
        piece, row = at // sub, at % sub
        count = min(sub - row, value.shape[0] - done)
        target[piece // pieces, piece % pieces, row : row + count, :] = value[done : done + count].astype(
            target.dtype
        )
        done += count


def fused_kernel(
    sizes,
    state_in,
    cot_in,
    flux_cot_in,
    conv_in,
    mix_in,
    flux_weight_in,
    regrid_in,
    atm_in,
    offset_in,
    wet,
    input_out,
    weight_out,
    flux_out,
    cot,
    flux_cot,
    conv,
    mix,
    flux_weight,
    regrid,
    atm,
    offset,
    padded,
    padded_grad,
    wide,
    columns,
    turned,
    grad_columns,
    entry_cell,
    entry_map,
    flux_send,
    flux_recv,
    flux_rows,
    grads,
    grads_half,
    recv_lat,
    sum_lat,
    recv_ens,
    sum_ens,
    recv_lon,
    rows_all,
    flux_lat,
    flux_ens,
    flux_lon,
    load_sems,
    state_sems,
    grad_sems,
    flux_sems,
    flux_lat_sems,
    flux_ens_sems,
    flux_lon_sems,
    lat_sems,
    ens_sems,
    lon_sems,
    out_sems,
):
    members, lat_tiles, lon_tiles, grad_scale, chunks = sizes
    ens, lat, lon = lax.axis_index("ens"), lax.axis_index("oy"), lax.axis_index("ox")
    rows, cells, channels = cot.shape
    fields = flux_weight.shape[0]
    intersections = atm.shape[1]
    maps = regrid.shape[0]
    tiles = lat_tiles * lon_tiles
    flat = lat * lon_tiles + lon
    cells_here = flux_cot.shape[0]

    barrier = pltpu.get_barrier_semaphore()
    for step in range(1, tiles):
        peer = lax.rem(flat + step, tiles)
        pl.semaphore_signal(
            barrier, inc=1, device_id={"oy": peer // lon_tiles, "ox": lax.rem(peer, lon_tiles)}, device_id_type=MESH
        )
    for step in range(1, members):
        pl.semaphore_signal(
            barrier, inc=1, device_id={"ens": lax.rem(ens + step, members)}, device_id_type=MESH
        )
    loads = [
        pltpu.make_async_copy(src, dst, load_sems.at[n])
        for n, (src, dst) in enumerate(
            [
                (atm_in, atm),
                (offset_in, offset),
                (flux_cot_in, flux_cot),
                (regrid_in, regrid),
                (cot_in, cot),
                (mix_in, mix),
                (state_in, padded.at[pl.ds(1, rows), pl.ds(EDGE, cells)]),
                (flux_weight_in, flux_weight),
                (conv_in, conv),
            ]
        )
    ]
    for load in loads:
        load.start()

    outside = lat * (rows + 1)
    padded[pl.ds(outside, 1)] = jnp.zeros((1,) + padded.shape[1:], BF16)
    padded_grad[pl.ds(outside, 1)] = jnp.zeros((1,) + padded.shape[1:], BF16)

    pl.semaphore_wait(barrier, tiles - 1 + members - 1)
    state_copies = start_all(
        halo_copies(state_in, (0, 0), padded, rows, cells, lat, lon, lon_tiles, state_sems)
    )

    loads[0].wait()
    loads[1].wait()
    entry = 0
    for k in range(intersections):
        for tile in range(tiles):
            for row in range(rows):
                at = (tile % lon_tiles, k, (tile // lon_tiles) * rows + row)
                entry_cell[pl.ds(entry, fields), :] = jnp.full((fields, cells), atm[at], jnp.int32)
                entry_map[pl.ds(entry, fields), :] = jnp.full((fields, cells), offset[at], jnp.int32)
                entry += fields
    field_iota = lax.broadcasted_iota(jnp.int32, entry_cell.shape, 0) % fields
    lane = lax.broadcasted_iota(jnp.int32, entry_cell.shape, 1)
    which_cell = entry_cell[...] * fields + (field_iota - lane - flat * cells_here)
    which_map = entry_map[...]
    loads[2].wait()
    one_hot = [
        jnp.where(which_cell == part * cells, 1.0, 0.0).astype(BF16) for part in range(cells_here // cells)
    ]
    picked = dot(jnp.concatenate(one_hot, axis=1), flux_cot[...])
    loads[3].wait()
    products = jnp.zeros(which_cell.shape, F32)
    for m in range(0, maps, 2):
        chosen = [jnp.where(which_map == n, picked, 0.0).astype(BF16) for n in range(m, min(m + 2, maps))]
        taken = [regrid[n] for n in range(m, min(m + 2, maps))]
        products = products + dot(
            jnp.concatenate(chosen, axis=1), jnp.concatenate(taken, axis=1), ((1,), (1,))
        )
    products = products.astype(BF16).astype(F32)
    span = tiles * rows * fields
    share = products[:span]
    for k in range(1, intersections):
        share = share + products[k * span : (k + 1) * span]
    flux_send[...] = share.reshape(flux_send.shape)
    flux_recv[pl.ds(flat, 1)] = flux_send[pl.ds(flat, 1)]

    flux_copies = []
    for step in range(1, tiles):
        peer = lax.rem(flat + step, tiles)
        flux_copies.append(
            remote(
                flux_send.at[peer],
                flux_recv.at[flat],
                flux_sems[0].at[step - 1],
                flux_sems[1].at[step - 1],
                {"oy": peer // lon_tiles, "ox": lax.rem(peer, lon_tiles)},
            )
        )
    start_all(flux_copies)

    for load in loads[4:]:
        load.wait()
    flux_rows[...] = jnp.zeros(flux_rows.shape, F32)
    for n in range(2 * rows):
        flux_rows[n * fields : (n + 1) * fields, :] = flux_weight[...].astype(F32)
    cot_flat = cot[...].reshape(rows * cells, channels)
    act_grad = dot(cot_flat, mix[...], ((1,), (1,)))
    wait_all(state_copies)
    shift_cells(padded, wide, columns, rows, cells, (0, 1, 2))
    hidden = jnp.zeros((rows * cells, channels), F32)
    for p in range(3):
        hidden = hidden + dot(
            columns[p : p + rows].reshape(rows * cells, 3 * channels),
            conv[3 * p : 3 * p + 3].reshape(3 * channels, channels),
        )
    gate = jax.nn.sigmoid(hidden)
    activation = (hidden * gate).astype(BF16)
    slope = gate * (1.0 + hidden * (1.0 - gate))
    turned[...] = columns[...].reshape((rows + 2) * cells, 3 * channels).T
    term = dot(activation, cot_flat, ((0,), (0,)))
    store_rows(grads, 9 * channels, term)
    store_rows(grads_half, 9 * channels, term)

    wait_all(flux_copies)
    row_iota = lax.broadcasted_iota(jnp.int32, (rows * fields, cells), 0) // fields
    flux = flux_recv[0]
    for tile in range(1, tiles):
        flux = flux + flux_recv[tile]
    flux = jnp.where(row_iota < wet[0, 0], flux, 0.0)
    flux_high = flux.astype(BF16).astype(F32)
    flux_low = flux - flux_high
    both = jnp.concatenate([flux_high, flux_low], axis=0)
    both_iota = jnp.concatenate([row_iota, row_iota], axis=0)
    heads = flux_rows[...].astype(BF16)
    masked = []
    for row in range(rows):
        mine = jnp.where(both_iota == row, both, 0.0).astype(BF16)
        masked.append(mine)
        here = slice(row * cells, (row + 1) * cells)
        extra = dot(mine, heads, ((0,), (0,)))
        padded_grad[row + 1, EDGE : EDGE + cells] = ((act_grad[here] + extra) * slope[here]).astype(BF16)
    grad_copies = start_all(
        halo_copies(padded_grad, (1, EDGE), padded_grad, rows, cells, lat, lon, lon_tiles, grad_sems)
    )

    def tap_grads(target, first, last):
        hidden_grad = padded_grad[1 : rows + 1, EDGE : EDGE + cells].reshape(rows * cells, channels)
        tap = first
        while tap < last:
            p, q = tap // 3, tap % 3
            count = min(3 - q, last - tap)
            left = turned[q * channels : (q + count) * channels, p * cells : (p + rows) * cells]
            store_rows(target, tap * channels, dot(left, hidden_grad))
            tap += count

    taps = grads.shape[1] * grads.shape[2] // channels
    for part in range(lat_tiles):

        @pl.when(lat != part)
        def _():
            tap_grads(grads_half, part * taps, min((part + 1) * taps, 9))

    lat_copies = [
        start_all(
            exchange(
                "oy",
                lat_tiles,
                lat,
                lambda to: grads_half.at[to, :, pl.ds(at, count)],
                lambda me: recv_lat.at[:, pl.ds(at, count)],
                lat_sems,
                n * lat_tiles,
            )
        )
        for n, (at, count) in enumerate(chunks)
    ]
    flux_rows[...] = dot(jnp.concatenate(masked, axis=1), activation)
    total = flux_rows[:fields, :]
    for n in range(1, 2 * rows):
        total = total + flux_rows[n * fields : (n + 1) * fields, :]
    flux_lat[pl.ds(lat, 1)] = jnp.zeros((1,) + flux_lat.shape[1:], F32)
    flux_lat[pl.ds(lat, 1), 0:fields, :] = total[None]
    flux_lat_copies = start_all(
        exchange("oy", lat_tiles, lat, lambda to: flux_lat.at[lat], lambda me: flux_lat.at[me], flux_lat_sems)
    )

    for part in range(lat_tiles):

        @pl.when(lat == part)
        def _():
            tap_grads(grads, part * taps, min((part + 1) * taps, 9))

    ens_copies = []
    for n, (at, count) in enumerate(chunks):
        wait_all(lat_copies[n])
        own = grads[pl.ds(lat, 1), :, at : at + count]
        part = (own[0] + recv_lat[:, at : at + count].astype(F32)).astype(BF16)
        sum_lat[:, :, at : at + count] = part.reshape(lon_tiles, members, count, channels)
        ens_copies.append(
            start_all(
                exchange(
                    "ens",
                    members,
                    ens,
                    lambda to: sum_lat.at[:, to, pl.ds(at, count)],
                    lambda me: recv_ens.at[me, :, pl.ds(at, count)],
                    ens_sems,
                    n * members,
                )
            )
        )
    recv_ens[pl.ds(ens, 1)] = sum_lat[:, pl.ds(ens, 1)].reshape((1,) + recv_ens.shape[1:])
    wait_all(flux_lat_copies)
    total = flux_lat[0]
    for n in range(1, lat_tiles):
        total = total + flux_lat[n]
    flux_ens[pl.ds(ens, 1)] = total[None]
    flux_ens_copies = start_all(
        exchange("ens", members, ens, lambda to: flux_ens.at[ens], lambda me: flux_ens.at[me], flux_ens_sems)
    )

    wait_all(grad_copies)
    shift_cells(padded_grad, wide, grad_columns, rows, cells, (2, 1, 0))
    input_grad = cot_flat.astype(F32)
    for p in range(3):
        back = grad_columns[2 - p : 2 - p + rows].reshape(rows * cells, 3 * channels)
        taps = jnp.concatenate([conv[3 * p + q] for q in range(3)], axis=1)
        input_grad = input_grad + dot(back, taps, ((1,), (1,)))
    input_out[...] = input_grad.astype(BF16).reshape(input_out.shape)

    lon_copies, out_copies = [], []

    def gather_chunk(n):
        at, count = chunks[n]
        wait_all(lon_copies[n])
        total = recv_lon[0, at : at + count].astype(F32)
        for other in range(1, lon_tiles):
            total = total + recv_lon[other, at : at + count].astype(F32)
        rows_all[pl.ds(ens, 1), at : at + count] = (total * grad_scale).astype(BF16)[None]
        out_copies.append(
            start_all(
                exchange(
                    "ens",
                    members,
                    ens,
                    lambda to: rows_all.at[ens, pl.ds(at, count)],
                    lambda me: rows_all.at[me, pl.ds(at, count)],
                    out_sems,
                    n * members,
                )
            )
        )

    for n, (at, count) in enumerate(chunks):
        wait_all(ens_copies[n])
        total = recv_ens[0, :, at : at + count].astype(F32)
        for other in range(1, members):
            total = total + recv_ens[other, :, at : at + count].astype(F32)
        sum_ens[:, at : at + count] = total.astype(BF16)
        lon_copies.append(
            start_all(
                exchange(
                    "ox",
                    lon_tiles,
                    lon,
                    lambda to: sum_ens.at[to, pl.ds(at, count)],
                    lambda me: recv_lon.at[me, pl.ds(at, count)],
                    lon_sems,
                    n * lon_tiles,
                )
            )
        )
        recv_lon[pl.ds(lon, 1), at : at + count] = sum_ens[pl.ds(lon, 1), at : at + count]
        if n == 0:
            wait_all(flux_ens_copies)
            total = flux_ens[0]
            for other in range(1, members):
                total = total + flux_ens[other]
            flux_lon[pl.ds(lon, 1)] = total[None]
            flux_lon_copies = start_all(
                exchange("ox", lon_tiles, lon, lambda to: flux_lon.at[lon], lambda me: flux_lon.at[me], flux_lon_sems)
            )
        else:
            gather_chunk(n - 1)
    wait_all(flux_lon_copies)
    total = flux_lon[0]
    for n in range(1, lon_tiles):
        total = total + flux_lon[n]
    flux_out[...] = total[:fields] * grad_scale
    gather_chunk(len(chunks) - 1)
    for copies in out_copies:
        wait_all(copies)
    weight_out[...] = rows_all[...]
    started = state_copies + flux_copies + grad_copies + flux_lat_copies + flux_ens_copies + flux_lon_copies
    for copies in [started] + lat_copies + ens_copies + lon_copies + out_copies:
        for copy in copies:
            copy.wait_send()


def place_kernel(input_grad, weight_rows, flux_grad, input_out, weight_out, flux_out, wide, sems):
    copies = [
        pltpu.make_async_copy(input_grad, input_out, sems.at[0]),
        pltpu.make_async_copy(flux_grad, flux_out, sems.at[1]),
        pltpu.make_async_copy(wide, weight_out, sems.at[2]),
    ]
    copies[0].start()
    copies[1].start()
    wide[...] = weight_rows[...].reshape(wide.shape).astype(F32)
    copies[2].start()
    for copy in copies:
        copy.wait()


def place(input_grad, weight_rows, flux_grad):
    channels = weight_rows.shape[2]
    weight_shape = (weight_rows.shape[0] * weight_rows.shape[1], channels)
    vmem = pl.BlockSpec(memory_space=pltpu.VMEM)
    hbm = pl.BlockSpec(memory_space=pltpu.HBM)
    return pl.pallas_call(
        place_kernel,
        out_shape=(
            jax.ShapeDtypeStruct(input_grad.shape, BF16),
            jax.ShapeDtypeStruct(weight_shape, F32),
            jax.ShapeDtypeStruct(flux_grad.shape, F32),
        ),
        in_specs=[vmem] * 3,
        out_specs=(hbm, hbm, hbm),
        scratch_shapes=[pltpu.VMEM(weight_shape, F32), pltpu.SemaphoreType.DMA((3,))],
        compiler_params=pltpu.CompilerParams(vmem_limit_bytes=56 << 20),
    )(input_grad, weight_rows, flux_grad)


def fused_body(
    state,
    state_cot,
    flux_cot,
    conv_weight,
    mix_weight,
    flux_weight,
    regrid_weights,
    intersection_atm,
    intersection_offset,
    wet_rows,
):
    members, lat_tiles, lon_tiles = (lax.axis_size(name) for name in ("ens", "oy", "ox"))
    rows, cells, channels = state.shape[1:]
    fields = flux_weight.shape[0]
    tiles = lat_tiles * lon_tiles
    grad_rows = (conv_weight.shape[0] + 1) * channels
    band = grad_rows // lat_tiles
    pieces = lon_tiles * members
    sub = band // pieces
    grad_scale = 1.0 / math.sqrt(members * lat_tiles * rows * lon_tiles * cells)
    entries = tiles * rows * intersection_atm.shape[2] * fields
    halo = (rows + 2, cells + 2 * EDGE, channels)
    spread = (rows + 2, cells, 3 * channels)
    small = 2 * fields
    size = 2 * EDGE
    chunks = [(at, min(size, sub - at)) for at in range(0, sub, size)]

    def pair(count):
        return (pltpu.SemaphoreType.DMA((count,)), pltpu.SemaphoreType.DMA((count,)))

    vmem = pl.BlockSpec(memory_space=pltpu.VMEM)
    smem = pl.BlockSpec(memory_space=pltpu.SMEM)
    hbm = pl.BlockSpec(memory_space=pltpu.HBM)
    flux_flat = flux_cot[0].reshape(-1, cells)
    tables = [table.transpose(1, 2, 0) for table in (intersection_atm, intersection_offset)]
    scratch = [
        pltpu.VMEM((rows, cells, channels), BF16),
        pltpu.VMEM(flux_flat.shape, BF16),
        pltpu.VMEM(conv_weight.shape, BF16),
        pltpu.VMEM(mix_weight.shape, BF16),
        pltpu.VMEM(flux_weight.shape, BF16),
        pltpu.VMEM(regrid_weights.shape, BF16),
        pltpu.SMEM(tables[0].shape, jnp.int32),
        pltpu.SMEM(tables[1].shape, jnp.int32),
        pltpu.VMEM(halo, BF16),
        pltpu.VMEM(halo, BF16),
        pltpu.VMEM(halo, F32),
        pltpu.VMEM(spread, BF16),
        pltpu.VMEM((3 * channels, (rows + 2) * cells), BF16),
        pltpu.VMEM(spread, BF16),
        pltpu.VMEM((entries, cells), jnp.int32),
        pltpu.VMEM((entries, cells), jnp.int32),
        pltpu.VMEM((tiles, rows * fields, cells), F32),
        pltpu.VMEM((tiles, rows * fields, cells), F32),
        pltpu.VMEM((2 * rows * fields, channels), F32),
        pltpu.VMEM((lat_tiles, pieces, sub, channels), F32),
        pltpu.VMEM((lat_tiles, pieces, sub, channels), BF16),
        pltpu.VMEM((pieces, sub, channels), BF16),
        pltpu.VMEM((lon_tiles, members, sub, channels), BF16),
        pltpu.VMEM((members, lon_tiles, sub, channels), BF16),
        pltpu.VMEM((lon_tiles, sub, channels), BF16),
        pltpu.VMEM((lon_tiles, sub, channels), BF16),
        pltpu.VMEM((members, sub, channels), BF16),
        pltpu.VMEM((lat_tiles, small, channels), F32),
        pltpu.VMEM((members, small, channels), F32),
        pltpu.VMEM((lon_tiles, small, channels), F32),
        pltpu.SemaphoreType.DMA((9,)),
        pair(5),
        pair(5),
        pair(tiles),
        pair(lat_tiles),
        pair(members),
        pair(lon_tiles),
        pair(len(chunks) * lat_tiles),
        pair(len(chunks) * members),
        pair(len(chunks) * lon_tiles),
        pair(len(chunks) * members),
    ]
    cost = pl.CostEstimate(
        flops=2 * rows * cells * channels * channels * 29, bytes_accessed=3 << 20, transcendentals=rows * cells * channels
    )
    outs = pl.pallas_call(
        functools.partial(fused_kernel, (members, lat_tiles, lon_tiles, grad_scale, chunks)),
        out_shape=(
            jax.ShapeDtypeStruct(state.shape, BF16),
            jax.ShapeDtypeStruct((members, sub, channels), BF16),
            jax.ShapeDtypeStruct((fields, channels), F32),
        ),
        in_specs=[hbm] * 9 + [smem],
        out_specs=(vmem, vmem, vmem),
        scratch_shapes=scratch,
        cost_estimate=cost,
        compiler_params=pltpu.CompilerParams(
            collective_id=0, has_side_effects=True, vmem_limit_bytes=56 << 20
        ),
    )(
        state[0],
        state_cot[0],
        flux_flat,
        conv_weight,
        mix_weight,
        flux_weight,
        regrid_weights,
        tables[0],
        tables[1],
        wet_rows,
    )
    return place(*outs)


def step(state, state_cot, flux_cot, conv_weight, *rest):
    members, lat_tiles, lon_tiles = (lax.axis_size(name) for name in ("ens", "oy", "ox"))
    grad_rows = (conv_weight.shape[0] + 1) * state.shape[3]
    whole_tiles = grad_rows % (lat_tiles * lon_tiles * members * EDGE) == 0
    whole_taps = grad_rows // lat_tiles % state.shape[3] == 0
    fused = lat_tiles == 2 and lon_tiles > 1 and whole_tiles and whole_taps
    return (fused_body if fused else body)(state, state_cot, flux_cot, conv_weight, *rest)


def solution(mesh):
    in_specs = (
        P("ens", "oy", "ox", None),
        P("ens", "oy", "ox", None),
        P("ens", ("oy", "ox"), None, None),
        P(),
        P(),
        P(),
        P(),
        P(),
        P(),
        P("oy", "ox"),
    )
    out_specs = (P("ens", "oy", "ox", None), P(("oy", "ox"), None), P())
    return jax.shard_map(step, mesh=mesh, in_specs=in_specs, out_specs=out_specs, check_vma=False)
```

```python
import functools
import math

import jax
import jax.numpy as jnp
from jax import lax
from jax.experimental import pallas as pl
from jax.experimental.pallas import tpu as pltpu
from jax.sharding import PartitionSpec as P

CAP = 5


def with_halo(cells, sides, width):
    for axis, dim in sides:
        count = lax.axis_size(axis)
        head = lax.slice_in_dim(cells, 0, width, axis=dim)
        tail = lax.slice_in_dim(cells, cells.shape[dim] - width, cells.shape[dim], axis=dim)
        cells = jnp.concatenate(
            [
                lax.ppermute(tail, axis, [(i, (i + 1) % count) for i in range(count)]),
                cells,
                lax.ppermute(head, axis, [((i + 1) % count, i) for i in range(count)]),
            ],
            axis=dim,
        )
    return cells


def shifted(value, axis, steps):
    count = lax.axis_size(axis)
    pairs = [(source, (source + steps) % count) for source in range(count)]
    return lax.ppermute(value, axis, pairs)


def zero_ends(padded, row_index, lat_tiles):
    top_keep = jnp.where(row_index > 0, 1.0, 0.0).astype(padded.dtype)
    bottom = jnp.where(row_index < lat_tiles - 1, 1.0, 0.0).astype(padded.dtype)
    return jnp.concatenate([padded[:1] * top_keep, padded[1:-1], padded[-1:] * bottom], axis=0)


def owner_rank(owners):
    entry_count = owners.shape[-1]
    same_owner = owners[..., :, None] == owners[..., None, :]
    earlier = jnp.arange(entry_count)[None, :] < jnp.arange(entry_count)[:, None]
    return jnp.sum(jnp.logical_and(same_owner, earlier), axis=-1)


def body(
    state,
    state_cot,
    flux_cot,
    conv_weight,
    mix_weight,
    flux_weight,
    regrid_weights,
    intersection_atm,
    intersection_offset,
    wet_rows,
):
    lat_tiles = lax.axis_size("oy")
    lon_tiles = lax.axis_size("ox")
    members = lax.axis_size("ens")
    row_index = lax.axis_index("oy")
    col_index = lax.axis_index("ox")
    tile_state = state[0]
    tile_rows, block_cells, channels = tile_state.shape
    cot_flat = state_cot[0].reshape(-1, channels)
    grad_scale = 1.0 / math.sqrt(members * lat_tiles * tile_rows * lon_tiles * block_cells)
    padded = with_halo(tile_state, (("oy", 0), ("ox", 1)), 1)
    padded = zero_ends(padded, row_index, lat_tiles)
    hidden = jnp.zeros((tile_rows * block_cells, channels), jnp.float32)
    for tap_index in range(9):
        tap_row, tap_col = (tap_index // 3, tap_index % 3)
        patch_rows = padded[tap_row : tap_row + tile_rows, tap_col : tap_col + block_cells].reshape(
            -1, channels
        )
        hidden = hidden + jnp.dot(
            patch_rows, conv_weight[tap_index], preferred_element_type=jnp.float32
        )
    activation = jax.nn.silu(hidden).astype(jnp.bfloat16)
    atm_dev = flux_cot.shape[1]
    cot_blocks = flux_cot[0]
    flux_fields = cot_blocks.shape[1]
    intersections = intersection_atm.shape[2]
    entries = tile_rows * intersections
    per_dev = (
        intersection_atm.reshape(lat_tiles, tile_rows, lon_tiles, intersections)
        .transpose(0, 2, 1, 3)
        .reshape(lat_tiles, lon_tiles, entries)
    )
    per_dev_offset = (
        intersection_offset.reshape(lat_tiles, tile_rows, lon_tiles, intersections)
        .transpose(0, 2, 1, 3)
        .reshape(lat_tiles, lon_tiles, entries)
    )
    band_rows = jnp.stack([row_index, (row_index + lat_tiles - 1) % lat_tiles])
    candidate = jnp.take(per_dev, band_rows, axis=0)
    candidate_offset = jnp.take(per_dev_offset, band_rows, axis=0)
    flat_index = row_index * lon_tiles + col_index
    candidate_owner = candidate // atm_dev
    is_mine = candidate_owner == flat_index
    slot_rank = owner_rank(candidate_owner)
    local_block = jnp.where(is_mine, candidate % atm_dev, 0)
    picked_cot = cot_blocks[local_block]
    picked_maps = regrid_weights[candidate_offset]
    products = jnp.einsum(
        "qsefa,qseoa->qsefo", picked_cot, picked_maps, preferred_element_type=jnp.float32
    )
    one_hot = jnp.logical_and(
        slot_rank[..., None] == jnp.arange(CAP)[None, None, None, :], is_mine[..., None]
    ).astype(jnp.float32)
    outbound = jnp.einsum("qsec,qsefo->qscfo", one_hot, products).astype(jnp.bfloat16)
    own_entries = per_dev[row_index, col_index]
    own_owner = own_entries // atm_dev
    own_slot = owner_rank(own_owner)
    same_in, next_in = (
        lax.all_to_all(outbound[0], "ox", split_axis=0, concat_axis=0, tiled=True),
        lax.all_to_all(outbound[1], "ox", split_axis=0, concat_axis=0, tiled=True),
    )
    next_in = shifted(next_in, "oy", -1)
    arrived = jnp.concatenate([same_in, next_in], axis=0).reshape(-1, flux_fields, block_cells)
    in_next = (own_owner // lon_tiles != row_index).astype(jnp.int32)
    slot_index = (in_next * lon_tiles + own_owner % lon_tiles) * CAP + own_slot
    values = (
        arrived[slot_index]
        .astype(jnp.float32)
        .reshape(tile_rows, intersections, flux_fields, block_cells)
    )
    wet_mask = (jnp.arange(tile_rows) < wet_rows[0, 0]).astype(jnp.float32)
    flux_cells = jnp.sum(values, axis=1) * wet_mask[:, None, None]
    act_grad = lax.dot_general(
        cot_flat, mix_weight, (((1,), (1,)), ((), ())), preferred_element_type=jnp.float32
    )
    act_grad = act_grad + jnp.einsum(
        "rfb,fc->rbc", flux_cells, flux_weight.astype(jnp.float32)
    ).reshape(-1, channels)
    gate_sig = jax.nn.sigmoid(hidden)
    hidden_grad = (act_grad * gate_sig * (1.0 + hidden * (1.0 - gate_sig))).astype(jnp.bfloat16)
    padded_grad = with_halo(
        hidden_grad.reshape(tile_rows, block_cells, channels), (("oy", 0), ("ox", 1)), 1
    )
    padded_grad = zero_ends(padded_grad, row_index, lat_tiles)
    input_grad = cot_flat.astype(jnp.float32)
    tap_grads = []
    for tap_index in range(9):
        tap_row, tap_col = (tap_index // 3, tap_index % 3)
        back_rows = padded_grad[
            2 - tap_row : 2 - tap_row + tile_rows, 2 - tap_col : 2 - tap_col + block_cells
        ].reshape(-1, channels)
        input_grad = input_grad + lax.dot_general(
            back_rows,
            conv_weight[tap_index],
            (((1,), (1,)), ((), ())),
            preferred_element_type=jnp.float32,
        )
        patch_rows = padded[tap_row : tap_row + tile_rows, tap_col : tap_col + block_cells].reshape(
            -1, channels
        )
        tap_grads.append(
            lax.dot_general(
                patch_rows,
                hidden_grad,
                (((0,), (0,)), ((), ())),
                preferred_element_type=jnp.float32,
            )
        )
    tap_grads.append(
        lax.dot_general(
            activation, cot_flat, (((0,), (0,)), ((), ())), preferred_element_type=jnp.float32
        )
    )
    weight_term = jnp.concatenate(tap_grads, axis=0) * grad_scale
    flux_term = (
        jnp.einsum(
            "rfb,rbc->fc",
            flux_cells,
            activation.reshape(tile_rows, block_cells, channels).astype(jnp.float32),
        )
        * grad_scale
    )
    weight_rows = lax.psum_scatter(weight_term, ("oy", "ox"), scatter_dimension=0, tiled=True)
    weight_out = lax.psum(weight_rows, "ens")
    flux_total = lax.psum(flux_term, ("ens", "oy", "ox"))
    input_out = input_grad.reshape(1, tile_rows, block_cells, channels).astype(jnp.bfloat16)
    return (input_out, weight_out, flux_total)


F32 = jnp.float32
BF16 = jnp.bfloat16
MESH = pl.DeviceIdType.MESH
EDGE = 16


def dot(a, b, dims=((1,), (0,))):
    return lax.dot_general(a, b, (dims, ((), ())), preferred_element_type=F32)


def remote(src, dst, send_sem, recv_sem, target):
    return pltpu.make_async_remote_copy(
        src_ref=src,
        dst_ref=dst,
        send_sem=send_sem,
        recv_sem=recv_sem,
        device_id=target,
        device_id_type=MESH,
    )


def start_all(copies):
    for copy in copies:
        copy.start()
    return copies


def halo_copies(src, src_at, padded, rows, cells, lat, lon, lon_tiles, sems):
    row0, col0 = src_at
    other = 1 - lat
    east = lax.rem(lon + 1, lon_tiles)
    west = lax.rem(lon + lon_tiles - 1, lon_tiles)
    edge_row = row0 + other * (rows - 1)
    land_row = lat * (rows + 1)
    body_rows, dst_rows = pl.ds(row0, rows), pl.ds(1, rows)
    head, last = pl.ds(col0, EDGE), pl.ds(col0 + cells - EDGE, EDGE)
    left, middle, right = pl.ds(0, EDGE), pl.ds(EDGE, cells), pl.ds(EDGE + cells, EDGE)
    plan = [
        (src.at[pl.ds(edge_row, 1), pl.ds(col0, cells)], padded.at[pl.ds(land_row, 1), middle], other, lon),
        (src.at[body_rows, last], padded.at[dst_rows, left], lat, east),
        (src.at[body_rows, head], padded.at[dst_rows, right], lat, west),
        (src.at[pl.ds(edge_row, 1), last], padded.at[pl.ds(land_row, 1), left], other, east),
        (src.at[pl.ds(edge_row, 1), head], padded.at[pl.ds(land_row, 1), right], other, west),
    ]
    send, recv = sems
    return [
        remote(a, b, send.at[n], recv.at[n], {"oy": y, "ox": x})
        for n, (a, b, y, x) in enumerate(plan)
    ]


def exchange(axis, count, me, source, target, sems, base=0):
    send, recv = sems
    copies = []
    for step in range(1, count):
        to = lax.rem(me + step, count)
        copies.append(
            remote(source(to), target(me), send.at[base + step - 1], recv.at[base + step - 1], {axis: to})
        )
    return copies


def wait_all(copies):
    for copy in copies:
        copy.wait_recv()


def shift_cells(padded, wide, columns, rows, cells, order):
    channels = padded.shape[2]
    for row in range(rows + 2):
        wide[row] = padded[row].astype(F32)
        for n, col in enumerate(order):
            here = slice(n * channels, (n + 1) * channels)
            if col == 1:
                columns[row, :, here] = padded[row, EDGE : EDGE + cells]
            else:
                columns[row, :, here] = wide[row, pl.ds(EDGE - 1 + col, cells), :].astype(BF16)


def store_rows(target, first, value):
    pieces, sub = target.shape[1:3]
    done = 0
    while done < value.shape[0]:
        at = first + done
        piece, row = at // sub, at % sub
        count = min(sub - row, value.shape[0] - done)
        target[piece // pieces, piece % pieces, row : row + count, :] = value[done : done + count].astype(
            target.dtype
        )
        done += count


def fused_kernel(
    sizes,
    state_in,
    cot_in,
    flux_cot_in,
    conv_in,
    mix_in,
    flux_weight_in,
    regrid_in,
    atm_in,
    offset_in,
    wet,
    input_out,
    weight_out,
    flux_out,
    cot,
    flux_cot,
    conv,
    mix,
    flux_weight,
    regrid,
    atm,
    offset,
    padded,
    padded_grad,
    wide,
    columns,
    turned,
    grad_columns,
    entry_cell,
    entry_map,
    flux_send,
    flux_recv,
    flux_rows,
    grads,
    grads_half,
    recv_lat,
    sum_lat,
    recv_ens,
    sum_ens,
    recv_lon,
    rows_all,
    input_sum,
    flux_lat,
    flux_ens,
    flux_lon,
    load_sems,
    state_sems,
    grad_sems,
    flux_sems,
    flux_lat_sems,
    flux_ens_sems,
    flux_lon_sems,
    lat_sems,
    ens_sems,
    lon_sems,
    out_sems,
):
    members, lat_tiles, lon_tiles, grad_scale, chunks = sizes
    ens, lat, lon = lax.axis_index("ens"), lax.axis_index("oy"), lax.axis_index("ox")
    rows, cells, channels = cot.shape
    fields = flux_weight.shape[0]
    intersections = atm.shape[1]
    maps = regrid.shape[0]
    tiles = lat_tiles * lon_tiles
    flat = lat * lon_tiles + lon
    cells_here = flux_cot.shape[0]

    barrier = pltpu.get_barrier_semaphore()
    for step in range(1, tiles):
        peer = lax.rem(flat + step, tiles)
        pl.semaphore_signal(
            barrier, inc=1, device_id={"oy": peer // lon_tiles, "ox": lax.rem(peer, lon_tiles)}, device_id_type=MESH
        )
    for step in range(1, members):
        pl.semaphore_signal(
            barrier, inc=1, device_id={"ens": lax.rem(ens + step, members)}, device_id_type=MESH
        )
    loads = [
        pltpu.make_async_copy(src, dst, load_sems.at[n])
        for n, (src, dst) in enumerate(
            [
                (atm_in, atm),
                (offset_in, offset),
                (flux_cot_in, flux_cot),
                (regrid_in, regrid),
                (cot_in, cot),
                (mix_in, mix),
                (state_in, padded.at[pl.ds(1, rows), pl.ds(EDGE, cells)]),
                (flux_weight_in, flux_weight),
                (conv_in, conv),
            ]
        )
    ]
    for load in loads:
        load.start()

    outside = lat * (rows + 1)
    padded[pl.ds(outside, 1)] = jnp.zeros((1,) + padded.shape[1:], BF16)
    padded_grad[pl.ds(outside, 1)] = jnp.zeros((1,) + padded.shape[1:], BF16)

    pl.semaphore_wait(barrier, tiles - 1 + members - 1)
    state_copies = start_all(
        halo_copies(state_in, (0, 0), padded, rows, cells, lat, lon, lon_tiles, state_sems)
    )

    loads[0].wait()
    loads[1].wait()
    entry = 0
    for k in range(intersections):
        for tile in range(tiles):
            for row in range(rows):
                at = (tile % lon_tiles, k, (tile // lon_tiles) * rows + row)
                entry_cell[pl.ds(entry, fields), :] = jnp.full((fields, cells), atm[at], jnp.int32)
                entry_map[pl.ds(entry, fields), :] = jnp.full((fields, cells), offset[at], jnp.int32)
                entry += fields
    field_iota = lax.broadcasted_iota(jnp.int32, entry_cell.shape, 0) % fields
    lane = lax.broadcasted_iota(jnp.int32, entry_cell.shape, 1)
    which_cell = entry_cell[...] * fields + (field_iota - lane - flat * cells_here)
    which_map = entry_map[...]
    loads[2].wait()
    one_hot = [
        jnp.where(which_cell == part * cells, 1.0, 0.0).astype(BF16) for part in range(cells_here // cells)
    ]
    picked = dot(jnp.concatenate(one_hot, axis=1), flux_cot[...])
    loads[3].wait()
    span = tiles * rows * fields
    part_of = [slice(k * span, (k + 1) * span) for k in range(intersections)]
    share = jnp.zeros((span, cells), F32)
    for m in range(0, maps, 2):
        chosen, taken = [], []
        for n in range(m, min(m + 2, maps)):
            total = jnp.where(which_map[part_of[0]] == n, picked[part_of[0]], 0.0)
            for k in range(1, intersections):
                total = total + jnp.where(which_map[part_of[k]] == n, picked[part_of[k]], 0.0)
            chosen.append(total.astype(BF16))
            taken.append(regrid[n])
        share = share + dot(jnp.concatenate(chosen, axis=1), jnp.concatenate(taken, axis=1), ((1,), (1,)))
    flux_send[...] = share.reshape(flux_send.shape)
    flux_recv[pl.ds(flat, 1)] = flux_send[pl.ds(flat, 1)]

    flux_copies = []
    for step in range(1, tiles):
        peer = lax.rem(flat + step, tiles)
        flux_copies.append(
            remote(
                flux_send.at[peer],
                flux_recv.at[flat],
                flux_sems[0].at[step - 1],
                flux_sems[1].at[step - 1],
                {"oy": peer // lon_tiles, "ox": lax.rem(peer, lon_tiles)},
            )
        )
    start_all(flux_copies)

    for load in loads[4:]:
        load.wait()
    flux_rows[...] = jnp.zeros(flux_rows.shape, F32)
    for n in range(2 * rows):
        flux_rows[n * fields : (n + 1) * fields, :] = flux_weight[...].astype(F32)
    cot_flat = cot[...].reshape(rows * cells, channels)
    act_grad = dot(cot_flat, mix[...], ((1,), (1,)))
    wait_all(state_copies)
    shift_cells(padded, wide, columns, rows, cells, (0, 1, 2))
    hidden = jnp.zeros((rows * cells, channels), F32)
    for p in range(3):
        hidden = hidden + dot(
            columns[p : p + rows].reshape(rows * cells, 3 * channels),
            conv[3 * p : 3 * p + 3].reshape(3 * channels, channels),
        )
        first, last = p * (rows + 2) // 3, (p + 1) * (rows + 2) // 3
        if last > first:
            turned[:, first * cells : last * cells] = (
                columns[first:last].reshape((last - first) * cells, 3 * channels).T
            )
    gate = jax.nn.sigmoid(hidden)
    activation = (hidden * gate).astype(BF16)
    slope = gate * (1.0 + hidden * (1.0 - gate))
    term = dot(activation, cot_flat, ((0,), (0,)))
    store_rows(grads, 9 * channels, term)
    store_rows(grads_half, 9 * channels, term)

    wait_all(flux_copies)
    row_iota = lax.broadcasted_iota(jnp.int32, (rows * fields, cells), 0) // fields
    flux = flux_recv[0]
    for tile in range(1, tiles):
        flux = flux + flux_recv[tile]
    flux = jnp.where(row_iota < wet[0, 0], flux, 0.0)
    flux_high = flux.astype(BF16).astype(F32)
    flux_low = flux - flux_high
    both = jnp.concatenate([flux_high, flux_low], axis=0)
    both_iota = jnp.concatenate([row_iota, row_iota], axis=0)
    heads = flux_rows[...].astype(BF16)
    masked = []
    for row in range(rows):
        mine = jnp.where(both_iota == row, both, 0.0).astype(BF16)
        masked.append(mine)
        here = slice(row * cells, (row + 1) * cells)
        extra = dot(mine, heads, ((0,), (0,)))
        padded_grad[row + 1, EDGE : EDGE + cells] = ((act_grad[here] + extra) * slope[here]).astype(BF16)
    grad_copies = start_all(
        halo_copies(padded_grad, (1, EDGE), padded_grad, rows, cells, lat, lon, lon_tiles, grad_sems)
    )

    def tap_grads(target, first, last):
        hidden_grad = padded_grad[1 : rows + 1, EDGE : EDGE + cells].reshape(rows * cells, channels)
        tap = first
        while tap < last:
            p, q = tap // 3, tap % 3
            count = min(3 - q, last - tap)
            left = turned[q * channels : (q + count) * channels, p * cells : (p + rows) * cells]
            store_rows(target, tap * channels, dot(left, hidden_grad))
            tap += count

    taps = grads.shape[1] * grads.shape[2] // channels
    for part in range(lat_tiles):

        @pl.when(lat != part)
        def _():
            tap_grads(grads_half, part * taps, min((part + 1) * taps, 9))

    lat_copies = [
        start_all(
            exchange(
                "oy",
                lat_tiles,
                lat,
                lambda to: grads_half.at[to, :, pl.ds(at, count)],
                lambda me: recv_lat.at[:, pl.ds(at, count)],
                lat_sems,
                n * lat_tiles,
            )
        )
        for n, (at, count) in enumerate(chunks)
    ]
    flux_rows[...] = dot(jnp.concatenate(masked, axis=1), activation)
    total = flux_rows[:fields, :]
    for n in range(1, 2 * rows):
        total = total + flux_rows[n * fields : (n + 1) * fields, :]
    flux_lat[pl.ds(lat, 1)] = jnp.zeros((1,) + flux_lat.shape[1:], F32)
    flux_lat[pl.ds(lat, 1), 0:fields, :] = total[None]
    flux_lat_copies = start_all(
        exchange("oy", lat_tiles, lat, lambda to: flux_lat.at[lat], lambda me: flux_lat.at[me], flux_lat_sems)
    )

    for part in range(lat_tiles):

        @pl.when(lat == part)
        def _():
            tap_grads(grads, part * taps, min((part + 1) * taps, 9))

    ens_copies = []
    for n, (at, count) in enumerate(chunks):
        wait_all(lat_copies[n])
        own = grads[pl.ds(lat, 1), :, at : at + count]
        part = (own[0] + recv_lat[:, at : at + count].astype(F32)).astype(BF16)
        sum_lat[:, :, at : at + count] = part.reshape(lon_tiles, members, count, channels)
        ens_copies.append(
            start_all(
                exchange(
                    "ens",
                    members,
                    ens,
                    lambda to: sum_lat.at[:, to, pl.ds(at, count)],
                    lambda me: recv_ens.at[me, :, pl.ds(at, count)],
                    ens_sems,
                    n * members,
                )
            )
        )
    recv_ens[pl.ds(ens, 1)] = sum_lat[:, pl.ds(ens, 1)].reshape((1,) + recv_ens.shape[1:])
    wait_all(flux_lat_copies)
    total = flux_lat[0]
    for n in range(1, lat_tiles):
        total = total + flux_lat[n]
    flux_ens[pl.ds(ens, 1)] = total[None]
    flux_ens_copies = start_all(
        exchange("ens", members, ens, lambda to: flux_ens.at[ens], lambda me: flux_ens.at[me], flux_ens_sems)
    )

    wait_all(grad_copies)
    shift_cells(padded_grad, wide, grad_columns, rows, cells, (2, 1, 0))
    def input_part(p):
        back = grad_columns[2 - p : 2 - p + rows].reshape(rows * cells, 3 * channels)
        taps = jnp.concatenate([conv[3 * p + q] for q in range(3)], axis=1)
        before = input_sum[...] if p else cot_flat.astype(F32)
        total = before + dot(back, taps, ((1,), (1,)))
        if p < 2:
            input_sum[...] = total
        else:
            input_out[...] = total.astype(BF16).reshape(input_out.shape)

    input_part(0)
    lon_copies, out_copies = [], []

    def gather_chunk(n):
        at, count = chunks[n]
        wait_all(lon_copies[n])
        total = recv_lon[0, at : at + count].astype(F32)
        for other in range(1, lon_tiles):
            total = total + recv_lon[other, at : at + count].astype(F32)
        rows_all[pl.ds(ens, 1), at : at + count] = (total * grad_scale).astype(BF16)[None]
        out_copies.append(
            start_all(
                exchange(
                    "ens",
                    members,
                    ens,
                    lambda to: rows_all.at[ens, pl.ds(at, count)],
                    lambda me: rows_all.at[me, pl.ds(at, count)],
                    out_sems,
                    n * members,
                )
            )
        )

    for n, (at, count) in enumerate(chunks):
        wait_all(ens_copies[n])
        total = recv_ens[0, :, at : at + count].astype(F32)
        for other in range(1, members):
            total = total + recv_ens[other, :, at : at + count].astype(F32)
        sum_ens[:, at : at + count] = total.astype(BF16)
        lon_copies.append(
            start_all(
                exchange(
                    "ox",
                    lon_tiles,
                    lon,
                    lambda to: sum_ens.at[to, pl.ds(at, count)],
                    lambda me: recv_lon.at[me, pl.ds(at, count)],
                    lon_sems,
                    n * lon_tiles,
                )
            )
        )
        recv_lon[pl.ds(lon, 1), at : at + count] = sum_ens[pl.ds(lon, 1), at : at + count]
        if n == 0:
            wait_all(flux_ens_copies)
            total = flux_ens[0]
            for other in range(1, members):
                total = total + flux_ens[other]
            flux_lon[pl.ds(lon, 1)] = total[None]
            flux_lon_copies = start_all(
                exchange("ox", lon_tiles, lon, lambda to: flux_lon.at[lon], lambda me: flux_lon.at[me], flux_lon_sems)
            )
        else:
            gather_chunk(n - 1)
        if n < 2:
            input_part(n + 1)
    for p in range(len(chunks) + 1, 3):
        input_part(p)
    wait_all(flux_lon_copies)
    total = flux_lon[0]
    for n in range(1, lon_tiles):
        total = total + flux_lon[n]
    flux_out[...] = total[:fields] * grad_scale
    gather_chunk(len(chunks) - 1)
    for copies in out_copies:
        wait_all(copies)
    weight_out[...] = rows_all[...]
    started = state_copies + flux_copies + grad_copies + flux_lat_copies + flux_ens_copies + flux_lon_copies
    for copies in [started] + lat_copies + ens_copies + lon_copies + out_copies:
        for copy in copies:
            copy.wait_send()


def place_kernel(input_grad, weight_rows, flux_grad, input_out, weight_out, flux_out, wide, sems):
    copies = [
        pltpu.make_async_copy(input_grad, input_out, sems.at[0]),
        pltpu.make_async_copy(flux_grad, flux_out, sems.at[1]),
        pltpu.make_async_copy(wide, weight_out, sems.at[2]),
    ]
    copies[0].start()
    copies[1].start()
    wide[...] = weight_rows[...].reshape(wide.shape).astype(F32)
    copies[2].start()
    for copy in copies:
        copy.wait()


def place(input_grad, weight_rows, flux_grad):
    channels = weight_rows.shape[2]
    weight_shape = (weight_rows.shape[0] * weight_rows.shape[1], channels)
    vmem = pl.BlockSpec(memory_space=pltpu.VMEM)
    hbm = pl.BlockSpec(memory_space=pltpu.HBM)
    return pl.pallas_call(
        place_kernel,
        out_shape=(
            jax.ShapeDtypeStruct(input_grad.shape, BF16),
            jax.ShapeDtypeStruct(weight_shape, F32),
            jax.ShapeDtypeStruct(flux_grad.shape, F32),
        ),
        in_specs=[vmem] * 3,
        out_specs=(hbm, hbm, hbm),
        scratch_shapes=[pltpu.VMEM(weight_shape, F32), pltpu.SemaphoreType.DMA((3,))],
        compiler_params=pltpu.CompilerParams(vmem_limit_bytes=56 << 20),
    )(input_grad, weight_rows, flux_grad)


def fused_body(
    state,
    state_cot,
    flux_cot,
    conv_weight,
    mix_weight,
    flux_weight,
    regrid_weights,
    intersection_atm,
    intersection_offset,
    wet_rows,
):
    members, lat_tiles, lon_tiles = (lax.axis_size(name) for name in ("ens", "oy", "ox"))
    rows, cells, channels = state.shape[1:]
    fields = flux_weight.shape[0]
    tiles = lat_tiles * lon_tiles
    grad_rows = (conv_weight.shape[0] + 1) * channels
    band = grad_rows // lat_tiles
    pieces = lon_tiles * members
    sub = band // pieces
    grad_scale = 1.0 / math.sqrt(members * lat_tiles * rows * lon_tiles * cells)
    entries = tiles * rows * intersection_atm.shape[2] * fields
    halo = (rows + 2, cells + 2 * EDGE, channels)
    spread = (rows + 2, cells, 3 * channels)
    small = 2 * fields
    size = 2 * EDGE
    chunks = [(at, min(size, sub - at)) for at in range(0, sub, size)]

    def pair(count):
        return (pltpu.SemaphoreType.DMA((count,)), pltpu.SemaphoreType.DMA((count,)))

    vmem = pl.BlockSpec(memory_space=pltpu.VMEM)
    smem = pl.BlockSpec(memory_space=pltpu.SMEM)
    hbm = pl.BlockSpec(memory_space=pltpu.HBM)
    flux_flat = flux_cot[0].reshape(-1, cells)
    tables = [table.transpose(1, 2, 0) for table in (intersection_atm, intersection_offset)]
    scratch = [
        pltpu.VMEM((rows, cells, channels), BF16),
        pltpu.VMEM(flux_flat.shape, BF16),
        pltpu.VMEM(conv_weight.shape, BF16),
        pltpu.VMEM(mix_weight.shape, BF16),
        pltpu.VMEM(flux_weight.shape, BF16),
        pltpu.VMEM(regrid_weights.shape, BF16),
        pltpu.SMEM(tables[0].shape, jnp.int32),
        pltpu.SMEM(tables[1].shape, jnp.int32),
        pltpu.VMEM(halo, BF16),
        pltpu.VMEM(halo, BF16),
        pltpu.VMEM(halo, F32),
        pltpu.VMEM(spread, BF16),
        pltpu.VMEM((3 * channels, (rows + 2) * cells), BF16),
        pltpu.VMEM(spread, BF16),
        pltpu.VMEM((entries, cells), jnp.int32),
        pltpu.VMEM((entries, cells), jnp.int32),
        pltpu.VMEM((tiles, rows * fields, cells), F32),
        pltpu.VMEM((tiles, rows * fields, cells), F32),
        pltpu.VMEM((2 * rows * fields, channels), F32),
        pltpu.VMEM((lat_tiles, pieces, sub, channels), F32),
        pltpu.VMEM((lat_tiles, pieces, sub, channels), BF16),
        pltpu.VMEM((pieces, sub, channels), BF16),
        pltpu.VMEM((lon_tiles, members, sub, channels), BF16),
        pltpu.VMEM((members, lon_tiles, sub, channels), BF16),
        pltpu.VMEM((lon_tiles, sub, channels), BF16),
        pltpu.VMEM((lon_tiles, sub, channels), BF16),
        pltpu.VMEM((members, sub, channels), BF16),
        pltpu.VMEM((rows * cells, channels), F32),
        pltpu.VMEM((lat_tiles, small, channels), F32),
        pltpu.VMEM((members, small, channels), F32),
        pltpu.VMEM((lon_tiles, small, channels), F32),
        pltpu.SemaphoreType.DMA((9,)),
        pair(5),
        pair(5),
        pair(tiles),
        pair(lat_tiles),
        pair(members),
        pair(lon_tiles),
        pair(len(chunks) * lat_tiles),
        pair(len(chunks) * members),
        pair(len(chunks) * lon_tiles),
        pair(len(chunks) * members),
    ]
    cost = pl.CostEstimate(
        flops=2 * rows * cells * channels * channels * 29, bytes_accessed=3 << 20, transcendentals=rows * cells * channels
    )
    outs = pl.pallas_call(
        functools.partial(fused_kernel, (members, lat_tiles, lon_tiles, grad_scale, chunks)),
        out_shape=(
            jax.ShapeDtypeStruct(state.shape, BF16),
            jax.ShapeDtypeStruct((members, sub, channels), BF16),
            jax.ShapeDtypeStruct((fields, channels), F32),
        ),
        in_specs=[hbm] * 9 + [smem],
        out_specs=(vmem, vmem, vmem),
        scratch_shapes=scratch,
        cost_estimate=cost,
        compiler_params=pltpu.CompilerParams(
            collective_id=0, has_side_effects=True, vmem_limit_bytes=56 << 20
        ),
    )(
        state[0],
        state_cot[0],
        flux_flat,
        conv_weight,
        mix_weight,
        flux_weight,
        regrid_weights,
        tables[0],
        tables[1],
        wet_rows,
    )
    return place(*outs)


def step(state, state_cot, flux_cot, conv_weight, *rest):
    members, lat_tiles, lon_tiles = (lax.axis_size(name) for name in ("ens", "oy", "ox"))
    grad_rows = (conv_weight.shape[0] + 1) * state.shape[3]
    whole_tiles = grad_rows % (lat_tiles * lon_tiles * members * EDGE) == 0
    whole_taps = grad_rows // lat_tiles % state.shape[3] == 0
    fused = lat_tiles == 2 and lon_tiles > 1 and whole_tiles and whole_taps
    return (fused_body if fused else body)(state, state_cot, flux_cot, conv_weight, *rest)


def solution(mesh):
    in_specs = (
        P("ens", "oy", "ox", None),
        P("ens", "oy", "ox", None),
        P("ens", ("oy", "ox"), None, None),
        P(),
        P(),
        P(),
        P(),
        P(),
        P(),
        P("oy", "ox"),
    )
    out_specs = (P("ens", "oy", "ox", None), P(("oy", "ox"), None), P())
    return jax.shard_map(step, mesh=mesh, in_specs=in_specs, out_specs=out_specs, check_vma=False)
```

```python
import functools
import math

import jax
import jax.numpy as jnp
from jax import lax
from jax.experimental import pallas as pl
from jax.experimental.pallas import tpu as pltpu
from jax.sharding import PartitionSpec as P

CAP = 5


def with_halo(cells, sides, width):
    for axis, dim in sides:
        count = lax.axis_size(axis)
        head = lax.slice_in_dim(cells, 0, width, axis=dim)
        tail = lax.slice_in_dim(cells, cells.shape[dim] - width, cells.shape[dim], axis=dim)
        cells = jnp.concatenate(
            [
                lax.ppermute(tail, axis, [(i, (i + 1) % count) for i in range(count)]),
                cells,
                lax.ppermute(head, axis, [((i + 1) % count, i) for i in range(count)]),
            ],
            axis=dim,
        )
    return cells


def shifted(value, axis, steps):
    count = lax.axis_size(axis)
    pairs = [(source, (source + steps) % count) for source in range(count)]
    return lax.ppermute(value, axis, pairs)


def zero_ends(padded, row_index, lat_tiles):
    top_keep = jnp.where(row_index > 0, 1.0, 0.0).astype(padded.dtype)
    bottom = jnp.where(row_index < lat_tiles - 1, 1.0, 0.0).astype(padded.dtype)
    return jnp.concatenate([padded[:1] * top_keep, padded[1:-1], padded[-1:] * bottom], axis=0)


def owner_rank(owners):
    entry_count = owners.shape[-1]
    same_owner = owners[..., :, None] == owners[..., None, :]
    earlier = jnp.arange(entry_count)[None, :] < jnp.arange(entry_count)[:, None]
    return jnp.sum(jnp.logical_and(same_owner, earlier), axis=-1)


def body(
    state,
    state_cot,
    flux_cot,
    conv_weight,
    mix_weight,
    flux_weight,
    regrid_weights,
    intersection_atm,
    intersection_offset,
    wet_rows,
):
    lat_tiles = lax.axis_size("oy")
    lon_tiles = lax.axis_size("ox")
    members = lax.axis_size("ens")
    row_index = lax.axis_index("oy")
    col_index = lax.axis_index("ox")
    tile_state = state[0]
    tile_rows, block_cells, channels = tile_state.shape
    cot_flat = state_cot[0].reshape(-1, channels)
    grad_scale = 1.0 / math.sqrt(members * lat_tiles * tile_rows * lon_tiles * block_cells)
    padded = with_halo(tile_state, (("oy", 0), ("ox", 1)), 1)
    padded = zero_ends(padded, row_index, lat_tiles)
    hidden = jnp.zeros((tile_rows * block_cells, channels), jnp.float32)
    for tap_index in range(9):
        tap_row, tap_col = (tap_index // 3, tap_index % 3)
        patch_rows = padded[tap_row : tap_row + tile_rows, tap_col : tap_col + block_cells].reshape(
            -1, channels
        )
        hidden = hidden + jnp.dot(
            patch_rows, conv_weight[tap_index], preferred_element_type=jnp.float32
        )
    activation = jax.nn.silu(hidden).astype(jnp.bfloat16)
    atm_dev = flux_cot.shape[1]
    cot_blocks = flux_cot[0]
    flux_fields = cot_blocks.shape[1]
    intersections = intersection_atm.shape[2]
    entries = tile_rows * intersections
    per_dev = (
        intersection_atm.reshape(lat_tiles, tile_rows, lon_tiles, intersections)
        .transpose(0, 2, 1, 3)
        .reshape(lat_tiles, lon_tiles, entries)
    )
    per_dev_offset = (
        intersection_offset.reshape(lat_tiles, tile_rows, lon_tiles, intersections)
        .transpose(0, 2, 1, 3)
        .reshape(lat_tiles, lon_tiles, entries)
    )
    band_rows = jnp.stack([row_index, (row_index + lat_tiles - 1) % lat_tiles])
    candidate = jnp.take(per_dev, band_rows, axis=0)
    candidate_offset = jnp.take(per_dev_offset, band_rows, axis=0)
    flat_index = row_index * lon_tiles + col_index
    candidate_owner = candidate // atm_dev
    is_mine = candidate_owner == flat_index
    slot_rank = owner_rank(candidate_owner)
    local_block = jnp.where(is_mine, candidate % atm_dev, 0)
    picked_cot = cot_blocks[local_block]
    picked_maps = regrid_weights[candidate_offset]
    products = jnp.einsum(
        "qsefa,qseoa->qsefo", picked_cot, picked_maps, preferred_element_type=jnp.float32
    )
    one_hot = jnp.logical_and(
        slot_rank[..., None] == jnp.arange(CAP)[None, None, None, :], is_mine[..., None]
    ).astype(jnp.float32)
    outbound = jnp.einsum("qsec,qsefo->qscfo", one_hot, products).astype(jnp.bfloat16)
    own_entries = per_dev[row_index, col_index]
    own_owner = own_entries // atm_dev
    own_slot = owner_rank(own_owner)
    same_in, next_in = (
        lax.all_to_all(outbound[0], "ox", split_axis=0, concat_axis=0, tiled=True),
        lax.all_to_all(outbound[1], "ox", split_axis=0, concat_axis=0, tiled=True),
    )
    next_in = shifted(next_in, "oy", -1)
    arrived = jnp.concatenate([same_in, next_in], axis=0).reshape(-1, flux_fields, block_cells)
    in_next = (own_owner // lon_tiles != row_index).astype(jnp.int32)
    slot_index = (in_next * lon_tiles + own_owner % lon_tiles) * CAP + own_slot
    values = (
        arrived[slot_index]
        .astype(jnp.float32)
        .reshape(tile_rows, intersections, flux_fields, block_cells)
    )
    wet_mask = (jnp.arange(tile_rows) < wet_rows[0, 0]).astype(jnp.float32)
    flux_cells = jnp.sum(values, axis=1) * wet_mask[:, None, None]
    act_grad = lax.dot_general(
        cot_flat, mix_weight, (((1,), (1,)), ((), ())), preferred_element_type=jnp.float32
    )
    act_grad = act_grad + jnp.einsum(
        "rfb,fc->rbc", flux_cells, flux_weight.astype(jnp.float32)
    ).reshape(-1, channels)
    gate_sig = jax.nn.sigmoid(hidden)
    hidden_grad = (act_grad * gate_sig * (1.0 + hidden * (1.0 - gate_sig))).astype(jnp.bfloat16)
    padded_grad = with_halo(
        hidden_grad.reshape(tile_rows, block_cells, channels), (("oy", 0), ("ox", 1)), 1
    )
    padded_grad = zero_ends(padded_grad, row_index, lat_tiles)
    input_grad = cot_flat.astype(jnp.float32)
    tap_grads = []
    for tap_index in range(9):
        tap_row, tap_col = (tap_index // 3, tap_index % 3)
        back_rows = padded_grad[
            2 - tap_row : 2 - tap_row + tile_rows, 2 - tap_col : 2 - tap_col + block_cells
        ].reshape(-1, channels)
        input_grad = input_grad + lax.dot_general(
            back_rows,
            conv_weight[tap_index],
            (((1,), (1,)), ((), ())),
            preferred_element_type=jnp.float32,
        )
        patch_rows = padded[tap_row : tap_row + tile_rows, tap_col : tap_col + block_cells].reshape(
            -1, channels
        )
        tap_grads.append(
            lax.dot_general(
                patch_rows,
                hidden_grad,
                (((0,), (0,)), ((), ())),
                preferred_element_type=jnp.float32,
            )
        )
    tap_grads.append(
        lax.dot_general(
            activation, cot_flat, (((0,), (0,)), ((), ())), preferred_element_type=jnp.float32
        )
    )
    weight_term = jnp.concatenate(tap_grads, axis=0) * grad_scale
    flux_term = (
        jnp.einsum(
            "rfb,rbc->fc",
            flux_cells,
            activation.reshape(tile_rows, block_cells, channels).astype(jnp.float32),
        )
        * grad_scale
    )
    weight_rows = lax.psum_scatter(weight_term, ("oy", "ox"), scatter_dimension=0, tiled=True)
    weight_out = lax.psum(weight_rows, "ens")
    flux_total = lax.psum(flux_term, ("ens", "oy", "ox"))
    input_out = input_grad.reshape(1, tile_rows, block_cells, channels).astype(jnp.bfloat16)
    return (input_out, weight_out, flux_total)


F32 = jnp.float32
BF16 = jnp.bfloat16
MESH = pl.DeviceIdType.MESH
EDGE = 16


def dot(a, b, dims=((1,), (0,))):
    return lax.dot_general(a, b, (dims, ((), ())), preferred_element_type=F32)


def remote(src, dst, send_sem, recv_sem, target):
    return pltpu.make_async_remote_copy(
        src_ref=src,
        dst_ref=dst,
        send_sem=send_sem,
        recv_sem=recv_sem,
        device_id=target,
        device_id_type=MESH,
    )


def start_all(copies):
    for copy in copies:
        copy.start()
    return copies


def halo_copies(src, src_at, padded, rows, cells, lat, lon, lon_tiles, sems):
    row0, col0 = src_at
    other = 1 - lat
    east = lax.rem(lon + 1, lon_tiles)
    west = lax.rem(lon + lon_tiles - 1, lon_tiles)
    edge_row = row0 + other * (rows - 1)
    land_row = lat * (rows + 1)
    body_rows, dst_rows = pl.ds(row0, rows), pl.ds(1, rows)
    head, last = pl.ds(col0, EDGE), pl.ds(col0 + cells - EDGE, EDGE)
    left, middle, right = pl.ds(0, EDGE), pl.ds(EDGE, cells), pl.ds(EDGE + cells, EDGE)
    plan = [
        (src.at[pl.ds(edge_row, 1), pl.ds(col0, cells)], padded.at[pl.ds(land_row, 1), middle], other, lon),
        (src.at[body_rows, last], padded.at[dst_rows, left], lat, east),
        (src.at[body_rows, head], padded.at[dst_rows, right], lat, west),
        (src.at[pl.ds(edge_row, 1), last], padded.at[pl.ds(land_row, 1), left], other, east),
        (src.at[pl.ds(edge_row, 1), head], padded.at[pl.ds(land_row, 1), right], other, west),
    ]
    send, recv = sems
    return [
        remote(a, b, send.at[n], recv.at[n], {"oy": y, "ox": x})
        for n, (a, b, y, x) in enumerate(plan)
    ]


def exchange(axis, count, me, source, target, sems, base=0):
    send, recv = sems
    copies = []
    for step in range(1, count):
        to = lax.rem(me + step, count)
        copies.append(
            remote(source(to), target(me), send.at[base + step - 1], recv.at[base + step - 1], {axis: to})
        )
    return copies


def wait_all(copies):
    for copy in copies:
        copy.wait_recv()


def shift_cells(padded, wide, columns, rows, cells, order, edges=True):
    channels = padded.shape[2]
    middle = slice(EDGE, EDGE + cells)
    for row in range(rows + 2):
        if edges:
            wide[row] = padded[row].astype(F32)
        else:
            wide[row, 0:EDGE] = jnp.zeros((EDGE, channels), F32)
            wide[row, middle] = padded[row, middle].astype(F32)
            wide[row, EDGE + cells :] = jnp.zeros((EDGE, channels), F32)
        for n, col in enumerate(order):
            here = slice(n * channels, (n + 1) * channels)
            if col == 1:
                columns[row, :, here] = padded[row, middle]
            else:
                columns[row, :, here] = wide[row, pl.ds(EDGE - 1 + col, cells), :].astype(BF16)


def turn(columns, turned, q):
    channels = columns.shape[2] // 3
    here = slice(q * channels, (q + 1) * channels)
    turned[here, :] = columns[:, :, here].reshape(-1, channels).T


def store_rows(target, first, value):
    pieces, sub = target.shape[1:3]
    done = 0
    while done < value.shape[0]:
        at = first + done
        piece, row = at // sub, at % sub
        count = min(sub - row, value.shape[0] - done)
        target[piece // pieces, piece % pieces, row : row + count, :] = value[done : done + count].astype(
            target.dtype
        )
        done += count


def fused_kernel(
    sizes,
    state_in,
    cot_in,
    flux_cot_in,
    conv_in,
    mix_in,
    flux_weight_in,
    regrid_in,
    atm_in,
    offset_in,
    wet,
    input_out,
    weight_out,
    flux_out,
    cot,
    flux_cot,
    conv,
    mix,
    flux_weight,
    regrid,
    atm,
    offset,
    padded,
    padded_grad,
    wide,
    columns,
    turned,
    grad_columns,
    entry_cell,
    entry_map,
    flux_send,
    flux_recv,
    flux_rows,
    grads,
    grads_half,
    recv_lat,
    sum_lat,
    recv_ens,
    sum_ens,
    recv_lon,
    rows_all,
    input_sum,
    hidden_sum,
    edge,
    edge_part,
    flux_lat,
    flux_ens,
    flux_lon,
    load_sems,
    state_sems,
    grad_sems,
    flux_sems,
    flux_lat_sems,
    flux_ens_sems,
    flux_lon_sems,
    lat_sems,
    ens_sems,
    lon_sems,
    out_sems,
):
    members, lat_tiles, lon_tiles, grad_scale, chunks = sizes
    ens, lat, lon = lax.axis_index("ens"), lax.axis_index("oy"), lax.axis_index("ox")
    rows, cells, channels = cot.shape
    fields = flux_weight.shape[0]
    intersections = atm.shape[1]
    maps = regrid.shape[0]
    tiles = lat_tiles * lon_tiles
    flat = lat * lon_tiles + lon
    cells_here = flux_cot.shape[0]

    barrier = pltpu.get_barrier_semaphore()
    for step in range(1, tiles):
        peer = lax.rem(flat + step, tiles)
        pl.semaphore_signal(
            barrier, inc=1, device_id={"oy": peer // lon_tiles, "ox": lax.rem(peer, lon_tiles)}, device_id_type=MESH
        )
    for step in range(1, members):
        pl.semaphore_signal(
            barrier, inc=1, device_id={"ens": lax.rem(ens + step, members)}, device_id_type=MESH
        )
    loads = [
        pltpu.make_async_copy(src, dst, load_sems.at[n])
        for n, (src, dst) in enumerate(
            [
                (atm_in, atm),
                (offset_in, offset),
                (flux_cot_in, flux_cot),
                (regrid_in, regrid),
                (cot_in, cot),
                (mix_in, mix),
                (state_in, padded.at[pl.ds(1, rows), pl.ds(EDGE, cells)]),
                (flux_weight_in, flux_weight),
                (conv_in, conv),
            ]
        )
    ]
    for load in loads:
        load.start()

    outside = lat * (rows + 1)
    padded[pl.ds(outside, 1)] = jnp.zeros((1,) + padded.shape[1:], BF16)
    padded_grad[pl.ds(outside, 1)] = jnp.zeros((1,) + padded.shape[1:], BF16)


    loads[0].wait()
    loads[1].wait()
    entry = 0
    for k in range(intersections):
        for tile in range(tiles):
            for row in range(rows):
                at = (tile % lon_tiles, k, (tile // lon_tiles) * rows + row)
                entry_cell[pl.ds(entry, fields), :] = jnp.full((fields, cells), atm[at], jnp.int32)
                entry_map[pl.ds(entry, fields), :] = jnp.full((fields, cells), offset[at], jnp.int32)
                entry += fields
    field_iota = lax.broadcasted_iota(jnp.int32, entry_cell.shape, 0) % fields
    lane = lax.broadcasted_iota(jnp.int32, entry_cell.shape, 1)
    which_cell = entry_cell[...] * fields + (field_iota - lane - flat * cells_here)
    which_map = entry_map[...]
    loads[2].wait()
    one_hot = [
        jnp.where(which_cell == part * cells, 1.0, 0.0).astype(BF16) for part in range(cells_here // cells)
    ]
    picked = dot(jnp.concatenate(one_hot, axis=1), flux_cot[...])
    loads[3].wait()
    span = tiles * rows * fields
    part_of = [slice(k * span, (k + 1) * span) for k in range(intersections)]
    share = jnp.zeros((span, cells), F32)
    for m in range(0, maps, 2):
        chosen, taken = [], []
        for n in range(m, min(m + 2, maps)):
            total = jnp.where(which_map[part_of[0]] == n, picked[part_of[0]], 0.0)
            for k in range(1, intersections):
                total = total + jnp.where(which_map[part_of[k]] == n, picked[part_of[k]], 0.0)
            chosen.append(total.astype(BF16))
            taken.append(regrid[n])
        share = share + dot(jnp.concatenate(chosen, axis=1), jnp.concatenate(taken, axis=1), ((1,), (1,)))
    flux_send[...] = share.reshape(flux_send.shape)
    flux_recv[pl.ds(flat, 1)] = flux_send[pl.ds(flat, 1)]

    pl.semaphore_wait(barrier, tiles - 1 + members - 1)
    state_copies = start_all(
        halo_copies(state_in, (0, 0), padded, rows, cells, lat, lon, lon_tiles, state_sems)
    )

    flux_copies = []
    for step in range(1, tiles):
        peer = lax.rem(flat + step, tiles)
        flux_copies.append(
            remote(
                flux_send.at[peer],
                flux_recv.at[flat],
                flux_sems[0].at[step - 1],
                flux_sems[1].at[step - 1],
                {"oy": peer // lon_tiles, "ox": lax.rem(peer, lon_tiles)},
            )
        )
    start_all(flux_copies)

    for load in loads[4:]:
        load.wait()
    flux_rows[...] = jnp.zeros(flux_rows.shape, F32)
    for n in range(2 * rows):
        flux_rows[n * fields : (n + 1) * fields, :] = flux_weight[...].astype(F32)
    cot_flat = cot[...].reshape(rows * cells, channels)
    act_grad = dot(cot_flat, mix[...], ((1,), (1,)))
    state_copies[0].wait_recv()
    shift_cells(padded, wide, columns, rows, cells, (0, 1, 2), False)
    hidden = jnp.zeros((rows * cells, channels), F32)
    for p in range(3):
        hidden = hidden + dot(
            columns[p : p + rows].reshape(rows * cells, 3 * channels),
            conv[3 * p : 3 * p + 3].reshape(3 * channels, channels),
        )
    hidden_sum[...] = hidden
    turn(columns, turned, 1)

    wait_all(state_copies[1:])
    edge[...] = jnp.zeros(edge.shape, F32)
    cell_iota = lax.broadcasted_iota(jnp.int32, (EDGE, channels), 0)
    for row in range(rows + 2):
        west = padded[row, 0:EDGE].astype(F32)[EDGE - 1 :]
        east = padded[row, EDGE + cells :].astype(F32)[:1]
        edge[0, row : row + 1] = west
        edge[1, row : row + 1] = east
        kept = columns[row, 0:EDGE, 0:channels].astype(F32)
        columns[row, 0:EDGE, 0:channels] = jnp.where(cell_iota == 0, west, kept).astype(BF16)
        kept = columns[row, cells - EDGE :, 2 * channels :].astype(F32)
        columns[row, cells - EDGE :, 2 * channels :] = jnp.where(cell_iota == EDGE - 1, east, kept).astype(BF16)
    for side in range(2):
        cells_there = edge[side].astype(BF16)
        for p in range(3):
            edge_part[side, p] = dot(cells_there, conv[3 * p + 2 * side])
        for row in range(rows):
            at = row * cells + side * (cells - 1)
            added = hidden_sum[at : at + 1]
            for p in range(3):
                added = added + edge_part[side, p, row + p : row + p + 1]
            hidden_sum[at : at + 1] = added
    hidden = hidden_sum[...]
    turn(columns, turned, 0)
    turn(columns, turned, 2)
    gate = jax.nn.sigmoid(hidden)
    activation = (hidden * gate).astype(BF16)
    slope = gate * (1.0 + hidden * (1.0 - gate))
    term = dot(activation, cot_flat, ((0,), (0,)))
    store_rows(grads, 9 * channels, term)
    store_rows(grads_half, 9 * channels, term)

    wait_all(flux_copies)
    row_iota = lax.broadcasted_iota(jnp.int32, (rows * fields, cells), 0) // fields
    flux = flux_recv[0]
    for tile in range(1, tiles):
        flux = flux + flux_recv[tile]
    flux = jnp.where(row_iota < wet[0, 0], flux, 0.0)
    flux_high = flux.astype(BF16).astype(F32)
    flux_low = flux - flux_high
    both = jnp.concatenate([flux_high, flux_low], axis=0)
    both_iota = jnp.concatenate([row_iota, row_iota], axis=0)
    heads = flux_rows[...].astype(BF16)
    masked = []
    for row in range(rows):
        mine = jnp.where(both_iota == row, both, 0.0).astype(BF16)
        masked.append(mine)
        here = slice(row * cells, (row + 1) * cells)
        extra = dot(mine, heads, ((0,), (0,)))
        padded_grad[row + 1, EDGE : EDGE + cells] = ((act_grad[here] + extra) * slope[here]).astype(BF16)
    grad_copies = start_all(
        halo_copies(padded_grad, (1, EDGE), padded_grad, rows, cells, lat, lon, lon_tiles, grad_sems)
    )

    def tap_grads(target, first, last):
        hidden_grad = padded_grad[1 : rows + 1, EDGE : EDGE + cells].reshape(rows * cells, channels)
        tap = first
        while tap < last:
            p, q = tap // 3, tap % 3
            count = min(3 - q, last - tap)
            left = turned[q * channels : (q + count) * channels, p * cells : (p + rows) * cells]
            store_rows(target, tap * channels, dot(left, hidden_grad))
            tap += count

    taps = grads.shape[1] * grads.shape[2] // channels
    for part in range(lat_tiles):

        @pl.when(lat != part)
        def _():
            tap_grads(grads_half, part * taps, min((part + 1) * taps, 9))

    lat_copies = [
        start_all(
            exchange(
                "oy",
                lat_tiles,
                lat,
                lambda to: grads_half.at[to, :, pl.ds(at, count)],
                lambda me: recv_lat.at[:, pl.ds(at, count)],
                lat_sems,
                n * lat_tiles,
            )
        )
        for n, (at, count) in enumerate(chunks)
    ]
    flux_rows[...] = dot(jnp.concatenate(masked, axis=1), activation)
    total = flux_rows[:fields, :]
    for n in range(1, 2 * rows):
        total = total + flux_rows[n * fields : (n + 1) * fields, :]
    flux_lat[pl.ds(lat, 1)] = jnp.zeros((1,) + flux_lat.shape[1:], F32)
    flux_lat[pl.ds(lat, 1), 0:fields, :] = total[None]
    flux_lat_copies = start_all(
        exchange("oy", lat_tiles, lat, lambda to: flux_lat.at[lat], lambda me: flux_lat.at[me], flux_lat_sems)
    )

    for part in range(lat_tiles):

        @pl.when(lat == part)
        def _():
            tap_grads(grads, part * taps, min((part + 1) * taps, 9))

    ens_copies = []
    for n, (at, count) in enumerate(chunks):
        wait_all(lat_copies[n])
        own = grads[pl.ds(lat, 1), :, at : at + count]
        part = (own[0] + recv_lat[:, at : at + count].astype(F32)).astype(BF16)
        sum_lat[:, :, at : at + count] = part.reshape(lon_tiles, members, count, channels)
        ens_copies.append(
            start_all(
                exchange(
                    "ens",
                    members,
                    ens,
                    lambda to: sum_lat.at[:, to, pl.ds(at, count)],
                    lambda me: recv_ens.at[me, :, pl.ds(at, count)],
                    ens_sems,
                    n * members,
                )
            )
        )
    recv_ens[pl.ds(ens, 1)] = sum_lat[:, pl.ds(ens, 1)].reshape((1,) + recv_ens.shape[1:])
    wait_all(flux_lat_copies)
    total = flux_lat[0]
    for n in range(1, lat_tiles):
        total = total + flux_lat[n]
    flux_ens[pl.ds(ens, 1)] = total[None]
    flux_ens_copies = start_all(
        exchange("ens", members, ens, lambda to: flux_ens.at[ens], lambda me: flux_ens.at[me], flux_ens_sems)
    )

    wait_all(grad_copies)
    shift_cells(padded_grad, wide, grad_columns, rows, cells, (2, 1, 0))
    def input_part(p):
        back = grad_columns[2 - p : 2 - p + rows].reshape(rows * cells, 3 * channels)
        taps = jnp.concatenate([conv[3 * p + q] for q in range(3)], axis=1)
        before = input_sum[...] if p else cot_flat.astype(F32)
        total = before + dot(back, taps, ((1,), (1,)))
        if p < 2:
            input_sum[...] = total
        else:
            input_out[...] = total.astype(BF16).reshape(input_out.shape)

    input_part(0)
    lon_copies, out_copies = [], []

    def gather_chunk(n):
        at, count = chunks[n]
        wait_all(lon_copies[n])
        total = recv_lon[0, at : at + count].astype(F32)
        for other in range(1, lon_tiles):
            total = total + recv_lon[other, at : at + count].astype(F32)
        rows_all[pl.ds(ens, 1), at : at + count] = (total * grad_scale).astype(BF16)[None]
        out_copies.append(
            start_all(
                exchange(
                    "ens",
                    members,
                    ens,
                    lambda to: rows_all.at[ens, pl.ds(at, count)],
                    lambda me: rows_all.at[me, pl.ds(at, count)],
                    out_sems,
                    n * members,
                )
            )
        )

    for n, (at, count) in enumerate(chunks):
        wait_all(ens_copies[n])
        total = recv_ens[0, :, at : at + count].astype(F32)
        for other in range(1, members):
            total = total + recv_ens[other, :, at : at + count].astype(F32)
        sum_ens[:, at : at + count] = total.astype(BF16)
        lon_copies.append(
            start_all(
                exchange(
                    "ox",
                    lon_tiles,
                    lon,
                    lambda to: sum_ens.at[to, pl.ds(at, count)],
                    lambda me: recv_lon.at[me, pl.ds(at, count)],
                    lon_sems,
                    n * lon_tiles,
                )
            )
        )
        recv_lon[pl.ds(lon, 1), at : at + count] = sum_ens[pl.ds(lon, 1), at : at + count]
        if n == 0:
            wait_all(flux_ens_copies)
            total = flux_ens[0]
            for other in range(1, members):
                total = total + flux_ens[other]
            flux_lon[pl.ds(lon, 1)] = total[None]
            flux_lon_copies = start_all(
                exchange("ox", lon_tiles, lon, lambda to: flux_lon.at[lon], lambda me: flux_lon.at[me], flux_lon_sems)
            )
        else:
            gather_chunk(n - 1)
        if n < 2:
            input_part(n + 1)
    for p in range(len(chunks) + 1, 3):
        input_part(p)
    wait_all(flux_lon_copies)
    total = flux_lon[0]
    for n in range(1, lon_tiles):
        total = total + flux_lon[n]
    flux_out[...] = total[:fields] * grad_scale
    gather_chunk(len(chunks) - 1)
    for copies in out_copies:
        wait_all(copies)
    weight_out[...] = rows_all[...]
    started = state_copies + flux_copies + grad_copies + flux_lat_copies + flux_ens_copies + flux_lon_copies
    for copies in [started] + lat_copies + ens_copies + lon_copies + out_copies:
        for copy in copies:
            copy.wait_send()


def place_kernel(input_grad, weight_rows, flux_grad, input_out, weight_out, flux_out, wide, sems):
    copies = [
        pltpu.make_async_copy(input_grad, input_out, sems.at[0]),
        pltpu.make_async_copy(flux_grad, flux_out, sems.at[1]),
        pltpu.make_async_copy(wide, weight_out, sems.at[2]),
    ]
    copies[0].start()
    copies[1].start()
    wide[...] = weight_rows[...].reshape(wide.shape).astype(F32)
    copies[2].start()
    for copy in copies:
        copy.wait()


def place(input_grad, weight_rows, flux_grad):
    channels = weight_rows.shape[2]
    weight_shape = (weight_rows.shape[0] * weight_rows.shape[1], channels)
    vmem = pl.BlockSpec(memory_space=pltpu.VMEM)
    hbm = pl.BlockSpec(memory_space=pltpu.HBM)
    return pl.pallas_call(
        place_kernel,
        out_shape=(
            jax.ShapeDtypeStruct(input_grad.shape, BF16),
            jax.ShapeDtypeStruct(weight_shape, F32),
            jax.ShapeDtypeStruct(flux_grad.shape, F32),
        ),
        in_specs=[vmem] * 3,
        out_specs=(hbm, hbm, hbm),
        scratch_shapes=[pltpu.VMEM(weight_shape, F32), pltpu.SemaphoreType.DMA((3,))],
        compiler_params=pltpu.CompilerParams(vmem_limit_bytes=56 << 20),
    )(input_grad, weight_rows, flux_grad)


def fused_body(
    state,
    state_cot,
    flux_cot,
    conv_weight,
    mix_weight,
    flux_weight,
    regrid_weights,
    intersection_atm,
    intersection_offset,
    wet_rows,
):
    members, lat_tiles, lon_tiles = (lax.axis_size(name) for name in ("ens", "oy", "ox"))
    rows, cells, channels = state.shape[1:]
    fields = flux_weight.shape[0]
    tiles = lat_tiles * lon_tiles
    grad_rows = (conv_weight.shape[0] + 1) * channels
    band = grad_rows // lat_tiles
    pieces = lon_tiles * members
    sub = band // pieces
    grad_scale = 1.0 / math.sqrt(members * lat_tiles * rows * lon_tiles * cells)
    entries = tiles * rows * intersection_atm.shape[2] * fields
    halo = (rows + 2, cells + 2 * EDGE, channels)
    spread = (rows + 2, cells, 3 * channels)
    small = 2 * fields
    edge_rows = -(-(rows + 2) // EDGE) * EDGE
    size = 2 * EDGE
    chunks = [(at, min(size, sub - at)) for at in range(0, sub, size)]

    def pair(count):
        return (pltpu.SemaphoreType.DMA((count,)), pltpu.SemaphoreType.DMA((count,)))

    vmem = pl.BlockSpec(memory_space=pltpu.VMEM)
    smem = pl.BlockSpec(memory_space=pltpu.SMEM)
    hbm = pl.BlockSpec(memory_space=pltpu.HBM)
    flux_flat = flux_cot[0].reshape(-1, cells)
    tables = [table.transpose(1, 2, 0) for table in (intersection_atm, intersection_offset)]
    scratch = [
        pltpu.VMEM((rows, cells, channels), BF16),
        pltpu.VMEM(flux_flat.shape, BF16),
        pltpu.VMEM(conv_weight.shape, BF16),
        pltpu.VMEM(mix_weight.shape, BF16),
        pltpu.VMEM(flux_weight.shape, BF16),
        pltpu.VMEM(regrid_weights.shape, BF16),
        pltpu.SMEM(tables[0].shape, jnp.int32),
        pltpu.SMEM(tables[1].shape, jnp.int32),
        pltpu.VMEM(halo, BF16),
        pltpu.VMEM(halo, BF16),
        pltpu.VMEM(halo, F32),
        pltpu.VMEM(spread, BF16),
        pltpu.VMEM((3 * channels, (rows + 2) * cells), BF16),
        pltpu.VMEM(spread, BF16),
        pltpu.VMEM((entries, cells), jnp.int32),
        pltpu.VMEM((entries, cells), jnp.int32),
        pltpu.VMEM((tiles, rows * fields, cells), F32),
        pltpu.VMEM((tiles, rows * fields, cells), F32),
        pltpu.VMEM((2 * rows * fields, channels), F32),
        pltpu.VMEM((lat_tiles, pieces, sub, channels), F32),
        pltpu.VMEM((lat_tiles, pieces, sub, channels), BF16),
        pltpu.VMEM((pieces, sub, channels), BF16),
        pltpu.VMEM((lon_tiles, members, sub, channels), BF16),
        pltpu.VMEM((members, lon_tiles, sub, channels), BF16),
        pltpu.VMEM((lon_tiles, sub, channels), BF16),
        pltpu.VMEM((lon_tiles, sub, channels), BF16),
        pltpu.VMEM((members, sub, channels), BF16),
        pltpu.VMEM((rows * cells, channels), F32),
        pltpu.VMEM((rows * cells, channels), F32),
        pltpu.VMEM((2, edge_rows, channels), F32),
        pltpu.VMEM((2, 3, edge_rows, channels), F32),
        pltpu.VMEM((lat_tiles, small, channels), F32),
        pltpu.VMEM((members, small, channels), F32),
        pltpu.VMEM((lon_tiles, small, channels), F32),
        pltpu.SemaphoreType.DMA((9,)),
        pair(5),
        pair(5),
        pair(tiles),
        pair(lat_tiles),
        pair(members),
        pair(lon_tiles),
        pair(len(chunks) * lat_tiles),
        pair(len(chunks) * members),
        pair(len(chunks) * lon_tiles),
        pair(len(chunks) * members),
    ]
    cost = pl.CostEstimate(
        flops=2 * rows * cells * channels * channels * 29, bytes_accessed=3 << 20, transcendentals=rows * cells * channels
    )
    outs = pl.pallas_call(
        functools.partial(fused_kernel, (members, lat_tiles, lon_tiles, grad_scale, chunks)),
        out_shape=(
            jax.ShapeDtypeStruct(state.shape, BF16),
            jax.ShapeDtypeStruct((members, sub, channels), BF16),
            jax.ShapeDtypeStruct((fields, channels), F32),
        ),
        in_specs=[hbm] * 9 + [smem],
        out_specs=(vmem, vmem, vmem),
        scratch_shapes=scratch,
        cost_estimate=cost,
        compiler_params=pltpu.CompilerParams(
            collective_id=0, has_side_effects=True, vmem_limit_bytes=56 << 20
        ),
    )(
        state[0],
        state_cot[0],
        flux_flat,
        conv_weight,
        mix_weight,
        flux_weight,
        regrid_weights,
        tables[0],
        tables[1],
        wet_rows,
    )
    return place(*outs)


def step(state, state_cot, flux_cot, conv_weight, *rest):
    members, lat_tiles, lon_tiles = (lax.axis_size(name) for name in ("ens", "oy", "ox"))
    grad_rows = (conv_weight.shape[0] + 1) * state.shape[3]
    whole_tiles = grad_rows % (lat_tiles * lon_tiles * members * EDGE) == 0
    whole_taps = grad_rows // lat_tiles % state.shape[3] == 0
    fused = lat_tiles == 2 and lon_tiles > 1 and whole_tiles and whole_taps
    return (fused_body if fused else body)(state, state_cot, flux_cot, conv_weight, *rest)


def solution(mesh):
    in_specs = (
        P("ens", "oy", "ox", None),
        P("ens", "oy", "ox", None),
        P("ens", ("oy", "ox"), None, None),
        P(),
        P(),
        P(),
        P(),
        P(),
        P(),
        P("oy", "ox"),
    )
    out_specs = (P("ens", "oy", "ox", None), P(("oy", "ox"), None), P())
    return jax.shard_map(step, mesh=mesh, in_specs=in_specs, out_specs=out_specs, check_vma=False)
```

```python
import functools
import math

import jax
import jax.numpy as jnp
from jax import lax
from jax.experimental import pallas as pl
from jax.experimental.pallas import tpu as pltpu
from jax.sharding import PartitionSpec as P

CAP = 5


def with_halo(cells, sides, width):
    for axis, dim in sides:
        count = lax.axis_size(axis)
        head = lax.slice_in_dim(cells, 0, width, axis=dim)
        tail = lax.slice_in_dim(cells, cells.shape[dim] - width, cells.shape[dim], axis=dim)
        cells = jnp.concatenate(
            [
                lax.ppermute(tail, axis, [(i, (i + 1) % count) for i in range(count)]),
                cells,
                lax.ppermute(head, axis, [((i + 1) % count, i) for i in range(count)]),
            ],
            axis=dim,
        )
    return cells


def shifted(value, axis, steps):
    count = lax.axis_size(axis)
    pairs = [(source, (source + steps) % count) for source in range(count)]
    return lax.ppermute(value, axis, pairs)


def zero_ends(padded, row_index, lat_tiles):
    top_keep = jnp.where(row_index > 0, 1.0, 0.0).astype(padded.dtype)
    bottom = jnp.where(row_index < lat_tiles - 1, 1.0, 0.0).astype(padded.dtype)
    return jnp.concatenate([padded[:1] * top_keep, padded[1:-1], padded[-1:] * bottom], axis=0)


def owner_rank(owners):
    entry_count = owners.shape[-1]
    same_owner = owners[..., :, None] == owners[..., None, :]
    earlier = jnp.arange(entry_count)[None, :] < jnp.arange(entry_count)[:, None]
    return jnp.sum(jnp.logical_and(same_owner, earlier), axis=-1)


def body(
    state,
    state_cot,
    flux_cot,
    conv_weight,
    mix_weight,
    flux_weight,
    regrid_weights,
    intersection_atm,
    intersection_offset,
    wet_rows,
):
    lat_tiles = lax.axis_size("oy")
    lon_tiles = lax.axis_size("ox")
    members = lax.axis_size("ens")
    row_index = lax.axis_index("oy")
    col_index = lax.axis_index("ox")
    tile_state = state[0]
    tile_rows, block_cells, channels = tile_state.shape
    cot_flat = state_cot[0].reshape(-1, channels)
    grad_scale = 1.0 / math.sqrt(members * lat_tiles * tile_rows * lon_tiles * block_cells)
    padded = with_halo(tile_state, (("oy", 0), ("ox", 1)), 1)
    padded = zero_ends(padded, row_index, lat_tiles)
    hidden = jnp.zeros((tile_rows * block_cells, channels), jnp.float32)
    for tap_index in range(9):
        tap_row, tap_col = (tap_index // 3, tap_index % 3)
        patch_rows = padded[tap_row : tap_row + tile_rows, tap_col : tap_col + block_cells].reshape(
            -1, channels
        )
        hidden = hidden + jnp.dot(
            patch_rows, conv_weight[tap_index], preferred_element_type=jnp.float32
        )
    activation = jax.nn.silu(hidden).astype(jnp.bfloat16)
    atm_dev = flux_cot.shape[1]
    cot_blocks = flux_cot[0]
    flux_fields = cot_blocks.shape[1]
    intersections = intersection_atm.shape[2]
    entries = tile_rows * intersections
    per_dev = (
        intersection_atm.reshape(lat_tiles, tile_rows, lon_tiles, intersections)
        .transpose(0, 2, 1, 3)
        .reshape(lat_tiles, lon_tiles, entries)
    )
    per_dev_offset = (
        intersection_offset.reshape(lat_tiles, tile_rows, lon_tiles, intersections)
        .transpose(0, 2, 1, 3)
        .reshape(lat_tiles, lon_tiles, entries)
    )
    band_rows = jnp.stack([row_index, (row_index + lat_tiles - 1) % lat_tiles])
    candidate = jnp.take(per_dev, band_rows, axis=0)
    candidate_offset = jnp.take(per_dev_offset, band_rows, axis=0)
    flat_index = row_index * lon_tiles + col_index
    candidate_owner = candidate // atm_dev
    is_mine = candidate_owner == flat_index
    slot_rank = owner_rank(candidate_owner)
    local_block = jnp.where(is_mine, candidate % atm_dev, 0)
    picked_cot = cot_blocks[local_block]
    picked_maps = regrid_weights[candidate_offset]
    products = jnp.einsum(
        "qsefa,qseoa->qsefo", picked_cot, picked_maps, preferred_element_type=jnp.float32
    )
    one_hot = jnp.logical_and(
        slot_rank[..., None] == jnp.arange(CAP)[None, None, None, :], is_mine[..., None]
    ).astype(jnp.float32)
    outbound = jnp.einsum("qsec,qsefo->qscfo", one_hot, products).astype(jnp.bfloat16)
    own_entries = per_dev[row_index, col_index]
    own_owner = own_entries // atm_dev
    own_slot = owner_rank(own_owner)
    same_in, next_in = (
        lax.all_to_all(outbound[0], "ox", split_axis=0, concat_axis=0, tiled=True),
        lax.all_to_all(outbound[1], "ox", split_axis=0, concat_axis=0, tiled=True),
    )
    next_in = shifted(next_in, "oy", -1)
    arrived = jnp.concatenate([same_in, next_in], axis=0).reshape(-1, flux_fields, block_cells)
    in_next = (own_owner // lon_tiles != row_index).astype(jnp.int32)
    slot_index = (in_next * lon_tiles + own_owner % lon_tiles) * CAP + own_slot
    values = (
        arrived[slot_index]
        .astype(jnp.float32)
        .reshape(tile_rows, intersections, flux_fields, block_cells)
    )
    wet_mask = (jnp.arange(tile_rows) < wet_rows[0, 0]).astype(jnp.float32)
    flux_cells = jnp.sum(values, axis=1) * wet_mask[:, None, None]
    act_grad = lax.dot_general(
        cot_flat, mix_weight, (((1,), (1,)), ((), ())), preferred_element_type=jnp.float32
    )
    act_grad = act_grad + jnp.einsum(
        "rfb,fc->rbc", flux_cells, flux_weight.astype(jnp.float32)
    ).reshape(-1, channels)
    gate_sig = jax.nn.sigmoid(hidden)
    hidden_grad = (act_grad * gate_sig * (1.0 + hidden * (1.0 - gate_sig))).astype(jnp.bfloat16)
    padded_grad = with_halo(
        hidden_grad.reshape(tile_rows, block_cells, channels), (("oy", 0), ("ox", 1)), 1
    )
    padded_grad = zero_ends(padded_grad, row_index, lat_tiles)
    input_grad = cot_flat.astype(jnp.float32)
    tap_grads = []
    for tap_index in range(9):
        tap_row, tap_col = (tap_index // 3, tap_index % 3)
        back_rows = padded_grad[
            2 - tap_row : 2 - tap_row + tile_rows, 2 - tap_col : 2 - tap_col + block_cells
        ].reshape(-1, channels)
        input_grad = input_grad + lax.dot_general(
            back_rows,
            conv_weight[tap_index],
            (((1,), (1,)), ((), ())),
            preferred_element_type=jnp.float32,
        )
        patch_rows = padded[tap_row : tap_row + tile_rows, tap_col : tap_col + block_cells].reshape(
            -1, channels
        )
        tap_grads.append(
            lax.dot_general(
                patch_rows,
                hidden_grad,
                (((0,), (0,)), ((), ())),
                preferred_element_type=jnp.float32,
            )
        )
    tap_grads.append(
        lax.dot_general(
            activation, cot_flat, (((0,), (0,)), ((), ())), preferred_element_type=jnp.float32
        )
    )
    weight_term = jnp.concatenate(tap_grads, axis=0) * grad_scale
    flux_term = (
        jnp.einsum(
            "rfb,rbc->fc",
            flux_cells,
            activation.reshape(tile_rows, block_cells, channels).astype(jnp.float32),
        )
        * grad_scale
    )
    weight_rows = lax.psum_scatter(weight_term, ("oy", "ox"), scatter_dimension=0, tiled=True)
    weight_out = lax.psum(weight_rows, "ens")
    flux_total = lax.psum(flux_term, ("ens", "oy", "ox"))
    input_out = input_grad.reshape(1, tile_rows, block_cells, channels).astype(jnp.bfloat16)
    return (input_out, weight_out, flux_total)


F32 = jnp.float32
BF16 = jnp.bfloat16
MESH = pl.DeviceIdType.MESH
EDGE = 16


def dot(a, b, dims=((1,), (0,))):
    return lax.dot_general(a, b, (dims, ((), ())), preferred_element_type=F32)


def remote(src, dst, send_sem, recv_sem, target):
    return pltpu.make_async_remote_copy(
        src_ref=src,
        dst_ref=dst,
        send_sem=send_sem,
        recv_sem=recv_sem,
        device_id=target,
        device_id_type=MESH,
    )


def start_all(copies):
    for copy in copies:
        copy.start()
    return copies


def halo_copies(src, src_at, padded, rows, cells, lat, lon, lon_tiles, sems):
    row0, col0 = src_at
    other = 1 - lat
    east = lax.rem(lon + 1, lon_tiles)
    west = lax.rem(lon + lon_tiles - 1, lon_tiles)
    edge_row = row0 + other * (rows - 1)
    land_row = lat * (rows + 1)
    body_rows, dst_rows = pl.ds(row0, rows), pl.ds(1, rows)
    head, last = pl.ds(col0, EDGE), pl.ds(col0 + cells - EDGE, EDGE)
    left, middle, right = pl.ds(0, EDGE), pl.ds(EDGE, cells), pl.ds(EDGE + cells, EDGE)
    plan = [
        (src.at[pl.ds(edge_row, 1), pl.ds(col0, cells)], padded.at[pl.ds(land_row, 1), middle], other, lon),
        (src.at[body_rows, last], padded.at[dst_rows, left], lat, east),
        (src.at[body_rows, head], padded.at[dst_rows, right], lat, west),
        (src.at[pl.ds(edge_row, 1), last], padded.at[pl.ds(land_row, 1), left], other, east),
        (src.at[pl.ds(edge_row, 1), head], padded.at[pl.ds(land_row, 1), right], other, west),
    ]
    send, recv = sems
    return [
        remote(a, b, send.at[n], recv.at[n], {"oy": y, "ox": x})
        for n, (a, b, y, x) in enumerate(plan)
    ]


def exchange(axis, count, me, source, target, sems, base=0):
    send, recv = sems
    copies = []
    for step in range(1, count):
        to = lax.rem(me + step, count)
        copies.append(
            remote(source(to), target(me), send.at[base + step - 1], recv.at[base + step - 1], {axis: to})
        )
    return copies


def wait_all(copies):
    for copy in copies:
        copy.wait_recv()


def shift_cells(padded, wide, columns, rows, cells, order, edges=True):
    channels = padded.shape[2]
    middle = slice(EDGE, EDGE + cells)
    for row in range(rows + 2):
        if edges:
            wide[row] = padded[row].astype(F32)
        else:
            wide[row, 0:EDGE] = jnp.zeros((EDGE, channels), F32)
            wide[row, middle] = padded[row, middle].astype(F32)
            wide[row, EDGE + cells :] = jnp.zeros((EDGE, channels), F32)
        for n, col in enumerate(order):
            here = slice(n * channels, (n + 1) * channels)
            if col == 1:
                columns[row, :, here] = padded[row, middle]
            else:
                columns[row, :, here] = wide[row, pl.ds(EDGE - 1 + col, cells), :].astype(BF16)


def turn(columns, turned, q):
    channels = columns.shape[2] // 3
    here = slice(q * channels, (q + 1) * channels)
    turned[here, :] = columns[:, :, here].reshape(-1, channels).T


def store_rows(target, first, value):
    pieces, sub = target.shape[1:3]
    done = 0
    while done < value.shape[0]:
        at = first + done
        piece, row = at // sub, at % sub
        count = min(sub - row, value.shape[0] - done)
        target[piece // pieces, piece % pieces, row : row + count, :] = value[done : done + count].astype(
            target.dtype
        )
        done += count


def fused_kernel(
    sizes,
    state_in,
    cot_in,
    flux_cot_in,
    conv_in,
    mix_in,
    flux_weight_in,
    regrid_in,
    atm_in,
    offset_in,
    wet,
    input_out,
    weight_out,
    flux_out,
    cot,
    flux_cot,
    conv,
    mix,
    flux_weight,
    regrid,
    atm,
    offset,
    padded,
    padded_grad,
    wide,
    columns,
    turned,
    grad_columns,
    entry_cell,
    entry_map,
    flux_send,
    flux_recv,
    flux_rows,
    grads,
    grads_half,
    recv_lat,
    sum_lat,
    recv_pair,
    sum_pair,
    recv_ens,
    sum_ens,
    recv_lon,
    rows_all,
    input_sum,
    hidden_sum,
    edge,
    edge_part,
    flux_lat,
    flux_ens,
    flux_lon,
    load_sems,
    state_sems,
    grad_sems,
    flux_sems,
    flux_lat_sems,
    flux_ens_sems,
    flux_lon_sems,
    lat_sems,
    ens_sems,
    lon_sems,
    out_sems,
):
    members, lat_tiles, lon_tiles, grad_scale, chunks = sizes
    ens, lat, lon = lax.axis_index("ens"), lax.axis_index("oy"), lax.axis_index("ox")
    rows, cells, channels = cot.shape
    fields = flux_weight.shape[0]
    intersections = atm.shape[1]
    maps = regrid.shape[0]
    tiles = lat_tiles * lon_tiles
    flat = lat * lon_tiles + lon
    cells_here = flux_cot.shape[0]

    barrier = pltpu.get_barrier_semaphore()
    for step in range(1, tiles):
        peer = lax.rem(flat + step, tiles)
        pl.semaphore_signal(
            barrier, inc=1, device_id={"oy": peer // lon_tiles, "ox": lax.rem(peer, lon_tiles)}, device_id_type=MESH
        )
    for step in range(1, members):
        pl.semaphore_signal(
            barrier, inc=1, device_id={"ens": lax.rem(ens + step, members)}, device_id_type=MESH
        )
    loads = [
        pltpu.make_async_copy(src, dst, load_sems.at[n])
        for n, (src, dst) in enumerate(
            [
                (atm_in, atm),
                (offset_in, offset),
                (flux_cot_in, flux_cot),
                (regrid_in, regrid),
                (cot_in, cot),
                (mix_in, mix),
                (state_in, padded.at[pl.ds(1, rows), pl.ds(EDGE, cells)]),
                (flux_weight_in, flux_weight),
                (conv_in, conv),
            ]
        )
    ]
    for load in loads:
        load.start()

    outside = lat * (rows + 1)
    padded[pl.ds(outside, 1)] = jnp.zeros((1,) + padded.shape[1:], BF16)
    padded_grad[pl.ds(outside, 1)] = jnp.zeros((1,) + padded.shape[1:], BF16)


    loads[0].wait()
    loads[1].wait()
    entry = 0
    for k in range(intersections):
        for tile in range(tiles):
            for row in range(rows):
                at = (tile % lon_tiles, k, (tile // lon_tiles) * rows + row)
                entry_cell[pl.ds(entry, fields), :] = jnp.full((fields, cells), atm[at], jnp.int32)
                entry_map[pl.ds(entry, fields), :] = jnp.full((fields, cells), offset[at], jnp.int32)
                entry += fields
    field_iota = lax.broadcasted_iota(jnp.int32, entry_cell.shape, 0) % fields
    lane = lax.broadcasted_iota(jnp.int32, entry_cell.shape, 1)
    which_cell = entry_cell[...] * fields + (field_iota - lane - flat * cells_here)
    which_map = entry_map[...]
    loads[2].wait()
    one_hot = [
        jnp.where(which_cell == part * cells, 1.0, 0.0).astype(BF16) for part in range(cells_here // cells)
    ]
    picked = dot(jnp.concatenate(one_hot, axis=1), flux_cot[...])
    loads[3].wait()
    span = tiles * rows * fields
    part_of = [slice(k * span, (k + 1) * span) for k in range(intersections)]
    share = jnp.zeros((span, cells), F32)
    for m in range(0, maps, 2):
        chosen, taken = [], []
        for n in range(m, min(m + 2, maps)):
            total = jnp.where(which_map[part_of[0]] == n, picked[part_of[0]], 0.0)
            for k in range(1, intersections):
                total = total + jnp.where(which_map[part_of[k]] == n, picked[part_of[k]], 0.0)
            chosen.append(total.astype(BF16))
            taken.append(regrid[n])
        share = share + dot(jnp.concatenate(chosen, axis=1), jnp.concatenate(taken, axis=1), ((1,), (1,)))
    flux_send[...] = share.reshape(flux_send.shape)
    flux_recv[pl.ds(flat, 1)] = flux_send[pl.ds(flat, 1)]

    pl.semaphore_wait(barrier, tiles - 1 + members - 1)
    state_copies = start_all(
        halo_copies(state_in, (0, 0), padded, rows, cells, lat, lon, lon_tiles, state_sems)
    )

    flux_copies = []
    for step in range(1, tiles):
        peer = lax.rem(flat + step, tiles)
        flux_copies.append(
            remote(
                flux_send.at[peer],
                flux_recv.at[flat],
                flux_sems[0].at[step - 1],
                flux_sems[1].at[step - 1],
                {"oy": peer // lon_tiles, "ox": lax.rem(peer, lon_tiles)},
            )
        )
    start_all(flux_copies)

    for load in loads[4:]:
        load.wait()
    flux_rows[...] = jnp.zeros(flux_rows.shape, F32)
    for n in range(2 * rows):
        flux_rows[n * fields : (n + 1) * fields, :] = flux_weight[...].astype(F32)
    cot_flat = cot[...].reshape(rows * cells, channels)
    act_grad = dot(cot_flat, mix[...], ((1,), (1,)))
    state_copies[0].wait_recv()
    shift_cells(padded, wide, columns, rows, cells, (0, 1, 2), False)
    hidden = jnp.zeros((rows * cells, channels), F32)
    for p in range(3):
        hidden = hidden + dot(
            columns[p : p + rows].reshape(rows * cells, 3 * channels),
            conv[3 * p : 3 * p + 3].reshape(3 * channels, channels),
        )
    hidden_sum[...] = hidden
    turn(columns, turned, 1)

    wait_all(state_copies[1:])
    edge[...] = jnp.zeros(edge.shape, F32)
    cell_iota = lax.broadcasted_iota(jnp.int32, (EDGE, channels), 0)
    for row in range(rows + 2):
        west = padded[row, 0:EDGE].astype(F32)[EDGE - 1 :]
        east = padded[row, EDGE + cells :].astype(F32)[:1]
        edge[0, row : row + 1] = west
        edge[1, row : row + 1] = east
        kept = columns[row, 0:EDGE, 0:channels].astype(F32)
        columns[row, 0:EDGE, 0:channels] = jnp.where(cell_iota == 0, west, kept).astype(BF16)
        kept = columns[row, cells - EDGE :, 2 * channels :].astype(F32)
        columns[row, cells - EDGE :, 2 * channels :] = jnp.where(cell_iota == EDGE - 1, east, kept).astype(BF16)
    for side in range(2):
        cells_there = edge[side].astype(BF16)
        for p in range(3):
            edge_part[side, p] = dot(cells_there, conv[3 * p + 2 * side])
        for row in range(rows):
            at = row * cells + side * (cells - 1)
            added = hidden_sum[at : at + 1]
            for p in range(3):
                added = added + edge_part[side, p, row + p : row + p + 1]
            hidden_sum[at : at + 1] = added
    hidden = hidden_sum[...]
    turn(columns, turned, 0)
    turn(columns, turned, 2)
    gate = jax.nn.sigmoid(hidden)
    activation = (hidden * gate).astype(BF16)
    slope = gate * (1.0 + hidden * (1.0 - gate))
    term = dot(activation, cot_flat, ((0,), (0,)))
    store_rows(grads, 9 * channels, term)
    store_rows(grads_half, 9 * channels, term)

    wait_all(flux_copies)
    row_iota = lax.broadcasted_iota(jnp.int32, (rows * fields, cells), 0) // fields
    flux = flux_recv[0]
    for tile in range(1, tiles):
        flux = flux + flux_recv[tile]
    flux = jnp.where(row_iota < wet[0, 0], flux, 0.0)
    flux_high = flux.astype(BF16).astype(F32)
    flux_low = flux - flux_high
    both = jnp.concatenate([flux_high, flux_low], axis=0)
    both_iota = jnp.concatenate([row_iota, row_iota], axis=0)
    heads = flux_rows[...].astype(BF16)
    masked = []
    for row in range(rows):
        mine = jnp.where(both_iota == row, both, 0.0).astype(BF16)
        masked.append(mine)
        here = slice(row * cells, (row + 1) * cells)
        extra = dot(mine, heads, ((0,), (0,)))
        padded_grad[row + 1, EDGE : EDGE + cells] = ((act_grad[here] + extra) * slope[here]).astype(BF16)
    grad_copies = start_all(
        halo_copies(padded_grad, (1, EDGE), padded_grad, rows, cells, lat, lon, lon_tiles, grad_sems)
    )

    def tap_grads(target, first, last):
        hidden_grad = padded_grad[1 : rows + 1, EDGE : EDGE + cells].reshape(rows * cells, channels)
        tap = first
        while tap < last:
            p, q = tap // 3, tap % 3
            count = min(3 - q, last - tap)
            left = turned[q * channels : (q + count) * channels, p * cells : (p + rows) * cells]
            store_rows(target, tap * channels, dot(left, hidden_grad))
            tap += count

    taps = grads.shape[1] * grads.shape[2] // channels
    for part in range(lat_tiles):

        @pl.when(lat != part)
        def _():
            tap_grads(grads_half, part * taps, min((part + 1) * taps, 9))

    lat_copies = [
        start_all(
            exchange(
                "oy",
                lat_tiles,
                lat,
                lambda to: grads_half.at[to, :, pl.ds(at, count)],
                lambda me: recv_lat.at[:, pl.ds(at, count)],
                lat_sems,
                n * lat_tiles,
            )
        )
        for n, (at, count) in enumerate(chunks)
    ]
    flux_rows[...] = dot(jnp.concatenate(masked, axis=1), activation)
    total = flux_rows[:fields, :]
    for n in range(1, 2 * rows):
        total = total + flux_rows[n * fields : (n + 1) * fields, :]
    flux_lat[pl.ds(lat, 1)] = jnp.zeros((1,) + flux_lat.shape[1:], F32)
    flux_lat[pl.ds(lat, 1), 0:fields, :] = total[None]
    flux_lat_copies = start_all(
        exchange("oy", lat_tiles, lat, lambda to: flux_lat.at[lat], lambda me: flux_lat.at[me], flux_lat_sems)
    )

    for part in range(lat_tiles):

        @pl.when(lat == part)
        def _():
            tap_grads(grads, part * taps, min((part + 1) * taps, 9))

    high, low = ens // 2, lax.rem(ens, 2)
    partners = (high * 2 + 1 - low, (1 - high) * 2 + low)
    halves = [pl.ds(0, lon_tiles // 2), pl.ds(lon_tiles // 2, lon_tiles // 2)]

    def pair_copies(n, phase):
        here = pl.ds(chunks[n][0], chunks[n][1])
        copies = []
        for half, span in enumerate(halves):
            if phase == 0:
                away = (slice(None), 1 - low) if half == 0 else (1 - high, slice(None))
                source = sum_lat.at[span, away[0], away[1], here]
                target = recv_pair.at[span, :, here]
                partner = partners[half]
            else:
                source = sum_pair.at[span, 1 - high if half == 0 else 1 - low, here]
                target = recv_ens.at[span, here]
                partner = partners[1 - half]
            sem = n * 4 + phase * 2 + half
            copies.append(remote(source, target, ens_sems[0].at[sem], ens_sems[1].at[sem], {"ens": partner}))
        return copies

    first_copies, second_copies = [], []
    for n, (at, count) in enumerate(chunks):
        wait_all(lat_copies[n])
        own = grads[pl.ds(lat, 1), :, at : at + count]
        part = (own[0] + recv_lat[:, at : at + count].astype(F32)).astype(BF16)
        sum_lat[:, :, :, at : at + count] = part.reshape(lon_tiles, 2, 2, count, channels)
        first_copies.append(start_all(pair_copies(n, 0)))
    wait_all(flux_lat_copies)
    total = flux_lat[0]
    for n in range(1, lat_tiles):
        total = total + flux_lat[n]
    flux_ens[pl.ds(ens, 1)] = total[None]
    flux_ens_copies = start_all(
        exchange("ens", members, ens, lambda to: flux_ens.at[ens], lambda me: flux_ens.at[me], flux_ens_sems)
    )

    wait_all(grad_copies)
    shift_cells(padded_grad, wide, grad_columns, rows, cells, (2, 1, 0))
    def input_part(p):
        back = grad_columns[2 - p : 2 - p + rows].reshape(rows * cells, 3 * channels)
        taps = jnp.concatenate([conv[3 * p + q] for q in range(3)], axis=1)
        before = input_sum[...] if p else cot_flat.astype(F32)
        total = before + dot(back, taps, ((1,), (1,)))
        if p < 2:
            input_sum[...] = total
        else:
            input_out[...] = total.astype(BF16).reshape(input_out.shape)

    input_part(0)
    lon_copies, out_copies = [], []

    def gather_chunk(n):
        at, count = chunks[n]
        wait_all(lon_copies[n])
        total = recv_lon[0, at : at + count].astype(F32)
        for other in range(1, lon_tiles):
            total = total + recv_lon[other, at : at + count].astype(F32)
        rows_all[pl.ds(ens, 1), at : at + count] = (total * grad_scale).astype(BF16)[None]
        out_copies.append(
            start_all(
                exchange(
                    "ens",
                    members,
                    ens,
                    lambda to: rows_all.at[ens, pl.ds(at, count)],
                    lambda me: rows_all.at[me, pl.ds(at, count)],
                    out_sems,
                    n * members,
                )
            )
        )

    def second_chunk(n):
        wait_all(first_copies[n])
        here = pl.ds(chunks[n][0], chunks[n][1])
        for half, span in enumerate(halves):
            if half == 0:
                own = sum_lat[span, :, pl.ds(low, 1), here]
            else:
                own = sum_lat[span, pl.ds(high, 1), :, here]
            came = recv_pair[span, :, here].astype(F32)
            sum_pair[span, :, here] = (own.reshape(came.shape).astype(F32) + came).astype(BF16)
        second_copies.append(start_all(pair_copies(n, 1)))

    def lon_chunk(n):
        at, count = chunks[n]
        here = pl.ds(at, count)
        wait_all(second_copies[n])
        for half, span in enumerate(halves):
            own = sum_pair[span, pl.ds(high if half == 0 else low, 1), here]
            came = recv_ens[span, here].astype(F32)
            sum_ens[span, here] = (own.reshape(came.shape).astype(F32) + came).astype(BF16)
        lon_copies.append(
            start_all(
                exchange(
                    "ox",
                    lon_tiles,
                    lon,
                    lambda to: sum_ens.at[to, here],
                    lambda me: recv_lon.at[me, here],
                    lon_sems,
                    n * lon_tiles,
                )
            )
        )
        recv_lon[pl.ds(lon, 1), here] = sum_ens[pl.ds(lon, 1), here]

    for n in range(len(chunks) + 2):
        if n < len(chunks):
            second_chunk(n)
        if 0 <= n - 1 < len(chunks):
            lon_chunk(n - 1)
        if n == 1:
            wait_all(flux_ens_copies)
            total = flux_ens[0]
            for other in range(1, members):
                total = total + flux_ens[other]
            flux_lon[pl.ds(lon, 1)] = total[None]
            flux_lon_copies = start_all(
                exchange("ox", lon_tiles, lon, lambda to: flux_lon.at[lon], lambda me: flux_lon.at[me], flux_lon_sems)
            )
        if 0 <= n - 2 < len(chunks) - 1:
            gather_chunk(n - 2)
        if n < 2:
            input_part(n + 1)
    wait_all(flux_lon_copies)
    total = flux_lon[0]
    for n in range(1, lon_tiles):
        total = total + flux_lon[n]
    flux_out[...] = total[:fields] * grad_scale
    gather_chunk(len(chunks) - 1)
    for copies in out_copies:
        wait_all(copies)
    weight_out[...] = rows_all[...]
    started = state_copies + flux_copies + grad_copies + flux_lat_copies + flux_ens_copies + flux_lon_copies
    for copies in [started] + lat_copies + first_copies + second_copies + lon_copies + out_copies:
        for copy in copies:
            copy.wait_send()


def place_kernel(input_grad, weight_rows, flux_grad, input_out, weight_out, flux_out, wide, sems):
    copies = [
        pltpu.make_async_copy(input_grad, input_out, sems.at[0]),
        pltpu.make_async_copy(flux_grad, flux_out, sems.at[1]),
        pltpu.make_async_copy(wide, weight_out, sems.at[2]),
    ]
    copies[0].start()
    copies[1].start()
    wide[...] = weight_rows[...].reshape(wide.shape).astype(F32)
    copies[2].start()
    for copy in copies:
        copy.wait()


def place(input_grad, weight_rows, flux_grad):
    channels = weight_rows.shape[2]
    weight_shape = (weight_rows.shape[0] * weight_rows.shape[1], channels)
    vmem = pl.BlockSpec(memory_space=pltpu.VMEM)
    hbm = pl.BlockSpec(memory_space=pltpu.HBM)
    return pl.pallas_call(
        place_kernel,
        out_shape=(
            jax.ShapeDtypeStruct(input_grad.shape, BF16),
            jax.ShapeDtypeStruct(weight_shape, F32),
            jax.ShapeDtypeStruct(flux_grad.shape, F32),
        ),
        in_specs=[vmem] * 3,
        out_specs=(hbm, hbm, hbm),
        scratch_shapes=[pltpu.VMEM(weight_shape, F32), pltpu.SemaphoreType.DMA((3,))],
        compiler_params=pltpu.CompilerParams(vmem_limit_bytes=56 << 20),
    )(input_grad, weight_rows, flux_grad)


def fused_body(
    state,
    state_cot,
    flux_cot,
    conv_weight,
    mix_weight,
    flux_weight,
    regrid_weights,
    intersection_atm,
    intersection_offset,
    wet_rows,
):
    members, lat_tiles, lon_tiles = (lax.axis_size(name) for name in ("ens", "oy", "ox"))
    rows, cells, channels = state.shape[1:]
    fields = flux_weight.shape[0]
    tiles = lat_tiles * lon_tiles
    grad_rows = (conv_weight.shape[0] + 1) * channels
    band = grad_rows // lat_tiles
    pieces = lon_tiles * members
    sub = band // pieces
    grad_scale = 1.0 / math.sqrt(members * lat_tiles * rows * lon_tiles * cells)
    entries = tiles * rows * intersection_atm.shape[2] * fields
    halo = (rows + 2, cells + 2 * EDGE, channels)
    spread = (rows + 2, cells, 3 * channels)
    small = 2 * fields
    edge_rows = -(-(rows + 2) // EDGE) * EDGE
    size = 2 * EDGE
    chunks = [(at, min(size, sub - at)) for at in range(0, sub, size)]

    def pair(count):
        return (pltpu.SemaphoreType.DMA((count,)), pltpu.SemaphoreType.DMA((count,)))

    vmem = pl.BlockSpec(memory_space=pltpu.VMEM)
    smem = pl.BlockSpec(memory_space=pltpu.SMEM)
    hbm = pl.BlockSpec(memory_space=pltpu.HBM)
    flux_flat = flux_cot[0].reshape(-1, cells)
    tables = [table.transpose(1, 2, 0) for table in (intersection_atm, intersection_offset)]
    scratch = [
        pltpu.VMEM((rows, cells, channels), BF16),
        pltpu.VMEM(flux_flat.shape, BF16),
        pltpu.VMEM(conv_weight.shape, BF16),
        pltpu.VMEM(mix_weight.shape, BF16),
        pltpu.VMEM(flux_weight.shape, BF16),
        pltpu.VMEM(regrid_weights.shape, BF16),
        pltpu.SMEM(tables[0].shape, jnp.int32),
        pltpu.SMEM(tables[1].shape, jnp.int32),
        pltpu.VMEM(halo, BF16),
        pltpu.VMEM(halo, BF16),
        pltpu.VMEM(halo, F32),
        pltpu.VMEM(spread, BF16),
        pltpu.VMEM((3 * channels, (rows + 2) * cells), BF16),
        pltpu.VMEM(spread, BF16),
        pltpu.VMEM((entries, cells), jnp.int32),
        pltpu.VMEM((entries, cells), jnp.int32),
        pltpu.VMEM((tiles, rows * fields, cells), F32),
        pltpu.VMEM((tiles, rows * fields, cells), F32),
        pltpu.VMEM((2 * rows * fields, channels), F32),
        pltpu.VMEM((lat_tiles, pieces, sub, channels), F32),
        pltpu.VMEM((lat_tiles, pieces, sub, channels), BF16),
        pltpu.VMEM((pieces, sub, channels), BF16),
        pltpu.VMEM((lon_tiles, 2, 2, sub, channels), BF16),
        pltpu.VMEM((lon_tiles, 2, sub, channels), BF16),
        pltpu.VMEM((lon_tiles, 2, sub, channels), BF16),
        pltpu.VMEM((lon_tiles, sub, channels), BF16),
        pltpu.VMEM((lon_tiles, sub, channels), BF16),
        pltpu.VMEM((lon_tiles, sub, channels), BF16),
        pltpu.VMEM((members, sub, channels), BF16),
        pltpu.VMEM((rows * cells, channels), F32),
        pltpu.VMEM((rows * cells, channels), F32),
        pltpu.VMEM((2, edge_rows, channels), F32),
        pltpu.VMEM((2, 3, edge_rows, channels), F32),
        pltpu.VMEM((lat_tiles, small, channels), F32),
        pltpu.VMEM((members, small, channels), F32),
        pltpu.VMEM((lon_tiles, small, channels), F32),
        pltpu.SemaphoreType.DMA((9,)),
        pair(5),
        pair(5),
        pair(tiles),
        pair(lat_tiles),
        pair(members),
        pair(lon_tiles),
        pair(len(chunks) * lat_tiles),
        pair(len(chunks) * members),
        pair(len(chunks) * lon_tiles),
        pair(len(chunks) * members),
    ]
    cost = pl.CostEstimate(
        flops=2 * rows * cells * channels * channels * 29, bytes_accessed=3 << 20, transcendentals=rows * cells * channels
    )
    outs = pl.pallas_call(
        functools.partial(fused_kernel, (members, lat_tiles, lon_tiles, grad_scale, chunks)),
        out_shape=(
            jax.ShapeDtypeStruct(state.shape, BF16),
            jax.ShapeDtypeStruct((members, sub, channels), BF16),
            jax.ShapeDtypeStruct((fields, channels), F32),
        ),
        in_specs=[hbm] * 9 + [smem],
        out_specs=(vmem, vmem, vmem),
        scratch_shapes=scratch,
        cost_estimate=cost,
        compiler_params=pltpu.CompilerParams(
            collective_id=0, has_side_effects=True, vmem_limit_bytes=56 << 20
        ),
    )(
        state[0],
        state_cot[0],
        flux_flat,
        conv_weight,
        mix_weight,
        flux_weight,
        regrid_weights,
        tables[0],
        tables[1],
        wet_rows,
    )
    return place(*outs)


def step(state, state_cot, flux_cot, conv_weight, *rest):
    members, lat_tiles, lon_tiles = (lax.axis_size(name) for name in ("ens", "oy", "ox"))
    grad_rows = (conv_weight.shape[0] + 1) * state.shape[3]
    whole_tiles = grad_rows % (lat_tiles * lon_tiles * members * EDGE) == 0
    whole_taps = grad_rows // lat_tiles % state.shape[3] == 0
    fused = lat_tiles == 2 and members == 4 and lon_tiles % 2 == 0 and whole_tiles and whole_taps
    return (fused_body if fused else body)(state, state_cot, flux_cot, conv_weight, *rest)


def solution(mesh):
    in_specs = (
        P("ens", "oy", "ox", None),
        P("ens", "oy", "ox", None),
        P("ens", ("oy", "ox"), None, None),
        P(),
        P(),
        P(),
        P(),
        P(),
        P(),
        P("oy", "ox"),
    )
    out_specs = (P("ens", "oy", "ox", None), P(("oy", "ox"), None), P())
    return jax.shard_map(step, mesh=mesh, in_specs=in_specs, out_specs=out_specs, check_vma=False)
```

```python
import functools
import math

import jax
import jax.numpy as jnp
from jax import lax
from jax.experimental import pallas as pl
from jax.experimental.pallas import tpu as pltpu
from jax.sharding import PartitionSpec as P

CAP = 5


def with_halo(cells, sides, width):
    for axis, dim in sides:
        count = lax.axis_size(axis)
        head = lax.slice_in_dim(cells, 0, width, axis=dim)
        tail = lax.slice_in_dim(cells, cells.shape[dim] - width, cells.shape[dim], axis=dim)
        cells = jnp.concatenate(
            [
                lax.ppermute(tail, axis, [(i, (i + 1) % count) for i in range(count)]),
                cells,
                lax.ppermute(head, axis, [((i + 1) % count, i) for i in range(count)]),
            ],
            axis=dim,
        )
    return cells


def shifted(value, axis, steps):
    count = lax.axis_size(axis)
    pairs = [(source, (source + steps) % count) for source in range(count)]
    return lax.ppermute(value, axis, pairs)


def zero_ends(padded, row_index, lat_tiles):
    top_keep = jnp.where(row_index > 0, 1.0, 0.0).astype(padded.dtype)
    bottom = jnp.where(row_index < lat_tiles - 1, 1.0, 0.0).astype(padded.dtype)
    return jnp.concatenate([padded[:1] * top_keep, padded[1:-1], padded[-1:] * bottom], axis=0)


def owner_rank(owners):
    entry_count = owners.shape[-1]
    same_owner = owners[..., :, None] == owners[..., None, :]
    earlier = jnp.arange(entry_count)[None, :] < jnp.arange(entry_count)[:, None]
    return jnp.sum(jnp.logical_and(same_owner, earlier), axis=-1)


def body(
    state,
    state_cot,
    flux_cot,
    conv_weight,
    mix_weight,
    flux_weight,
    regrid_weights,
    intersection_atm,
    intersection_offset,
    wet_rows,
):
    lat_tiles = lax.axis_size("oy")
    lon_tiles = lax.axis_size("ox")
    members = lax.axis_size("ens")
    row_index = lax.axis_index("oy")
    col_index = lax.axis_index("ox")
    tile_state = state[0]
    tile_rows, block_cells, channels = tile_state.shape
    cot_flat = state_cot[0].reshape(-1, channels)
    grad_scale = 1.0 / math.sqrt(members * lat_tiles * tile_rows * lon_tiles * block_cells)
    padded = with_halo(tile_state, (("oy", 0), ("ox", 1)), 1)
    padded = zero_ends(padded, row_index, lat_tiles)
    hidden = jnp.zeros((tile_rows * block_cells, channels), jnp.float32)
    for tap_index in range(9):
        tap_row, tap_col = (tap_index // 3, tap_index % 3)
        patch_rows = padded[tap_row : tap_row + tile_rows, tap_col : tap_col + block_cells].reshape(
            -1, channels
        )
        hidden = hidden + jnp.dot(
            patch_rows, conv_weight[tap_index], preferred_element_type=jnp.float32
        )
    activation = jax.nn.silu(hidden).astype(jnp.bfloat16)
    atm_dev = flux_cot.shape[1]
    cot_blocks = flux_cot[0]
    flux_fields = cot_blocks.shape[1]
    intersections = intersection_atm.shape[2]
    entries = tile_rows * intersections
    per_dev = (
        intersection_atm.reshape(lat_tiles, tile_rows, lon_tiles, intersections)
        .transpose(0, 2, 1, 3)
        .reshape(lat_tiles, lon_tiles, entries)
    )
    per_dev_offset = (
        intersection_offset.reshape(lat_tiles, tile_rows, lon_tiles, intersections)
        .transpose(0, 2, 1, 3)
        .reshape(lat_tiles, lon_tiles, entries)
    )
    band_rows = jnp.stack([row_index, (row_index + lat_tiles - 1) % lat_tiles])
    candidate = jnp.take(per_dev, band_rows, axis=0)
    candidate_offset = jnp.take(per_dev_offset, band_rows, axis=0)
    flat_index = row_index * lon_tiles + col_index
    candidate_owner = candidate // atm_dev
    is_mine = candidate_owner == flat_index
    slot_rank = owner_rank(candidate_owner)
    local_block = jnp.where(is_mine, candidate % atm_dev, 0)
    picked_cot = cot_blocks[local_block]
    picked_maps = regrid_weights[candidate_offset]
    products = jnp.einsum(
        "qsefa,qseoa->qsefo", picked_cot, picked_maps, preferred_element_type=jnp.float32
    )
    one_hot = jnp.logical_and(
        slot_rank[..., None] == jnp.arange(CAP)[None, None, None, :], is_mine[..., None]
    ).astype(jnp.float32)
    outbound = jnp.einsum("qsec,qsefo->qscfo", one_hot, products).astype(jnp.bfloat16)
    own_entries = per_dev[row_index, col_index]
    own_owner = own_entries // atm_dev
    own_slot = owner_rank(own_owner)
    same_in, next_in = (
        lax.all_to_all(outbound[0], "ox", split_axis=0, concat_axis=0, tiled=True),
        lax.all_to_all(outbound[1], "ox", split_axis=0, concat_axis=0, tiled=True),
    )
    next_in = shifted(next_in, "oy", -1)
    arrived = jnp.concatenate([same_in, next_in], axis=0).reshape(-1, flux_fields, block_cells)
    in_next = (own_owner // lon_tiles != row_index).astype(jnp.int32)
    slot_index = (in_next * lon_tiles + own_owner % lon_tiles) * CAP + own_slot
    values = (
        arrived[slot_index]
        .astype(jnp.float32)
        .reshape(tile_rows, intersections, flux_fields, block_cells)
    )
    wet_mask = (jnp.arange(tile_rows) < wet_rows[0, 0]).astype(jnp.float32)
    flux_cells = jnp.sum(values, axis=1) * wet_mask[:, None, None]
    act_grad = lax.dot_general(
        cot_flat, mix_weight, (((1,), (1,)), ((), ())), preferred_element_type=jnp.float32
    )
    act_grad = act_grad + jnp.einsum(
        "rfb,fc->rbc", flux_cells, flux_weight.astype(jnp.float32)
    ).reshape(-1, channels)
    gate_sig = jax.nn.sigmoid(hidden)
    hidden_grad = (act_grad * gate_sig * (1.0 + hidden * (1.0 - gate_sig))).astype(jnp.bfloat16)
    padded_grad = with_halo(
        hidden_grad.reshape(tile_rows, block_cells, channels), (("oy", 0), ("ox", 1)), 1
    )
    padded_grad = zero_ends(padded_grad, row_index, lat_tiles)
    input_grad = cot_flat.astype(jnp.float32)
    tap_grads = []
    for tap_index in range(9):
        tap_row, tap_col = (tap_index // 3, tap_index % 3)
        back_rows = padded_grad[
            2 - tap_row : 2 - tap_row + tile_rows, 2 - tap_col : 2 - tap_col + block_cells
        ].reshape(-1, channels)
        input_grad = input_grad + lax.dot_general(
            back_rows,
            conv_weight[tap_index],
            (((1,), (1,)), ((), ())),
            preferred_element_type=jnp.float32,
        )
        patch_rows = padded[tap_row : tap_row + tile_rows, tap_col : tap_col + block_cells].reshape(
            -1, channels
        )
        tap_grads.append(
            lax.dot_general(
                patch_rows,
                hidden_grad,
                (((0,), (0,)), ((), ())),
                preferred_element_type=jnp.float32,
            )
        )
    tap_grads.append(
        lax.dot_general(
            activation, cot_flat, (((0,), (0,)), ((), ())), preferred_element_type=jnp.float32
        )
    )
    weight_term = jnp.concatenate(tap_grads, axis=0) * grad_scale
    flux_term = (
        jnp.einsum(
            "rfb,rbc->fc",
            flux_cells,
            activation.reshape(tile_rows, block_cells, channels).astype(jnp.float32),
        )
        * grad_scale
    )
    weight_rows = lax.psum_scatter(weight_term, ("oy", "ox"), scatter_dimension=0, tiled=True)
    weight_out = lax.psum(weight_rows, "ens")
    flux_total = lax.psum(flux_term, ("ens", "oy", "ox"))
    input_out = input_grad.reshape(1, tile_rows, block_cells, channels).astype(jnp.bfloat16)
    return (input_out, weight_out, flux_total)


F32 = jnp.float32
BF16 = jnp.bfloat16
MESH = pl.DeviceIdType.MESH
EDGE = 16


def dot(a, b, dims=((1,), (0,))):
    return lax.dot_general(a, b, (dims, ((), ())), preferred_element_type=F32)


def remote(src, dst, send_sem, recv_sem, target):
    return pltpu.make_async_remote_copy(
        src_ref=src,
        dst_ref=dst,
        send_sem=send_sem,
        recv_sem=recv_sem,
        device_id=target,
        device_id_type=MESH,
    )


def start_all(copies):
    for copy in copies:
        copy.start()
    return copies


def halo_copies(src, src_at, padded, rows, cells, lat, lon, lon_tiles, sems):
    row0, col0 = src_at
    other = 1 - lat
    east = lax.rem(lon + 1, lon_tiles)
    west = lax.rem(lon + lon_tiles - 1, lon_tiles)
    edge_row = row0 + other * (rows - 1)
    land_row = lat * (rows + 1)
    body_rows, dst_rows = pl.ds(row0, rows), pl.ds(1, rows)
    head, last = pl.ds(col0, EDGE), pl.ds(col0 + cells - EDGE, EDGE)
    left, middle, right = pl.ds(0, EDGE), pl.ds(EDGE, cells), pl.ds(EDGE + cells, EDGE)
    plan = [
        (src.at[pl.ds(edge_row, 1), pl.ds(col0, cells)], padded.at[pl.ds(land_row, 1), middle], other, lon),
        (src.at[body_rows, last], padded.at[dst_rows, left], lat, east),
        (src.at[body_rows, head], padded.at[dst_rows, right], lat, west),
        (src.at[pl.ds(edge_row, 1), last], padded.at[pl.ds(land_row, 1), left], other, east),
        (src.at[pl.ds(edge_row, 1), head], padded.at[pl.ds(land_row, 1), right], other, west),
    ]
    send, recv = sems
    return [
        remote(a, b, send.at[n], recv.at[n], {"oy": y, "ox": x})
        for n, (a, b, y, x) in enumerate(plan)
    ]


def exchange(axis, count, me, source, target, sems, base=0):
    send, recv = sems
    copies = []
    for step in range(1, count):
        to = lax.rem(me + step, count)
        copies.append(
            remote(source(to), target(me), send.at[base + step - 1], recv.at[base + step - 1], {axis: to})
        )
    return copies


def wait_all(copies):
    for copy in copies:
        copy.wait_recv()


def shift_cells(padded, wide, columns, rows, cells, order, edges=True):
    channels = padded.shape[2]
    middle = slice(EDGE, EDGE + cells)
    for row in range(rows + 2):
        if edges:
            wide[row] = padded[row].astype(F32)
        else:
            wide[row, 0:EDGE] = jnp.zeros((EDGE, channels), F32)
            wide[row, middle] = padded[row, middle].astype(F32)
            wide[row, EDGE + cells :] = jnp.zeros((EDGE, channels), F32)
        for n, col in enumerate(order):
            here = slice(n * channels, (n + 1) * channels)
            if col == 1:
                columns[row, :, here] = padded[row, middle]
            else:
                columns[row, :, here] = wide[row, pl.ds(EDGE - 1 + col, cells), :].astype(BF16)


def turn(columns, turned, q):
    channels = columns.shape[2] // 3
    here = slice(q * channels, (q + 1) * channels)
    turned[here, :] = columns[:, :, here].reshape(-1, channels).T


def store_rows(target, first, value):
    pieces, sub = target.shape[1:3]
    done = 0
    while done < value.shape[0]:
        at = first + done
        piece, row = at // sub, at % sub
        count = min(sub - row, value.shape[0] - done)
        target[piece // pieces, piece % pieces, row : row + count, :] = value[done : done + count].astype(
            target.dtype
        )
        done += count


def fused_kernel(
    sizes,
    state_in,
    cot_in,
    flux_cot_in,
    conv_in,
    mix_in,
    flux_weight_in,
    regrid_in,
    atm_in,
    offset_in,
    wet,
    input_out,
    weight_out,
    flux_out,
    cot,
    flux_cot,
    conv,
    mix,
    flux_weight,
    regrid,
    atm,
    offset,
    padded,
    padded_grad,
    wide,
    columns,
    turned,
    grad_columns,
    entry_cell,
    entry_map,
    flux_send,
    flux_recv,
    flux_rows,
    grads,
    grads_half,
    recv_lat,
    sum_lat,
    recv_ens,
    sum_ens,
    recv_lon,
    rows_all,
    input_sum,
    hidden_sum,
    edge,
    edge_part,
    flux_lat,
    flux_ens,
    flux_lon,
    load_sems,
    state_sems,
    grad_sems,
    flux_sems,
    flux_lat_sems,
    flux_ens_sems,
    flux_lon_sems,
    lat_sems,
    ens_sems,
    lon_sems,
    out_sems,
):
    members, lat_tiles, lon_tiles, grad_scale, chunks = sizes
    ens, lat, lon = lax.axis_index("ens"), lax.axis_index("oy"), lax.axis_index("ox")
    rows, cells, channels = cot.shape
    fields = flux_weight.shape[0]
    intersections = atm.shape[1]
    maps = regrid.shape[0]
    tiles = lat_tiles * lon_tiles
    flat = lat * lon_tiles + lon
    cells_here = flux_cot.shape[0]

    barrier = pltpu.get_barrier_semaphore()
    for step in range(1, tiles):
        peer = lax.rem(flat + step, tiles)
        pl.semaphore_signal(
            barrier, inc=1, device_id={"oy": peer // lon_tiles, "ox": lax.rem(peer, lon_tiles)}, device_id_type=MESH
        )
    for step in range(1, members):
        pl.semaphore_signal(
            barrier, inc=1, device_id={"ens": lax.rem(ens + step, members)}, device_id_type=MESH
        )
    loads = [
        pltpu.make_async_copy(src, dst, load_sems.at[n])
        for n, (src, dst) in enumerate(
            [
                (atm_in, atm),
                (offset_in, offset),
                (flux_cot_in, flux_cot),
                (regrid_in, regrid),
                (cot_in, cot),
                (mix_in, mix),
                (state_in, padded.at[pl.ds(1, rows), pl.ds(EDGE, cells)]),
                (flux_weight_in, flux_weight),
                (conv_in, conv),
            ]
        )
    ]
    for load in loads:
        load.start()

    outside = lat * (rows + 1)
    padded[pl.ds(outside, 1)] = jnp.zeros((1,) + padded.shape[1:], BF16)
    padded_grad[pl.ds(outside, 1)] = jnp.zeros((1,) + padded.shape[1:], BF16)


    loads[0].wait()
    loads[1].wait()
    entry = 0
    for k in range(intersections):
        for tile in range(tiles):
            for row in range(rows):
                at = (tile % lon_tiles, k, (tile // lon_tiles) * rows + row)
                entry_cell[pl.ds(entry, fields), :] = jnp.full((fields, cells), atm[at], jnp.int32)
                entry_map[pl.ds(entry, fields), :] = jnp.full((fields, cells), offset[at], jnp.int32)
                entry += fields
    field_iota = lax.broadcasted_iota(jnp.int32, entry_cell.shape, 0) % fields
    lane = lax.broadcasted_iota(jnp.int32, entry_cell.shape, 1)
    which_cell = entry_cell[...] * fields + (field_iota - lane - flat * cells_here)
    which_map = entry_map[...]
    loads[2].wait()
    one_hot = [
        jnp.where(which_cell == part * cells, 1.0, 0.0).astype(BF16) for part in range(cells_here // cells)
    ]
    picked = dot(jnp.concatenate(one_hot, axis=1), flux_cot[...])
    loads[3].wait()
    span = tiles * rows * fields
    part_of = [slice(k * span, (k + 1) * span) for k in range(intersections)]
    share = jnp.zeros((span, cells), F32)
    for m in range(0, maps, 2):
        chosen, taken = [], []
        for n in range(m, min(m + 2, maps)):
            total = jnp.where(which_map[part_of[0]] == n, picked[part_of[0]], 0.0)
            for k in range(1, intersections):
                total = total + jnp.where(which_map[part_of[k]] == n, picked[part_of[k]], 0.0)
            chosen.append(total.astype(BF16))
            taken.append(regrid[n])
        share = share + dot(jnp.concatenate(chosen, axis=1), jnp.concatenate(taken, axis=1), ((1,), (1,)))
    flux_send[...] = share.reshape(flux_send.shape)
    flux_recv[pl.ds(flat, 1)] = flux_send[pl.ds(flat, 1)]

    pl.semaphore_wait(barrier, tiles - 1 + members - 1)
    state_copies = start_all(
        halo_copies(state_in, (0, 0), padded, rows, cells, lat, lon, lon_tiles, state_sems)
    )

    flux_copies = []
    for step in range(1, tiles):
        peer = lax.rem(flat + step, tiles)
        flux_copies.append(
            remote(
                flux_send.at[peer],
                flux_recv.at[flat],
                flux_sems[0].at[step - 1],
                flux_sems[1].at[step - 1],
                {"oy": peer // lon_tiles, "ox": lax.rem(peer, lon_tiles)},
            )
        )
    start_all(flux_copies)

    for load in loads[4:]:
        load.wait()
    flux_rows[...] = jnp.zeros(flux_rows.shape, F32)
    for n in range(2 * rows):
        flux_rows[n * fields : (n + 1) * fields, :] = flux_weight[...].astype(F32)
    cot_flat = cot[...].reshape(rows * cells, channels)
    act_grad = dot(cot_flat, mix[...], ((1,), (1,)))
    state_copies[0].wait_recv()
    shift_cells(padded, wide, columns, rows, cells, (0, 1, 2), False)
    hidden = jnp.zeros((rows * cells, channels), F32)
    for p in range(3):
        hidden = hidden + dot(
            columns[p : p + rows].reshape(rows * cells, 3 * channels),
            conv[3 * p : 3 * p + 3].reshape(3 * channels, channels),
        )
    hidden_sum[...] = hidden
    turn(columns, turned, 1)

    wait_all(state_copies[1:])
    edge[...] = jnp.zeros(edge.shape, F32)
    cell_iota = lax.broadcasted_iota(jnp.int32, (EDGE, channels), 0)
    for row in range(rows + 2):
        west = padded[row, 0:EDGE].astype(F32)[EDGE - 1 :]
        east = padded[row, EDGE + cells :].astype(F32)[:1]
        edge[0, row : row + 1] = west
        edge[1, row : row + 1] = east
        kept = columns[row, 0:EDGE, 0:channels].astype(F32)
        columns[row, 0:EDGE, 0:channels] = jnp.where(cell_iota == 0, west, kept).astype(BF16)
        kept = columns[row, cells - EDGE :, 2 * channels :].astype(F32)
        columns[row, cells - EDGE :, 2 * channels :] = jnp.where(cell_iota == EDGE - 1, east, kept).astype(BF16)
    for side in range(2):
        cells_there = edge[side].astype(BF16)
        for p in range(3):
            edge_part[side, p] = dot(cells_there, conv[3 * p + 2 * side])
        for row in range(rows):
            at = row * cells + side * (cells - 1)
            added = hidden_sum[at : at + 1]
            for p in range(3):
                added = added + edge_part[side, p, row + p : row + p + 1]
            hidden_sum[at : at + 1] = added
    hidden = hidden_sum[...]
    turn(columns, turned, 0)
    turn(columns, turned, 2)
    gate = jax.nn.sigmoid(hidden)
    activation = (hidden * gate).astype(BF16)
    slope = gate * (1.0 + hidden * (1.0 - gate))
    term = dot(activation, cot_flat, ((0,), (0,)))
    store_rows(grads, 9 * channels, term)
    store_rows(grads_half, 9 * channels, term)

    wait_all(flux_copies)
    row_iota = lax.broadcasted_iota(jnp.int32, (rows * fields, cells), 0) // fields
    flux = flux_recv[0]
    for tile in range(1, tiles):
        flux = flux + flux_recv[tile]
    flux = jnp.where(row_iota < wet[0, 0], flux, 0.0)
    flux_high = flux.astype(BF16).astype(F32)
    flux_low = flux - flux_high
    both = jnp.concatenate([flux_high, flux_low], axis=0)
    both_iota = jnp.concatenate([row_iota, row_iota], axis=0)
    heads = flux_rows[...].astype(BF16)
    masked = []
    for row in range(rows):
        mine = jnp.where(both_iota == row, both, 0.0).astype(BF16)
        masked.append(mine)
        here = slice(row * cells, (row + 1) * cells)
        extra = dot(mine, heads, ((0,), (0,)))
        padded_grad[row + 1, EDGE : EDGE + cells] = ((act_grad[here] + extra) * slope[here]).astype(BF16)
    grad_copies = start_all(
        halo_copies(padded_grad, (1, EDGE), padded_grad, rows, cells, lat, lon, lon_tiles, grad_sems)
    )

    def tap_grads(target, first, last):
        hidden_grad = padded_grad[1 : rows + 1, EDGE : EDGE + cells].reshape(rows * cells, channels)
        tap = first
        while tap < last:
            p, q = tap // 3, tap % 3
            count = min(3 - q, last - tap)
            left = turned[q * channels : (q + count) * channels, p * cells : (p + rows) * cells]
            store_rows(target, tap * channels, dot(left, hidden_grad))
            tap += count

    taps = grads.shape[1] * grads.shape[2] // channels
    for part in range(lat_tiles):

        @pl.when(lat != part)
        def _():
            tap_grads(grads_half, part * taps, min((part + 1) * taps, 9))

    lat_copies = [
        start_all(
            exchange(
                "oy",
                lat_tiles,
                lat,
                lambda to: grads_half.at[to, :, pl.ds(at, count)],
                lambda me: recv_lat.at[:, pl.ds(at, count)],
                lat_sems,
                n * lat_tiles,
            )
        )
        for n, (at, count) in enumerate(chunks)
    ]
    flux_rows[...] = dot(jnp.concatenate(masked, axis=1), activation)
    total = flux_rows[:fields, :]
    for n in range(1, 2 * rows):
        total = total + flux_rows[n * fields : (n + 1) * fields, :]
    flux_lat[pl.ds(lat, 1)] = jnp.zeros((1,) + flux_lat.shape[1:], F32)
    flux_lat[pl.ds(lat, 1), 0:fields, :] = total[None]
    flux_lat_copies = start_all(
        exchange("oy", lat_tiles, lat, lambda to: flux_lat.at[lat], lambda me: flux_lat.at[me], flux_lat_sems)
    )

    for part in range(lat_tiles):

        @pl.when(lat == part)
        def _():
            tap_grads(grads, part * taps, min((part + 1) * taps, 9))

    ens_copies = []
    for n, (at, count) in enumerate(chunks):
        wait_all(lat_copies[n])
        own = grads[pl.ds(lat, 1), :, at : at + count]
        part = (own[0] + recv_lat[:, at : at + count].astype(F32)).astype(BF16)
        sum_lat[:, :, at : at + count] = part.reshape(lon_tiles, members, count, channels)
        ens_copies.append(
            start_all(
                exchange(
                    "ens",
                    members,
                    ens,
                    lambda to: sum_lat.at[:, to, pl.ds(at, count)],
                    lambda me: recv_ens.at[me, :, pl.ds(at, count)],
                    ens_sems,
                    n * members,
                )
            )
        )
    recv_ens[pl.ds(ens, 1)] = sum_lat[:, pl.ds(ens, 1)].reshape((1,) + recv_ens.shape[1:])
    wait_all(flux_lat_copies)
    total = flux_lat[0]
    for n in range(1, lat_tiles):
        total = total + flux_lat[n]
    flux_ens[pl.ds(ens, 1)] = total[None]
    flux_ens_copies = start_all(
        exchange("ens", members, ens, lambda to: flux_ens.at[ens], lambda me: flux_ens.at[me], flux_ens_sems)
    )

    wait_all(grad_copies)
    shift_cells(padded_grad, wide, grad_columns, rows, cells, (2, 1, 0))
    def input_part(p):
        back = grad_columns[2 - p : 2 - p + rows].reshape(rows * cells, 3 * channels)
        taps = jnp.concatenate([conv[3 * p + q] for q in range(3)], axis=1)
        before = input_sum[...] if p else cot_flat.astype(F32)
        total = before + dot(back, taps, ((1,), (1,)))
        if p < 2:
            input_sum[...] = total
        else:
            input_out[...] = total.astype(BF16).reshape(input_out.shape)

    input_part(0)
    lon_copies, out_copies = [], []

    def gather_chunk(n):
        at, count = chunks[n]
        wait_all(lon_copies[n])
        total = recv_lon[0, at : at + count].astype(F32)
        for other in range(1, lon_tiles):
            total = total + recv_lon[other, at : at + count].astype(F32)
        rows_all[pl.ds(ens, 1), at : at + count] = (total * grad_scale).astype(BF16)[None]
        out_copies.append(
            start_all(
                exchange(
                    "ens",
                    members,
                    ens,
                    lambda to: rows_all.at[ens, pl.ds(at, count)],
                    lambda me: rows_all.at[me, pl.ds(at, count)],
                    out_sems,
                    n * members,
                )
            )
        )

    for n, (at, count) in enumerate(chunks):
        wait_all(ens_copies[n])
        total = recv_ens[0, :, at : at + count].astype(F32)
        for other in range(1, members):
            total = total + recv_ens[other, :, at : at + count].astype(F32)
        sum_ens[:, at : at + count] = total.astype(BF16)
        lon_copies.append(
            start_all(
                exchange(
                    "ox",
                    lon_tiles,
                    lon,
                    lambda to: sum_ens.at[to, pl.ds(at, count)],
                    lambda me: recv_lon.at[me, pl.ds(at, count)],
                    lon_sems,
                    n * lon_tiles,
                )
            )
        )
        recv_lon[pl.ds(lon, 1), at : at + count] = sum_ens[pl.ds(lon, 1), at : at + count]
        if n == 0:
            wait_all(flux_ens_copies)
            total = flux_ens[0]
            for other in range(1, members):
                total = total + flux_ens[other]
            flux_lon[pl.ds(lon, 1)] = total[None]
            flux_lon_copies = start_all(
                exchange("ox", lon_tiles, lon, lambda to: flux_lon.at[lon], lambda me: flux_lon.at[me], flux_lon_sems)
            )
        else:
            gather_chunk(n - 1)
        if n < 2:
            input_part(n + 1)
    for p in range(len(chunks) + 1, 3):
        input_part(p)
    wait_all(flux_lon_copies)
    total = flux_lon[0]
    for n in range(1, lon_tiles):
        total = total + flux_lon[n]
    flux_out[...] = total[:fields] * grad_scale
    gather_chunk(len(chunks) - 1)
    for copies in out_copies:
        wait_all(copies)
    weight_out[...] = rows_all[...]
    started = state_copies + flux_copies + grad_copies + flux_lat_copies + flux_ens_copies + flux_lon_copies
    for copies in [started] + lat_copies + ens_copies + lon_copies + out_copies:
        for copy in copies:
            copy.wait_send()


def place_kernel(input_grad, weight_rows, flux_grad, input_out, weight_out, flux_out, wide, sems):
    copies = [
        pltpu.make_async_copy(input_grad, input_out, sems.at[0]),
        pltpu.make_async_copy(flux_grad, flux_out, sems.at[1]),
        pltpu.make_async_copy(wide, weight_out, sems.at[2]),
    ]
    copies[0].start()
    copies[1].start()
    wide[...] = weight_rows[...].reshape(wide.shape).astype(F32)
    copies[2].start()
    for copy in copies:
        copy.wait()


def place(input_grad, weight_rows, flux_grad):
    channels = weight_rows.shape[2]
    weight_shape = (weight_rows.shape[0] * weight_rows.shape[1], channels)
    vmem = pl.BlockSpec(memory_space=pltpu.VMEM)
    hbm = pl.BlockSpec(memory_space=pltpu.HBM)
    return pl.pallas_call(
        place_kernel,
        out_shape=(
            jax.ShapeDtypeStruct(input_grad.shape, BF16),
            jax.ShapeDtypeStruct(weight_shape, F32),
            jax.ShapeDtypeStruct(flux_grad.shape, F32),
        ),
        in_specs=[vmem] * 3,
        out_specs=(hbm, hbm, hbm),
        scratch_shapes=[pltpu.VMEM(weight_shape, F32), pltpu.SemaphoreType.DMA((3,))],
        compiler_params=pltpu.CompilerParams(vmem_limit_bytes=56 << 20),
    )(input_grad, weight_rows, flux_grad)


def fused_body(
    state,
    state_cot,
    flux_cot,
    conv_weight,
    mix_weight,
    flux_weight,
    regrid_weights,
    intersection_atm,
    intersection_offset,
    wet_rows,
):
    members, lat_tiles, lon_tiles = (lax.axis_size(name) for name in ("ens", "oy", "ox"))
    rows, cells, channels = state.shape[1:]
    fields = flux_weight.shape[0]
    tiles = lat_tiles * lon_tiles
    grad_rows = (conv_weight.shape[0] + 1) * channels
    band = grad_rows // lat_tiles
    pieces = lon_tiles * members
    sub = band // pieces
    grad_scale = 1.0 / math.sqrt(members * lat_tiles * rows * lon_tiles * cells)
    entries = tiles * rows * intersection_atm.shape[2] * fields
    halo = (rows + 2, cells + 2 * EDGE, channels)
    spread = (rows + 2, cells, 3 * channels)
    small = 2 * fields
    edge_rows = -(-(rows + 2) // EDGE) * EDGE
    size = 3 * EDGE
    chunks = [(at, min(size, sub - at)) for at in range(0, sub, size)]

    def pair(count):
        return (pltpu.SemaphoreType.DMA((count,)), pltpu.SemaphoreType.DMA((count,)))

    vmem = pl.BlockSpec(memory_space=pltpu.VMEM)
    smem = pl.BlockSpec(memory_space=pltpu.SMEM)
    hbm = pl.BlockSpec(memory_space=pltpu.HBM)
    flux_flat = flux_cot[0].reshape(-1, cells)
    tables = [table.transpose(1, 2, 0) for table in (intersection_atm, intersection_offset)]
    scratch = [
        pltpu.VMEM((rows, cells, channels), BF16),
        pltpu.VMEM(flux_flat.shape, BF16),
        pltpu.VMEM(conv_weight.shape, BF16),
        pltpu.VMEM(mix_weight.shape, BF16),
        pltpu.VMEM(flux_weight.shape, BF16),
        pltpu.VMEM(regrid_weights.shape, BF16),
        pltpu.SMEM(tables[0].shape, jnp.int32),
        pltpu.SMEM(tables[1].shape, jnp.int32),
        pltpu.VMEM(halo, BF16),
        pltpu.VMEM(halo, BF16),
        pltpu.VMEM(halo, F32),
        pltpu.VMEM(spread, BF16),
        pltpu.VMEM((3 * channels, (rows + 2) * cells), BF16),
        pltpu.VMEM(spread, BF16),
        pltpu.VMEM((entries, cells), jnp.int32),
        pltpu.VMEM((entries, cells), jnp.int32),
        pltpu.VMEM((tiles, rows * fields, cells), F32),
        pltpu.VMEM((tiles, rows * fields, cells), F32),
        pltpu.VMEM((2 * rows * fields, channels), F32),
        pltpu.VMEM((lat_tiles, pieces, sub, channels), F32),
        pltpu.VMEM((lat_tiles, pieces, sub, channels), BF16),
        pltpu.VMEM((pieces, sub, channels), BF16),
        pltpu.VMEM((lon_tiles, members, sub, channels), BF16),
        pltpu.VMEM((members, lon_tiles, sub, channels), BF16),
        pltpu.VMEM((lon_tiles, sub, channels), BF16),
        pltpu.VMEM((lon_tiles, sub, channels), BF16),
        pltpu.VMEM((members, sub, channels), BF16),
        pltpu.VMEM((rows * cells, channels), F32),
        pltpu.VMEM((rows * cells, channels), F32),
        pltpu.VMEM((2, edge_rows, channels), F32),
        pltpu.VMEM((2, 3, edge_rows, channels), F32),
        pltpu.VMEM((lat_tiles, small, channels), F32),
        pltpu.VMEM((members, small, channels), F32),
        pltpu.VMEM((lon_tiles, small, channels), F32),
        pltpu.SemaphoreType.DMA((9,)),
        pair(5),
        pair(5),
        pair(tiles),
        pair(lat_tiles),
        pair(members),
        pair(lon_tiles),
        pair(len(chunks) * lat_tiles),
        pair(len(chunks) * members),
        pair(len(chunks) * lon_tiles),
        pair(len(chunks) * members),
    ]
    cost = pl.CostEstimate(
        flops=2 * rows * cells * channels * channels * 29, bytes_accessed=3 << 20, transcendentals=rows * cells * channels
    )
    outs = pl.pallas_call(
        functools.partial(fused_kernel, (members, lat_tiles, lon_tiles, grad_scale, chunks)),
        out_shape=(
            jax.ShapeDtypeStruct(state.shape, BF16),
            jax.ShapeDtypeStruct((members, sub, channels), BF16),
            jax.ShapeDtypeStruct((fields, channels), F32),
        ),
        in_specs=[hbm] * 9 + [smem],
        out_specs=(vmem, vmem, vmem),
        scratch_shapes=scratch,
        cost_estimate=cost,
        compiler_params=pltpu.CompilerParams(
            collective_id=0, has_side_effects=True, vmem_limit_bytes=56 << 20
        ),
    )(
        state[0],
        state_cot[0],
        flux_flat,
        conv_weight,
        mix_weight,
        flux_weight,
        regrid_weights,
        tables[0],
        tables[1],
        wet_rows,
    )
    return place(*outs)


def step(state, state_cot, flux_cot, conv_weight, *rest):
    members, lat_tiles, lon_tiles = (lax.axis_size(name) for name in ("ens", "oy", "ox"))
    grad_rows = (conv_weight.shape[0] + 1) * state.shape[3]
    whole_tiles = grad_rows % (lat_tiles * lon_tiles * members * EDGE) == 0
    whole_taps = grad_rows // lat_tiles % state.shape[3] == 0
    fused = lat_tiles == 2 and lon_tiles > 1 and whole_tiles and whole_taps
    return (fused_body if fused else body)(state, state_cot, flux_cot, conv_weight, *rest)


def solution(mesh):
    in_specs = (
        P("ens", "oy", "ox", None),
        P("ens", "oy", "ox", None),
        P("ens", ("oy", "ox"), None, None),
        P(),
        P(),
        P(),
        P(),
        P(),
        P(),
        P("oy", "ox"),
    )
    out_specs = (P("ens", "oy", "ox", None), P(("oy", "ox"), None), P())
    return jax.shard_map(step, mesh=mesh, in_specs=in_specs, out_specs=out_specs, check_vma=False)
```

```python
import functools
import math

import jax
import jax.numpy as jnp
from jax import lax
from jax.experimental import pallas as pl
from jax.experimental.pallas import tpu as pltpu
from jax.sharding import PartitionSpec as P

CAP = 5


def with_halo(cells, sides, width):
    for axis, dim in sides:
        count = lax.axis_size(axis)
        head = lax.slice_in_dim(cells, 0, width, axis=dim)
        tail = lax.slice_in_dim(cells, cells.shape[dim] - width, cells.shape[dim], axis=dim)
        cells = jnp.concatenate(
            [
                lax.ppermute(tail, axis, [(i, (i + 1) % count) for i in range(count)]),
                cells,
                lax.ppermute(head, axis, [((i + 1) % count, i) for i in range(count)]),
            ],
            axis=dim,
        )
    return cells


def shifted(value, axis, steps):
    count = lax.axis_size(axis)
    pairs = [(source, (source + steps) % count) for source in range(count)]
    return lax.ppermute(value, axis, pairs)


def zero_ends(padded, row_index, lat_tiles):
    top_keep = jnp.where(row_index > 0, 1.0, 0.0).astype(padded.dtype)
    bottom = jnp.where(row_index < lat_tiles - 1, 1.0, 0.0).astype(padded.dtype)
    return jnp.concatenate([padded[:1] * top_keep, padded[1:-1], padded[-1:] * bottom], axis=0)


def owner_rank(owners):
    entry_count = owners.shape[-1]
    same_owner = owners[..., :, None] == owners[..., None, :]
    earlier = jnp.arange(entry_count)[None, :] < jnp.arange(entry_count)[:, None]
    return jnp.sum(jnp.logical_and(same_owner, earlier), axis=-1)


def body(
    state,
    state_cot,
    flux_cot,
    conv_weight,
    mix_weight,
    flux_weight,
    regrid_weights,
    intersection_atm,
    intersection_offset,
    wet_rows,
):
    lat_tiles = lax.axis_size("oy")
    lon_tiles = lax.axis_size("ox")
    members = lax.axis_size("ens")
    row_index = lax.axis_index("oy")
    col_index = lax.axis_index("ox")
    tile_state = state[0]
    tile_rows, block_cells, channels = tile_state.shape
    cot_flat = state_cot[0].reshape(-1, channels)
    grad_scale = 1.0 / math.sqrt(members * lat_tiles * tile_rows * lon_tiles * block_cells)
    padded = with_halo(tile_state, (("oy", 0), ("ox", 1)), 1)
    padded = zero_ends(padded, row_index, lat_tiles)
    hidden = jnp.zeros((tile_rows * block_cells, channels), jnp.float32)
    for tap_index in range(9):
        tap_row, tap_col = (tap_index // 3, tap_index % 3)
        patch_rows = padded[tap_row : tap_row + tile_rows, tap_col : tap_col + block_cells].reshape(
            -1, channels
        )
        hidden = hidden + jnp.dot(
            patch_rows, conv_weight[tap_index], preferred_element_type=jnp.float32
        )
    activation = jax.nn.silu(hidden).astype(jnp.bfloat16)
    atm_dev = flux_cot.shape[1]
    cot_blocks = flux_cot[0]
    flux_fields = cot_blocks.shape[1]
    intersections = intersection_atm.shape[2]
    entries = tile_rows * intersections
    per_dev = (
        intersection_atm.reshape(lat_tiles, tile_rows, lon_tiles, intersections)
        .transpose(0, 2, 1, 3)
        .reshape(lat_tiles, lon_tiles, entries)
    )
    per_dev_offset = (
        intersection_offset.reshape(lat_tiles, tile_rows, lon_tiles, intersections)
        .transpose(0, 2, 1, 3)
        .reshape(lat_tiles, lon_tiles, entries)
    )
    band_rows = jnp.stack([row_index, (row_index + lat_tiles - 1) % lat_tiles])
    candidate = jnp.take(per_dev, band_rows, axis=0)
    candidate_offset = jnp.take(per_dev_offset, band_rows, axis=0)
    flat_index = row_index * lon_tiles + col_index
    candidate_owner = candidate // atm_dev
    is_mine = candidate_owner == flat_index
    slot_rank = owner_rank(candidate_owner)
    local_block = jnp.where(is_mine, candidate % atm_dev, 0)
    picked_cot = cot_blocks[local_block]
    picked_maps = regrid_weights[candidate_offset]
    products = jnp.einsum(
        "qsefa,qseoa->qsefo", picked_cot, picked_maps, preferred_element_type=jnp.float32
    )
    one_hot = jnp.logical_and(
        slot_rank[..., None] == jnp.arange(CAP)[None, None, None, :], is_mine[..., None]
    ).astype(jnp.float32)
    outbound = jnp.einsum("qsec,qsefo->qscfo", one_hot, products).astype(jnp.bfloat16)
    own_entries = per_dev[row_index, col_index]
    own_owner = own_entries // atm_dev
    own_slot = owner_rank(own_owner)
    same_in, next_in = (
        lax.all_to_all(outbound[0], "ox", split_axis=0, concat_axis=0, tiled=True),
        lax.all_to_all(outbound[1], "ox", split_axis=0, concat_axis=0, tiled=True),
    )
    next_in = shifted(next_in, "oy", -1)
    arrived = jnp.concatenate([same_in, next_in], axis=0).reshape(-1, flux_fields, block_cells)
    in_next = (own_owner // lon_tiles != row_index).astype(jnp.int32)
    slot_index = (in_next * lon_tiles + own_owner % lon_tiles) * CAP + own_slot
    values = (
        arrived[slot_index]
        .astype(jnp.float32)
        .reshape(tile_rows, intersections, flux_fields, block_cells)
    )
    wet_mask = (jnp.arange(tile_rows) < wet_rows[0, 0]).astype(jnp.float32)
    flux_cells = jnp.sum(values, axis=1) * wet_mask[:, None, None]
    act_grad = lax.dot_general(
        cot_flat, mix_weight, (((1,), (1,)), ((), ())), preferred_element_type=jnp.float32
    )
    act_grad = act_grad + jnp.einsum(
        "rfb,fc->rbc", flux_cells, flux_weight.astype(jnp.float32)
    ).reshape(-1, channels)
    gate_sig = jax.nn.sigmoid(hidden)
    hidden_grad = (act_grad * gate_sig * (1.0 + hidden * (1.0 - gate_sig))).astype(jnp.bfloat16)
    padded_grad = with_halo(
        hidden_grad.reshape(tile_rows, block_cells, channels), (("oy", 0), ("ox", 1)), 1
    )
    padded_grad = zero_ends(padded_grad, row_index, lat_tiles)
    input_grad = cot_flat.astype(jnp.float32)
    tap_grads = []
    for tap_index in range(9):
        tap_row, tap_col = (tap_index // 3, tap_index % 3)
        back_rows = padded_grad[
            2 - tap_row : 2 - tap_row + tile_rows, 2 - tap_col : 2 - tap_col + block_cells
        ].reshape(-1, channels)
        input_grad = input_grad + lax.dot_general(
            back_rows,
            conv_weight[tap_index],
            (((1,), (1,)), ((), ())),
            preferred_element_type=jnp.float32,
        )
        patch_rows = padded[tap_row : tap_row + tile_rows, tap_col : tap_col + block_cells].reshape(
            -1, channels
        )
        tap_grads.append(
            lax.dot_general(
                patch_rows,
                hidden_grad,
                (((0,), (0,)), ((), ())),
                preferred_element_type=jnp.float32,
            )
        )
    tap_grads.append(
        lax.dot_general(
            activation, cot_flat, (((0,), (0,)), ((), ())), preferred_element_type=jnp.float32
        )
    )
    weight_term = jnp.concatenate(tap_grads, axis=0) * grad_scale
    flux_term = (
        jnp.einsum(
            "rfb,rbc->fc",
            flux_cells,
            activation.reshape(tile_rows, block_cells, channels).astype(jnp.float32),
        )
        * grad_scale
    )
    weight_rows = lax.psum_scatter(weight_term, ("oy", "ox"), scatter_dimension=0, tiled=True)
    weight_out = lax.psum(weight_rows, "ens")
    flux_total = lax.psum(flux_term, ("ens", "oy", "ox"))
    input_out = input_grad.reshape(1, tile_rows, block_cells, channels).astype(jnp.bfloat16)
    return (input_out, weight_out, flux_total)


F32 = jnp.float32
BF16 = jnp.bfloat16
MESH = pl.DeviceIdType.MESH
EDGE = 16


def dot(a, b, dims=((1,), (0,))):
    return lax.dot_general(a, b, (dims, ((), ())), preferred_element_type=F32)


def remote(src, dst, send_sem, recv_sem, target):
    return pltpu.make_async_remote_copy(
        src_ref=src,
        dst_ref=dst,
        send_sem=send_sem,
        recv_sem=recv_sem,
        device_id=target,
        device_id_type=MESH,
    )


def start_all(copies):
    for copy in copies:
        copy.start()
    return copies


def halo_copies(src, src_at, padded, rows, cells, lat, lon, lon_tiles, sems):
    row0, col0 = src_at
    other = 1 - lat
    east = lax.rem(lon + 1, lon_tiles)
    west = lax.rem(lon + lon_tiles - 1, lon_tiles)
    edge_row = row0 + other * (rows - 1)
    land_row = lat * (rows + 1)
    body_rows, dst_rows = pl.ds(row0, rows), pl.ds(1, rows)
    head, last = pl.ds(col0, EDGE), pl.ds(col0 + cells - EDGE, EDGE)
    left, middle, right = pl.ds(0, EDGE), pl.ds(EDGE, cells), pl.ds(EDGE + cells, EDGE)
    plan = [
        (src.at[pl.ds(edge_row, 1), pl.ds(col0, cells)], padded.at[pl.ds(land_row, 1), middle], other, lon),
        (src.at[body_rows, last], padded.at[dst_rows, left], lat, east),
        (src.at[body_rows, head], padded.at[dst_rows, right], lat, west),
        (src.at[pl.ds(edge_row, 1), last], padded.at[pl.ds(land_row, 1), left], other, east),
        (src.at[pl.ds(edge_row, 1), head], padded.at[pl.ds(land_row, 1), right], other, west),
    ]
    send, recv = sems
    return [
        remote(a, b, send.at[n], recv.at[n], {"oy": y, "ox": x})
        for n, (a, b, y, x) in enumerate(plan)
    ]


def exchange(axis, count, me, source, target, sems, base=0):
    send, recv = sems
    copies = []
    for step in range(1, count):
        to = lax.rem(me + step, count)
        copies.append(
            remote(source(to), target(me), send.at[base + step - 1], recv.at[base + step - 1], {axis: to})
        )
    return copies


def wait_all(copies):
    for copy in copies:
        copy.wait_recv()


def shift_cells(padded, wide, columns, rows, cells, order, edges=True):
    channels = padded.shape[2]
    middle = slice(EDGE, EDGE + cells)
    for row in range(rows + 2):
        if edges:
            wide[row] = padded[row].astype(F32)
        else:
            wide[row, 0:EDGE] = jnp.zeros((EDGE, channels), F32)
            wide[row, middle] = padded[row, middle].astype(F32)
            wide[row, EDGE + cells :] = jnp.zeros((EDGE, channels), F32)
        for n, col in enumerate(order):
            here = slice(n * channels, (n + 1) * channels)
            if col == 1:
                columns[row, :, here] = padded[row, middle]
            else:
                columns[row, :, here] = wide[row, pl.ds(EDGE - 1 + col, cells), :].astype(BF16)


def turn(columns, turned, q):
    channels = columns.shape[2] // 3
    here = slice(q * channels, (q + 1) * channels)
    turned[here, :] = columns[:, :, here].reshape(-1, channels).T


def store_rows(target, first, value):
    pieces, sub = target.shape[1:3]
    done = 0
    while done < value.shape[0]:
        at = first + done
        piece, row = at // sub, at % sub
        count = min(sub - row, value.shape[0] - done)
        target[piece // pieces, piece % pieces, row : row + count, :] = value[done : done + count].astype(
            target.dtype
        )
        done += count


def fused_kernel(
    sizes,
    state_in,
    cot_in,
    flux_cot_in,
    conv_in,
    mix_in,
    flux_weight_in,
    regrid_in,
    atm_in,
    offset_in,
    wet,
    input_out,
    weight_out,
    flux_out,
    cot,
    flux_cot,
    conv,
    mix,
    flux_weight,
    regrid,
    atm,
    offset,
    padded,
    padded_grad,
    wide,
    columns,
    turned,
    grad_columns,
    entry_cell,
    entry_map,
    flux_send,
    flux_recv,
    flux_rows,
    grads,
    grads_half,
    recv_lat,
    sum_lat,
    recv_ens,
    sum_ens,
    recv_lon,
    rows_all,
    input_sum,
    hidden_sum,
    edge,
    edge_part,
    flux_lat,
    flux_ens,
    flux_lon,
    load_sems,
    state_sems,
    grad_sems,
    flux_sems,
    flux_lat_sems,
    flux_ens_sems,
    flux_lon_sems,
    lat_sems,
    ens_sems,
    lon_sems,
    out_sems,
):
    members, lat_tiles, lon_tiles, grad_scale, chunks = sizes
    ens, lat, lon = lax.axis_index("ens"), lax.axis_index("oy"), lax.axis_index("ox")
    rows, cells, channels = cot.shape
    fields = flux_weight.shape[0]
    intersections = atm.shape[1]
    maps = regrid.shape[0]
    tiles = lat_tiles * lon_tiles
    flat = lat * lon_tiles + lon
    cells_here = flux_cot.shape[0]

    barrier = pltpu.get_barrier_semaphore()
    for step in range(1, tiles):
        peer = lax.rem(flat + step, tiles)
        pl.semaphore_signal(
            barrier, inc=1, device_id={"oy": peer // lon_tiles, "ox": lax.rem(peer, lon_tiles)}, device_id_type=MESH
        )
    for step in range(1, members):
        pl.semaphore_signal(
            barrier, inc=1, device_id={"ens": lax.rem(ens + step, members)}, device_id_type=MESH
        )
    loads = [
        pltpu.make_async_copy(src, dst, load_sems.at[n])
        for n, (src, dst) in enumerate(
            [
                (atm_in, atm),
                (offset_in, offset),
                (flux_cot_in, flux_cot),
                (regrid_in, regrid),
                (cot_in, cot),
                (mix_in, mix),
                (state_in, padded.at[pl.ds(1, rows), pl.ds(EDGE, cells)]),
                (flux_weight_in, flux_weight),
                (conv_in, conv),
            ]
        )
    ]
    for load in loads:
        load.start()

    outside = lat * (rows + 1)
    padded[pl.ds(outside, 1)] = jnp.zeros((1,) + padded.shape[1:], BF16)
    padded_grad[pl.ds(outside, 1)] = jnp.zeros((1,) + padded.shape[1:], BF16)


    loads[0].wait()
    loads[1].wait()
    entry = 0
    for k in range(intersections):
        for tile in range(tiles):
            for row in range(rows):
                at = (tile % lon_tiles, k, (tile // lon_tiles) * rows + row)
                entry_cell[pl.ds(entry, fields), :] = jnp.full((fields, cells), atm[at], jnp.int32)
                entry_map[pl.ds(entry, fields), :] = jnp.full((fields, cells), offset[at], jnp.int32)
                entry += fields
    field_iota = lax.broadcasted_iota(jnp.int32, entry_cell.shape, 0) % fields
    lane = lax.broadcasted_iota(jnp.int32, entry_cell.shape, 1)
    which_cell = entry_cell[...] * fields + (field_iota - lane - flat * cells_here)
    which_map = entry_map[...]
    loads[2].wait()
    one_hot = [
        jnp.where(which_cell == part * cells, 1.0, 0.0).astype(BF16) for part in range(cells_here // cells)
    ]
    picked = dot(jnp.concatenate(one_hot, axis=1), flux_cot[...])
    loads[3].wait()
    span = tiles * rows * fields
    part_of = [slice(k * span, (k + 1) * span) for k in range(intersections)]
    share = jnp.zeros((span, cells), F32)
    for m in range(0, maps, 2):
        chosen, taken = [], []
        for n in range(m, min(m + 2, maps)):
            total = jnp.where(which_map[part_of[0]] == n, picked[part_of[0]], 0.0)
            for k in range(1, intersections):
                total = total + jnp.where(which_map[part_of[k]] == n, picked[part_of[k]], 0.0)
            chosen.append(total.astype(BF16))
            taken.append(regrid[n])
        share = share + dot(jnp.concatenate(chosen, axis=1), jnp.concatenate(taken, axis=1), ((1,), (1,)))
    flux_send[...] = share.reshape(flux_send.shape)
    flux_recv[pl.ds(flat, 1)] = flux_send[pl.ds(flat, 1)]

    pl.semaphore_wait(barrier, tiles - 1 + members - 1)
    state_copies = start_all(
        halo_copies(state_in, (0, 0), padded, rows, cells, lat, lon, lon_tiles, state_sems)
    )

    flux_copies = []
    for step in range(1, tiles):
        peer = lax.rem(flat + step, tiles)
        flux_copies.append(
            remote(
                flux_send.at[peer],
                flux_recv.at[flat],
                flux_sems[0].at[step - 1],
                flux_sems[1].at[step - 1],
                {"oy": peer // lon_tiles, "ox": lax.rem(peer, lon_tiles)},
            )
        )
    start_all(flux_copies)

    for load in loads[4:]:
        load.wait()
    flux_rows[...] = jnp.zeros(flux_rows.shape, F32)
    for n in range(2 * rows):
        flux_rows[n * fields : (n + 1) * fields, :] = flux_weight[...].astype(F32)
    cot_flat = cot[...].reshape(rows * cells, channels)
    act_grad = dot(cot_flat, mix[...], ((1,), (1,)))
    state_copies[0].wait_recv()
    shift_cells(padded, wide, columns, rows, cells, (0, 1, 2), False)
    hidden = jnp.zeros((rows * cells, channels), F32)
    for p in range(3):
        hidden = hidden + dot(
            columns[p : p + rows].reshape(rows * cells, 3 * channels),
            conv[3 * p : 3 * p + 3].reshape(3 * channels, channels),
        )
    hidden_sum[...] = hidden
    turn(columns, turned, 1)

    wait_all(state_copies[1:])
    edge[...] = jnp.zeros(edge.shape, F32)
    cell_iota = lax.broadcasted_iota(jnp.int32, (EDGE, channels), 0)
    for row in range(rows + 2):
        west = padded[row, 0:EDGE].astype(F32)[EDGE - 1 :]
        east = padded[row, EDGE + cells :].astype(F32)[:1]
        edge[0, row : row + 1] = west
        edge[1, row : row + 1] = east
        kept = columns[row, 0:EDGE, 0:channels].astype(F32)
        columns[row, 0:EDGE, 0:channels] = jnp.where(cell_iota == 0, west, kept).astype(BF16)
        kept = columns[row, cells - EDGE :, 2 * channels :].astype(F32)
        columns[row, cells - EDGE :, 2 * channels :] = jnp.where(cell_iota == EDGE - 1, east, kept).astype(BF16)
    for side in range(2):
        cells_there = edge[side].astype(BF16)
        for p in range(3):
            edge_part[side, p] = dot(cells_there, conv[3 * p + 2 * side])
        for row in range(rows):
            at = row * cells + side * (cells - 1)
            added = hidden_sum[at : at + 1]
            for p in range(3):
                added = added + edge_part[side, p, row + p : row + p + 1]
            hidden_sum[at : at + 1] = added
    hidden = hidden_sum[...]
    turn(columns, turned, 0)
    turn(columns, turned, 2)
    gate = jax.nn.sigmoid(hidden)
    activation = (hidden * gate).astype(BF16)
    slope = gate * (1.0 + hidden * (1.0 - gate))
    term = dot(activation, cot_flat, ((0,), (0,)))
    store_rows(grads, 9 * channels, term)
    store_rows(grads_half, 9 * channels, term)

    wait_all(flux_copies)
    row_iota = lax.broadcasted_iota(jnp.int32, (rows * fields, cells), 0) // fields
    flux = flux_recv[0]
    for tile in range(1, tiles):
        flux = flux + flux_recv[tile]
    flux = jnp.where(row_iota < wet[0, 0], flux, 0.0)
    flux_high = flux.astype(BF16).astype(F32)
    flux_low = flux - flux_high
    both = jnp.concatenate([flux_high, flux_low], axis=0)
    both_iota = jnp.concatenate([row_iota, row_iota], axis=0)
    heads = flux_rows[...].astype(BF16)
    masked = []
    for row in range(rows):
        mine = jnp.where(both_iota == row, both, 0.0).astype(BF16)
        masked.append(mine)
        here = slice(row * cells, (row + 1) * cells)
        extra = dot(mine, heads, ((0,), (0,)))
        padded_grad[row + 1, EDGE : EDGE + cells] = ((act_grad[here] + extra) * slope[here]).astype(BF16)
    grad_copies = start_all(
        halo_copies(padded_grad, (1, EDGE), padded_grad, rows, cells, lat, lon, lon_tiles, grad_sems)
    )

    def tap_grads(target, first, last):
        hidden_grad = padded_grad[1 : rows + 1, EDGE : EDGE + cells].reshape(rows * cells, channels)
        tap = first
        while tap < last:
            p, q = tap // 3, tap % 3
            count = min(3 - q, last - tap)
            left = turned[q * channels : (q + count) * channels, p * cells : (p + rows) * cells]
            store_rows(target, tap * channels, dot(left, hidden_grad))
            tap += count

    taps = grads.shape[1] * grads.shape[2] // channels
    for part in range(lat_tiles):

        @pl.when(lat != part)
        def _():
            tap_grads(grads_half, part * taps, min((part + 1) * taps, 9))

    lat_copies = [
        start_all(
            exchange(
                "oy",
                lat_tiles,
                lat,
                lambda to: grads_half.at[to, :, pl.ds(at, count)],
                lambda me: recv_lat.at[:, pl.ds(at, count)],
                lat_sems,
                n * lat_tiles,
            )
        )
        for n, (at, count) in enumerate(chunks)
    ]
    flux_rows[...] = dot(jnp.concatenate(masked, axis=1), activation)
    total = flux_rows[:fields, :]
    for n in range(1, 2 * rows):
        total = total + flux_rows[n * fields : (n + 1) * fields, :]
    flux_lat[pl.ds(lat, 1)] = jnp.zeros((1,) + flux_lat.shape[1:], F32)
    flux_lat[pl.ds(lat, 1), 0:fields, :] = total[None]
    flux_lat_copies = start_all(
        exchange("oy", lat_tiles, lat, lambda to: flux_lat.at[lat], lambda me: flux_lat.at[me], flux_lat_sems)
    )

    for part in range(lat_tiles):

        @pl.when(lat == part)
        def _():
            tap_grads(grads, part * taps, min((part + 1) * taps, 9))

    ens_copies = []
    for n, (at, count) in enumerate(chunks):
        wait_all(lat_copies[n])
        own = grads[pl.ds(lat, 1), :, at : at + count]
        part = (own[0] + recv_lat[:, at : at + count].astype(F32)).astype(BF16)
        sum_lat[:, :, at : at + count] = part.reshape(lon_tiles, members, count, channels)
        ens_copies.append(
            start_all(
                exchange(
                    "ens",
                    members,
                    ens,
                    lambda to: sum_lat.at[:, to, pl.ds(at, count)],
                    lambda me: recv_ens.at[me, :, pl.ds(at, count)],
                    ens_sems,
                    n * members,
                )
            )
        )
    recv_ens[pl.ds(ens, 1)] = sum_lat[:, pl.ds(ens, 1)].reshape((1,) + recv_ens.shape[1:])
    wait_all(flux_lat_copies)
    total = flux_lat[0]
    for n in range(1, lat_tiles):
        total = total + flux_lat[n]
    flux_ens[pl.ds(ens, 1)] = total[None]
    flux_ens_copies = start_all(
        exchange("ens", members, ens, lambda to: flux_ens.at[ens], lambda me: flux_ens.at[me], flux_ens_sems)
    )

    wait_all(grad_copies)
    shift_cells(padded_grad, wide, grad_columns, rows, cells, (2, 1, 0))
    def input_part(p):
        back = grad_columns[2 - p : 2 - p + rows].reshape(rows * cells, 3 * channels)
        taps = jnp.concatenate([conv[3 * p + q] for q in range(3)], axis=1)
        before = input_sum[...] if p else cot_flat.astype(F32)
        total = before + dot(back, taps, ((1,), (1,)))
        if p < 2:
            input_sum[...] = total
        else:
            input_out[...] = total.astype(BF16).reshape(input_out.shape)

    input_part(0)
    lon_copies, out_copies = [], []

    def gather_chunk(n):
        at, count = chunks[n]
        wait_all(lon_copies[n])
        total = recv_lon[0, at : at + count].astype(F32)
        for other in range(1, lon_tiles):
            total = total + recv_lon[other, at : at + count].astype(F32)
        rows_all[pl.ds(ens, 1), at : at + count] = (total * grad_scale).astype(BF16)[None]
        out_copies.append(
            start_all(
                exchange(
                    "ens",
                    members,
                    ens,
                    lambda to: rows_all.at[ens, pl.ds(at, count)],
                    lambda me: rows_all.at[me, pl.ds(at, count)],
                    out_sems,
                    n * members,
                )
            )
        )

    for n, (at, count) in enumerate(chunks):
        wait_all(ens_copies[n])
        total = recv_ens[0, :, at : at + count].astype(F32)
        for other in range(1, members):
            total = total + recv_ens[other, :, at : at + count].astype(F32)
        sum_ens[:, at : at + count] = total.astype(BF16)
        lon_copies.append(
            start_all(
                exchange(
                    "ox",
                    lon_tiles,
                    lon,
                    lambda to: sum_ens.at[to, pl.ds(at, count)],
                    lambda me: recv_lon.at[me, pl.ds(at, count)],
                    lon_sems,
                    n * lon_tiles,
                )
            )
        )
        recv_lon[pl.ds(lon, 1), at : at + count] = sum_ens[pl.ds(lon, 1), at : at + count]
        if n == 0:
            wait_all(flux_ens_copies)
            total = flux_ens[0]
            for other in range(1, members):
                total = total + flux_ens[other]
            flux_lon[pl.ds(lon, 1)] = total[None]
            flux_lon_copies = start_all(
                exchange("ox", lon_tiles, lon, lambda to: flux_lon.at[lon], lambda me: flux_lon.at[me], flux_lon_sems)
            )
        else:
            gather_chunk(n - 1)
        if n < 2:
            input_part(n + 1)
    for p in range(len(chunks) + 1, 3):
        input_part(p)
    wait_all(flux_lon_copies)
    total = flux_lon[0]
    for n in range(1, lon_tiles):
        total = total + flux_lon[n]
    flux_out[...] = total[:fields] * grad_scale
    gather_chunk(len(chunks) - 1)
    for copies in out_copies:
        wait_all(copies)
    weight_out[...] = rows_all[...]
    started = state_copies + flux_copies + grad_copies + flux_lat_copies + flux_ens_copies + flux_lon_copies
    for copies in [started] + lat_copies + ens_copies + lon_copies + out_copies:
        for copy in copies:
            copy.wait_send()


def place_kernel(input_grad, weight_rows, flux_grad, input_out, weight_out, flux_out, wide, sems):
    copies = [
        pltpu.make_async_copy(input_grad, input_out, sems.at[0]),
        pltpu.make_async_copy(flux_grad, flux_out, sems.at[1]),
        pltpu.make_async_copy(wide, weight_out, sems.at[2]),
    ]
    copies[0].start()
    copies[1].start()
    wide[...] = weight_rows[...].reshape(wide.shape).astype(F32)
    copies[2].start()
    for copy in copies:
        copy.wait()


def place(input_grad, weight_rows, flux_grad):
    channels = weight_rows.shape[2]
    weight_shape = (weight_rows.shape[0] * weight_rows.shape[1], channels)
    vmem = pl.BlockSpec(memory_space=pltpu.VMEM)
    hbm = pl.BlockSpec(memory_space=pltpu.HBM)
    return pl.pallas_call(
        place_kernel,
        out_shape=(
            jax.ShapeDtypeStruct(input_grad.shape, BF16),
            jax.ShapeDtypeStruct(weight_shape, F32),
            jax.ShapeDtypeStruct(flux_grad.shape, F32),
        ),
        in_specs=[vmem] * 3,
        out_specs=(hbm, hbm, hbm),
        scratch_shapes=[pltpu.VMEM(weight_shape, F32), pltpu.SemaphoreType.DMA((3,))],
        compiler_params=pltpu.CompilerParams(vmem_limit_bytes=56 << 20),
    )(input_grad, weight_rows, flux_grad)


def fused_body(
    state,
    state_cot,
    flux_cot,
    conv_weight,
    mix_weight,
    flux_weight,
    regrid_weights,
    intersection_atm,
    intersection_offset,
    wet_rows,
):
    members, lat_tiles, lon_tiles = (lax.axis_size(name) for name in ("ens", "oy", "ox"))
    rows, cells, channels = state.shape[1:]
    fields = flux_weight.shape[0]
    tiles = lat_tiles * lon_tiles
    grad_rows = (conv_weight.shape[0] + 1) * channels
    band = grad_rows // lat_tiles
    pieces = lon_tiles * members
    sub = band // pieces
    grad_scale = 1.0 / math.sqrt(members * lat_tiles * rows * lon_tiles * cells)
    entries = tiles * rows * intersection_atm.shape[2] * fields
    halo = (rows + 2, cells + 2 * EDGE, channels)
    spread = (rows + 2, cells, 3 * channels)
    small = 2 * fields
    edge_rows = -(-(rows + 2) // EDGE) * EDGE
    chunks = [(0, sub)]

    def pair(count):
        return (pltpu.SemaphoreType.DMA((count,)), pltpu.SemaphoreType.DMA((count,)))

    vmem = pl.BlockSpec(memory_space=pltpu.VMEM)
    smem = pl.BlockSpec(memory_space=pltpu.SMEM)
    hbm = pl.BlockSpec(memory_space=pltpu.HBM)
    flux_flat = flux_cot[0].reshape(-1, cells)
    tables = [table.transpose(1, 2, 0) for table in (intersection_atm, intersection_offset)]
    scratch = [
        pltpu.VMEM((rows, cells, channels), BF16),
        pltpu.VMEM(flux_flat.shape, BF16),
        pltpu.VMEM(conv_weight.shape, BF16),
        pltpu.VMEM(mix_weight.shape, BF16),
        pltpu.VMEM(flux_weight.shape, BF16),
        pltpu.VMEM(regrid_weights.shape, BF16),
        pltpu.SMEM(tables[0].shape, jnp.int32),
        pltpu.SMEM(tables[1].shape, jnp.int32),
        pltpu.VMEM(halo, BF16),
        pltpu.VMEM(halo, BF16),
        pltpu.VMEM(halo, F32),
        pltpu.VMEM(spread, BF16),
        pltpu.VMEM((3 * channels, (rows + 2) * cells), BF16),
        pltpu.VMEM(spread, BF16),
        pltpu.VMEM((entries, cells), jnp.int32),
        pltpu.VMEM((entries, cells), jnp.int32),
        pltpu.VMEM((tiles, rows * fields, cells), F32),
        pltpu.VMEM((tiles, rows * fields, cells), F32),
        pltpu.VMEM((2 * rows * fields, channels), F32),
        pltpu.VMEM((lat_tiles, pieces, sub, channels), F32),
        pltpu.VMEM((lat_tiles, pieces, sub, channels), BF16),
        pltpu.VMEM((pieces, sub, channels), BF16),
        pltpu.VMEM((lon_tiles, members, sub, channels), BF16),
        pltpu.VMEM((members, lon_tiles, sub, channels), BF16),
        pltpu.VMEM((lon_tiles, sub, channels), BF16),
        pltpu.VMEM((lon_tiles, sub, channels), BF16),
        pltpu.VMEM((members, sub, channels), BF16),
        pltpu.VMEM((rows * cells, channels), F32),
        pltpu.VMEM((rows * cells, channels), F32),
        pltpu.VMEM((2, edge_rows, channels), F32),
        pltpu.VMEM((2, 3, edge_rows, channels), F32),
        pltpu.VMEM((lat_tiles, small, channels), F32),
        pltpu.VMEM((members, small, channels), F32),
        pltpu.VMEM((lon_tiles, small, channels), F32),
        pltpu.SemaphoreType.DMA((9,)),
        pair(5),
        pair(5),
        pair(tiles),
        pair(lat_tiles),
        pair(members),
        pair(lon_tiles),
        pair(len(chunks) * lat_tiles),
        pair(len(chunks) * members),
        pair(len(chunks) * lon_tiles),
        pair(len(chunks) * members),
    ]
    cost = pl.CostEstimate(
        flops=2 * rows * cells * channels * channels * 29, bytes_accessed=3 << 20, transcendentals=rows * cells * channels
    )
    outs = pl.pallas_call(
        functools.partial(fused_kernel, (members, lat_tiles, lon_tiles, grad_scale, chunks)),
        out_shape=(
            jax.ShapeDtypeStruct(state.shape, BF16),
            jax.ShapeDtypeStruct((members, sub, channels), BF16),
            jax.ShapeDtypeStruct((fields, channels), F32),
        ),
        in_specs=[hbm] * 9 + [smem],
        out_specs=(vmem, vmem, vmem),
        scratch_shapes=scratch,
        cost_estimate=cost,
        compiler_params=pltpu.CompilerParams(
            collective_id=0, has_side_effects=True, vmem_limit_bytes=56 << 20
        ),
    )(
        state[0],
        state_cot[0],
        flux_flat,
        conv_weight,
        mix_weight,
        flux_weight,
        regrid_weights,
        tables[0],
        tables[1],
        wet_rows,
    )
    return place(*outs)


def step(state, state_cot, flux_cot, conv_weight, *rest):
    members, lat_tiles, lon_tiles = (lax.axis_size(name) for name in ("ens", "oy", "ox"))
    grad_rows = (conv_weight.shape[0] + 1) * state.shape[3]
    whole_tiles = grad_rows % (lat_tiles * lon_tiles * members * EDGE) == 0
    whole_taps = grad_rows // lat_tiles % state.shape[3] == 0
    fused = lat_tiles == 2 and lon_tiles > 1 and whole_tiles and whole_taps
    return (fused_body if fused else body)(state, state_cot, flux_cot, conv_weight, *rest)


def solution(mesh):
    in_specs = (
        P("ens", "oy", "ox", None),
        P("ens", "oy", "ox", None),
        P("ens", ("oy", "ox"), None, None),
        P(),
        P(),
        P(),
        P(),
        P(),
        P(),
        P("oy", "ox"),
    )
    out_specs = (P("ens", "oy", "ox", None), P(("oy", "ox"), None), P())
    return jax.shard_map(step, mesh=mesh, in_specs=in_specs, out_specs=out_specs, check_vma=False)
```
